32 devices in a mesh: dom: 4 (over x, core), ctx: 8 (over z, y).
Axes of the slice: x: 2, y: 2, z: 4, core: 2. Of those that a mesh axis runs over, the one named last changes fastest.
Arguments:
- q_new: bfloat16 [4096, 4096], P(('dom', 'ctx')), may hold values from -40 to 40
- kv_new: bfloat16 [4096, 2, 512], P(('dom', 'ctx')), may hold values from -5 to 5
- prompt_kv: bfloat16 [512, 2, 512], P('ctx'), may hold values from -5 to 5
- cache_kv: bfloat16 [32, 64, 2, 512], P('dom', 'ctx'), may hold values from -5 to 5
- ancestors: int32 [32], replicated, may hold values from 0 to 31, as said below
- lengths: int32 [32], replicated, may hold values from 1 to 8, as said below
Outputs:
- attended: bfloat16 [4096, 4096], P(('dom', 'ctx'))
The draws below stay inside these ranges and needn't reach their ends.
Inputs may be any that keep to these rules, and one draw needn't show every extreme that they name: The 32 particles form 4 groups of 8 consecutive ones; within a group, each run of 4 consecutive particles takes all its ancestors from one group, and the runs of a group take them from different groups (its own among the possible ones). Ancestors repeat freely. `lengths`: both ends are reached.
All inputs are finite; a program needn't handle non-finite values.
Results may differ from the reference program's by a relative error of at most 0.022.
Values may be sent and summed in bfloat16 or wider, within the bound.
No kernel may reach another device: no remote copies, remote signals or barrier semaphores. Data moves between devices by JAX's collectives and lax.ppermute only.
A program may use at most 128 MiB of HBM per device.

```python
import jax
import jax.numpy as jnp
from jax import lax

HD = 128
H = 32
KVH = 4
SPAN = 128
PAGE = 8
GQ = 8
PG = 8
P_SIZE = 32
CAP = 4
MAXP = 8
GEN = 64
PROMPT = 512
N_DOM = 4


def prompt_base(key):
    sub_key = jax.random.fold_in(key, 5)
    samples = jnp.clip(jax.random.normal(sub_key, (PROMPT, 2, KVH * HD), jnp.float32), -5.0, 5.0)
    return samples


def draw_prompt_kv(key, part):
    return prompt_base(key).astype(jnp.bfloat16)


def draw_q_new(key, part):
    sub_key = jax.random.fold_in(key, 6)
    samples = jnp.clip(2.5 * jax.random.normal(sub_key, (P_SIZE * SPAN, H * HD), jnp.float32), -12.5, 12.5)
    return samples.astype(jnp.bfloat16)


def draw_ancestors(key, part):
    half_groups = N_DOM // 2
    group_keys = jax.random.split(jax.random.fold_in(key, 21), N_DOM)
    orders = jax.vmap(lambda key_one: jax.random.permutation(key_one, N_DOM))(group_keys)[:, :half_groups]
    sources = jnp.repeat(orders, CAP, axis=1)
    chosen = jax.random.randint(jax.random.fold_in(key, 22), (N_DOM, PG), 0, PG)
    return (sources * PG + chosen).reshape(P_SIZE).astype(jnp.int32)


def draw_lengths(key, part):
    samples = jax.random.randint(jax.random.fold_in(key, 31), (P_SIZE,), 1, MAXP + 1)
    top_spot = jax.random.randint(jax.random.fold_in(key, 32), (), 0, P_SIZE)
    low_spot = (top_spot + 1 + jax.random.randint(jax.random.fold_in(key, 33), (), 0, P_SIZE - 1)) % P_SIZE
    samples = samples.at[top_spot].set(MAXP)
    samples = samples.at[low_spot].set(1)
    return samples.astype(jnp.int32)


def shard_levels(own_key, shape, cuts, least, top_value):
    def one(axis_at, shards_of):
        steps = jax.random.uniform(jax.random.fold_in(jax.random.fold_in(own_key, 6), axis_at), (shards_of,), jnp.float32, least / len(cuts), top_value / len(cuts))
        return jnp.repeat(jnp.exp(steps), shape[axis_at] // shards_of).reshape((-1,) + (1,) * (len(shape) - axis_at - 1))

    loudness = one(*cuts[0])
    for cut in cuts[1:]:
        loudness = loudness * one(*cut)
    return loudness


def centred(own_key, extent, scale, most, shards=(), held_as=jnp.bfloat16):
    level = shard_levels(own_key, extent, shards, -0.22, 0.18) if shards else 1.0
    drawn = jax.random.normal(own_key, extent, jnp.float32) * scale * level
    return jnp.minimum(jnp.maximum(drawn, -most), most).astype(held_as)


def setup_inputs(seed: int = 0) -> dict:
    key_list = jax.random.split(jax.random.key(seed), 7)
    q_new = draw_q_new(jax.random.fold_in(key_list[6], 71), 0)
    kv_new = centred(key_list[1], (P_SIZE * SPAN, 2, KVH * HD), 1.0, 5.0, ((0, 32),))
    prompt_kv = draw_prompt_kv(jax.random.fold_in(key_list[6], 71), 0)
    cache_kv = centred(key_list[3], (P_SIZE, GEN, 2, KVH * HD), 1.0, 5.0, ((0, 4), (1, 8)))
    ancestors = draw_ancestors(jax.random.fold_in(key_list[6], 71), 0)
    lengths = draw_lengths(jax.random.fold_in(key_list[6], 71), 0)
    return {"q_new": q_new, "kv_new": kv_new, "prompt_kv": prompt_kv, "cache_kv": cache_kv, "ancestors": ancestors, "lengths": lengths}


NEGATIVE = -1e30


def reference(q_new, kv_new, prompt_kv, cache_kv, ancestors, lengths):
    prompt_keys = prompt_kv[:, 0].astype(jnp.float32).reshape(PROMPT, KVH, HD)
    prompt_values = prompt_kv[:, 1].astype(jnp.float32).reshape(PROMPT, KVH, HD)
    positions = jnp.arange(SPAN, dtype=jnp.int32)
    causal = positions[None, :] <= positions[:, None]
    cache_positions = jnp.arange(GEN, dtype=jnp.int32)
    prompt_visible = jnp.ones((SPAN, PROMPT), dtype=jnp.bool_)

    def one_particle(particle):
        anchor = ancestors[particle]
        pages = lax.dynamic_index_in_dim(cache_kv, anchor, 0, keepdims=False).astype(jnp.float32)
        page_limit = lengths[anchor] * PAGE
        queries = lax.dynamic_slice_in_dim(q_new, particle * SPAN, SPAN, 0).astype(jnp.float32).reshape(SPAN, KVH, GQ, HD)
        fresh_kv = lax.dynamic_slice_in_dim(kv_new, particle * SPAN, SPAN, 0).astype(jnp.float32)
        key_rows = jnp.concatenate([prompt_keys, pages[:, 0].reshape(GEN, KVH, HD), fresh_kv[:, 0].reshape(SPAN, KVH, HD)], axis=0)
        value_rows = jnp.concatenate([prompt_values, pages[:, 1].reshape(GEN, KVH, HD), fresh_kv[:, 1].reshape(SPAN, KVH, HD)], axis=0)
        cache_visible = jnp.broadcast_to((cache_positions < page_limit)[None, :], (SPAN, GEN))
        visible = jnp.concatenate([prompt_visible, cache_visible, causal], axis=1)[:, None, None, :]
        scores = jnp.einsum("igjd,kgd->igjk", queries, key_rows) * (HD ** -0.5)
        scores = jnp.where(visible, scores, NEGATIVE)
        maxima = jnp.max(scores, axis=-1, keepdims=True)
        weights = jnp.where(visible, jnp.exp(scores - maxima), 0.0)
        totals = jnp.sum(weights, axis=-1)
        rounded = lax.optimization_barrier(weights.astype(jnp.bfloat16)).astype(jnp.float32)
        output = jnp.einsum("igjk,kgd->igjd", rounded, value_rows) / totals[..., None]
        return output.astype(jnp.bfloat16).reshape(SPAN, H * HD)

    result = lax.map(one_particle, jnp.arange(P_SIZE, dtype=jnp.int32))
    return result.reshape(P_SIZE * SPAN, H * HD)
```

```python
import functools

import jax
import jax.numpy as jnp
from jax import lax
from jax.experimental import pallas as pl
from jax.experimental.pallas import tpu as pltpu
from jax.sharding import PartitionSpec as P

HD = 128
SPAN = 128
PAGE = 8
RUN = 4
Z = 4
NEGATIVE = -1e30
SCALE2 = HD ** (-0.5) * 1.4426950408889634
VMEM = pl.BlockSpec(memory_space=pltpu.VMEM)
SMEM = pl.BlockSpec(memory_space=pltpu.SMEM)


def params():
    return pltpu.CompilerParams(vmem_limit_bytes=40 * 2**20)


def pack_kernel(dom_count, anc_ref, prompt_ref, cache_ref, half_ref, out_ref):
    group = cache_ref.shape[0]
    dom = lax.axis_index("dom")
    rows, width = half_ref.shape
    half_ref[...] = prompt_ref[pl.ds(pl.multiple_of((dom % 2) * rows, rows), rows)].reshape(rows, width)
    runs = group // RUN

    def one(step, carry):
        first = step * RUN
        anchor = anc_ref[first]

        @pl.when(anchor // group == dom)
        def _():
            for slot in range(RUN):
                local = anc_ref[first + slot] % group
                out_ref[step // runs, slot] = cache_ref[local].reshape(cache_ref.shape[1], width)

        return carry

    lax.fori_loop(0, dom_count * runs, one, 0)


def route_kernel(anc_ref, in_ref, out_ref):
    group = out_ref.shape[0]
    dom = lax.axis_index("dom")
    for run in range(group // RUN):
        source = anc_ref[dom * group + run * RUN] // group
        out_ref[pl.ds(run * RUN, RUN)] = in_ref[source]


def head_rows(q_ref, g, gq):
    return jnp.concatenate(
        [q_ref[:, (g * gq + j) * HD : (g * gq + j + 1) * HD] for j in range(gq)], axis=0
    )


def dot_nt(a, b):
    return lax.dot_general(a, b, (((1,), (1,)), ((), ())), preferred_element_type=jnp.float32)


def dot_nn(a, b):
    return lax.dot_general(a, b, (((1,), (0,)), ((), ())), preferred_element_type=jnp.float32)


def main_kernel(q_ref, new_ref, *refs):
    *pieces, acc_ref, max_ref, sum_ref = refs
    width = new_ref.shape[2]
    kvh = width // HD
    gq = q_ref.shape[1] // width
    new = new_ref[...].reshape(SPAN, 2 * width)
    ones = jnp.ones((SPAN + sum(p.shape[0] for p in pieces), HD), jnp.bfloat16)
    token = lax.broadcasted_iota(jnp.int32, (SPAN, SPAN), 0)
    key = lax.broadcasted_iota(jnp.int32, (SPAN, SPAN), 1)
    causal = key <= token
    for g in range(kvh):
        k_at = slice(g * HD, (g + 1) * HD)
        v_at = slice(width + g * HD, width + (g + 1) * HD)
        keys = jnp.concatenate([new[:, k_at]] + [p[:, k_at] for p in pieces], axis=0)
        values = jnp.concatenate([new[:, v_at]] + [p[:, v_at] for p in pieces], axis=0)
        values = jnp.concatenate([values, ones], axis=1)
        scores = dot_nt(head_rows(q_ref, g, gq), keys)
        weights, tops = [], []
        for j in range(gq):
            s = scores[j * SPAN : (j + 1) * SPAN]
            s_new = jnp.where(causal, s[:, :SPAN], NEGATIVE)
            s_old = s[:, SPAN:]
            top = s_new
            for at in range(0, s_old.shape[1], HD):
                top = jnp.maximum(top, s_old[:, at : at + HD])
            top = jnp.max(top, axis=1, keepdims=True)
            s = jnp.concatenate([s_new, s_old], axis=1)
            weights.append(jnp.exp2((s - top) * SCALE2).astype(jnp.bfloat16))
            tops.append(top)
        out = dot_nn(jnp.concatenate(weights, axis=0), values)
        for j in range(gq):
            at = slice((g * gq + j) * HD, (g * gq + j + 1) * HD)
            rows = slice(j * SPAN, (j + 1) * SPAN)
            acc_ref[:, at] = out[rows, :HD]
            sum_ref[:, at] = out[rows, HD:]
            max_ref[:, at] = jnp.broadcast_to(tops[j], (SPAN, HD))


def merge_kernel(particle_group, anc_ref, len_ref, q_ref, cache_ref, acc_ref, max_ref, sum_ref, out_ref, stage, sems):
    width = cache_ref.shape[1] // 2
    gen = cache_ref.shape[0]
    kvh = width // HD
    gq = q_ref.shape[1] // width
    particle = lax.axis_index("dom") * particle_group + lax.axis_index("ctx")
    limit = len_ref[anc_ref[particle]] * PAGE
    visible = lax.broadcasted_iota(jnp.int32, (SPAN, gen), 1) < limit
    ones = jnp.ones((gen, HD), jnp.bfloat16)
    copies = []
    for g in range(kvh):
        keys = cache_ref[:, g * HD : (g + 1) * HD]
        values = jnp.concatenate([cache_ref[:, width + g * HD : width + (g + 1) * HD], ones], axis=1)
        scores = dot_nt(head_rows(q_ref, g, gq), keys)
        weights, factors = [], []
        for j in range(gq):
            at = slice((g * gq + j) * HD, (g * gq + j + 1) * HD)
            s = jnp.where(visible, scores[j * SPAN : (j + 1) * SPAN], NEGATIVE)
            before = max_ref[:, at]
            top = jnp.maximum(before, jnp.max(s, axis=1, keepdims=True))
            wide = top[:, :gen] if gen <= HD else jnp.concatenate([top] * (gen // HD), axis=1)
            weights.append(jnp.exp2((s - wide) * SCALE2).astype(jnp.bfloat16))
            factors.append(jnp.exp2((before - top) * SCALE2))
        out = dot_nn(jnp.concatenate(weights, axis=0), values)
        for j in range(gq):
            at = slice((g * gq + j) * HD, (g * gq + j + 1) * HD)
            rows = slice(j * SPAN, (j + 1) * SPAN)
            total = sum_ref[:, at] * factors[j] + out[rows, HD:]
            value = acc_ref[:, at] * factors[j] + out[rows, :HD]
            stage[:, at] = (value / total).astype(jnp.bfloat16)
        columns = pl.ds(g * gq * HD, gq * HD)
        copy = pltpu.make_async_copy(stage.at[:, columns], out_ref.at[:, columns], sems.at[g])
        copy.start()
        copies.append(copy)
    for copy in copies:
        copy.wait()


def swap(x, axis, partner):
    return lax.ppermute(x, axis, [(i, partner(i)) for i in range(lax.axis_size(axis))])


def on_device(q_new, kv_new, prompt_kv, cache_kv, ancestors, lengths):
    dom_count = lax.axis_size("dom")
    ctx_count = lax.axis_size("ctx")
    group, page_rows, _, width = cache_kv.shape
    y_count = ctx_count // Z
    tokens, q_width = q_new.shape
    kvh = width // HD
    shape = jax.ShapeDtypeStruct
    half, outgoing = pl.pallas_call(
        functools.partial(pack_kernel, dom_count),
        out_shape=(
            shape((prompt_kv.shape[0] // 2, 2 * width), jnp.bfloat16),
            shape((dom_count, RUN, page_rows, 2 * width), jnp.bfloat16),
        ),
        in_specs=[SMEM, VMEM, VMEM],
        out_specs=(VMEM, VMEM),
        compiler_params=params(),
        name="pack",
    )(ancestors, prompt_kv, cache_kv)

    pieces = [half] + [swap(half, "ctx", lambda i, k=k: i ^ (k * y_count)) for k in range(1, Z)]
    pieces += [swap(p, "ctx", lambda i, k=k: i ^ k) for k in range(1, y_count) for p in pieces[:Z]]
    pieces += [swap(p, "dom", lambda i: i ^ 1) for p in pieces]

    incoming = lax.all_to_all(outgoing, "dom", split_axis=0, concat_axis=0, tiled=True)
    routed = pl.pallas_call(
        route_kernel,
        out_shape=shape((group, page_rows, 2 * width), jnp.bfloat16),
        in_specs=[SMEM, VMEM],
        out_specs=VMEM,
        compiler_params=params(),
        name="route",
    )(ancestors, incoming)
    pages = lax.all_to_all(routed, "ctx", split_axis=0, concat_axis=0, tiled=True)
    pages = pages.reshape(ctx_count * page_rows, 2 * width)

    key_count = SPAN + sum(p.shape[0] for p in pieces)
    flops = 4 * tokens * q_width * key_count
    acc, top, total = pl.pallas_call(
        main_kernel,
        out_shape=(shape((tokens, q_width), jnp.float32),) * 3,
        in_specs=[VMEM] * (2 + len(pieces)),
        out_specs=(VMEM,) * 3,
        compiler_params=params(),
        cost_estimate=pl.CostEstimate(
            flops=flops, bytes_accessed=2**23, transcendentals=tokens * q_width // HD * key_count
        ),
        name="prompt_and_new",
    )(q_new, kv_new, *pieces)
    return pl.pallas_call(
        functools.partial(merge_kernel, group),
        out_shape=shape((tokens, q_width), jnp.bfloat16),
        in_specs=[SMEM, SMEM] + [VMEM] * 5,
        out_specs=pl.BlockSpec(memory_space=pl.ANY),
        scratch_shapes=[pltpu.VMEM((tokens, q_width), jnp.bfloat16), pltpu.SemaphoreType.DMA((kvh,))],
        compiler_params=params(),
        name="cache_and_merge",
    )(ancestors, lengths, q_new, pages, acc, top, total)


def solution(mesh):
    placed = (
        P(("dom", "ctx"), None),
        P(("dom", "ctx"), None, None),
        P("ctx", None, None),
        P("dom", "ctx", None, None),
        P(),
        P(),
    )
    return jax.shard_map(
        on_device, mesh=mesh, in_specs=placed, out_specs=P(("dom", "ctx"), None), check_vma=False
    )
```

```python
import functools

import jax
import jax.numpy as jnp
from jax import lax
from jax.experimental import pallas as pl
from jax.experimental.pallas import tpu as pltpu
from jax.sharding import PartitionSpec as P

HD = 128
SPAN = 128
PAGE = 8
RUN = 4
NEGATIVE = -1e30
SCALE2 = HD ** (-0.5) * 1.4426950408889634
VMEM = pl.BlockSpec(memory_space=pltpu.VMEM)
HBM = pl.BlockSpec(memory_space=pltpu.HBM)


def params(mib):
    return pltpu.CompilerParams(vmem_limit_bytes=mib * 2**20)


def pack_kernel(dom_count, anc_hbm, len_hbm, prompt_hbm, cache_hbm, half_ref, out_ref, source_ref, limit_ref, anc_ref, len_ref, prompt_ref, cache_ref, sems):
    group = cache_ref.shape[0]
    dom = lax.axis_index("dom")
    copies_of, rows, width = half_ref.shape
    from_row = pl.multiple_of((dom % 2) * rows, rows)
    prompt_in = pltpu.make_async_copy(prompt_hbm.at[pl.ds(from_row, rows)], prompt_ref, sems.at[0])
    anc_in = pltpu.make_async_copy(anc_hbm, anc_ref, sems.at[1])
    len_in = pltpu.make_async_copy(len_hbm, len_ref, sems.at[2])
    cache_in = pltpu.make_async_copy(cache_hbm, cache_ref, sems.at[3])
    anc_in.start()
    len_in.start()
    prompt_in.start()
    cache_in.start()
    prompt_in.wait()
    half = prompt_ref[...].reshape(rows, width)
    for at in range(copies_of):
        half_ref[at] = half
    runs = group // RUN
    anc_in.wait()
    len_in.wait()
    for run in range(runs):
        source = anc_ref[dom * group + run * RUN] // group
        source_ref[run] = jnp.full(source_ref.shape[1:], source.astype(jnp.float32)).astype(jnp.bfloat16)
    particle = dom * group + lax.axis_index("ctx")
    limit_ref[...] = jnp.full(limit_ref.shape, len_ref[anc_ref[particle]] * PAGE)
    cache_in.wait()

    def one(step, carry):
        first = step * RUN
        anchor = anc_ref[first]

        @pl.when(anchor // group == dom)
        def _():
            for slot in range(RUN):
                local = anc_ref[first + slot] % group
                out_ref[step // runs, slot] = cache_ref[local].reshape(cache_ref.shape[1], width)

        return carry

    lax.fori_loop(0, dom_count * runs, one, 0)


def route_kernel(source_ref, in_ref, out_ref):
    dom_count, _, rows, width = in_ref.shape
    for run in range(source_ref.shape[0]):
        mask = source_ref[run]
        for slot in range(RUN):
            picked = in_ref[0, slot]
            for dom in range(1, dom_count):
                here = jnp.concatenate([mask == dom] * (width // mask.shape[1]), axis=1)
                picked = jnp.where(here, in_ref[dom, slot], picked)
            out_ref[run * RUN + slot] = picked


def head_rows(q_ref, g, gq):
    return jnp.concatenate(
        [q_ref[:, (g * gq + j) * HD : (g * gq + j + 1) * HD] for j in range(gq)], axis=0
    )


def dot_nt(a, b):
    return lax.dot_general(a, b, (((1,), (1,)), ((), ())), preferred_element_type=jnp.float32)


def dot_nn(a, b):
    return lax.dot_general(a, b, (((1,), (0,)), ((), ())), preferred_element_type=jnp.float32)


def row_top(parts):
    top = None
    for part in parts:
        for at in range(0, part.shape[1], HD):
            block = part[:, at : at + HD]
            if block.shape[1] < HD:
                continue
            top = block if top is None else jnp.maximum(top, block)
    top = jnp.max(top, axis=1, keepdims=True)
    for part in parts:
        if part.shape[1] % HD:
            top = jnp.maximum(top, jnp.max(part[:, part.shape[1] // HD * HD :], axis=1, keepdims=True))
    return top


def first_kernel(q_ref, new_ref, half_ref, acc_ref, max_ref, sum_ref):
    width = new_ref.shape[2]
    kvh = width // HD
    gq = q_ref.shape[1] // width
    new = new_ref[...].reshape(SPAN, 2 * width)
    ones = jnp.ones((SPAN + half_ref.shape[0], HD), jnp.bfloat16)
    token = lax.broadcasted_iota(jnp.int32, (SPAN, SPAN), 0)
    key = lax.broadcasted_iota(jnp.int32, (SPAN, SPAN), 1)
    causal = key <= token
    for g in range(kvh):
        k_at = slice(g * HD, (g + 1) * HD)
        v_at = slice(width + g * HD, width + (g + 1) * HD)
        keys = jnp.concatenate([new[:, k_at], half_ref[:, k_at]], axis=0)
        values = jnp.concatenate([new[:, v_at], half_ref[:, v_at]], axis=0)
        values = jnp.concatenate([values, ones], axis=1)
        scores = dot_nt(head_rows(q_ref, g, gq), keys)
        weights, tops = [], []
        for j in range(gq):
            s = scores[j * SPAN : (j + 1) * SPAN]
            s_new = jnp.where(causal, s[:, :SPAN], NEGATIVE)
            s_old = s[:, SPAN:]
            top = row_top([s_new, s_old])
            s = jnp.concatenate([s_new, s_old], axis=1)
            weights.append(jnp.exp2((s - top) * SCALE2).astype(jnp.bfloat16))
            tops.append(top)
        out = dot_nn(jnp.concatenate(weights, axis=0), values)
        for j in range(gq):
            at = slice((g * gq + j) * HD, (g * gq + j + 1) * HD)
            rows = slice(j * SPAN, (j + 1) * SPAN)
            acc_ref[:, at] = out[rows, :HD]
            sum_ref[:, at] = out[rows, HD:]
            max_ref[:, at] = jnp.broadcast_to(tops[j], (SPAN, HD))


def last_kernel(limit_ref, q_ref, half_ref, cache_ref, acc_ref, max_ref, sum_ref, out_ref, stage, sems):
    width = cache_ref.shape[1] // 2
    gen = cache_ref.shape[0]
    other = half_ref.shape[0]
    kvh = width // HD
    gq = q_ref.shape[1] // width
    visible = lax.broadcasted_iota(jnp.int32, (SPAN, gen), 1) < jnp.broadcast_to(limit_ref[:1], (SPAN, gen))
    ones = jnp.ones((other + gen, HD), jnp.bfloat16)
    copies = []
    for g in range(kvh):
        k_at = slice(g * HD, (g + 1) * HD)
        v_at = slice(width + g * HD, width + (g + 1) * HD)
        keys = jnp.concatenate([half_ref[:, k_at], cache_ref[:, k_at]], axis=0)
        values = jnp.concatenate([half_ref[:, v_at], cache_ref[:, v_at]], axis=0)
        values = jnp.concatenate([values, ones], axis=1)
        scores = dot_nt(head_rows(q_ref, g, gq), keys)
        weights, factors = [], []
        for j in range(gq):
            at = slice((g * gq + j) * HD, (g * gq + j + 1) * HD)
            s = scores[j * SPAN : (j + 1) * SPAN]
            s_cache = jnp.where(visible, s[:, other:], NEGATIVE)
            before = max_ref[:, at]
            top = jnp.maximum(before[:, :1], row_top([s[:, :other], s_cache]))
            s = jnp.concatenate([s[:, :other], s_cache], axis=1)
            weights.append(jnp.exp2((s - top) * SCALE2).astype(jnp.bfloat16))
            factors.append(jnp.exp2((before - top) * SCALE2))
        out = dot_nn(jnp.concatenate(weights, axis=0), values)
        for j in range(gq):
            at = slice((g * gq + j) * HD, (g * gq + j + 1) * HD)
            rows = slice(j * SPAN, (j + 1) * SPAN)
            total = sum_ref[:, at] * factors[j] + out[rows, HD:]
            value = acc_ref[:, at] * factors[j] + out[rows, :HD]
            stage[:, at] = (value / total).astype(jnp.bfloat16)
        columns = pl.ds(g * gq * HD, gq * HD)
        copy = pltpu.make_async_copy(stage.at[:, columns], out_ref.at[:, columns], sems.at[g])
        copy.start()
        copies.append(copy)
    for copy in copies:
        copy.wait()


def on_device(q_new, kv_new, prompt_kv, cache_kv, ancestors, lengths):
    dom_count = lax.axis_size("dom")
    ctx_count = lax.axis_size("ctx")
    group, page_rows, _, width = cache_kv.shape
    tokens, q_width = q_new.shape
    kvh = width // HD
    half_rows = prompt_kv.shape[0] // 2
    shape = jax.ShapeDtypeStruct
    halves, outgoing, sources, limit = pl.pallas_call(
        functools.partial(pack_kernel, dom_count),
        out_shape=(
            shape((ctx_count, half_rows, 2 * width), jnp.bfloat16),
            shape((dom_count, RUN, page_rows, 2 * width), jnp.bfloat16),
            shape((group // RUN, page_rows, HD), jnp.bfloat16),
            shape((8, ctx_count * page_rows), jnp.int32),
        ),
        in_specs=[HBM] * 4,
        out_specs=(VMEM,) * 4,
        scratch_shapes=[
            pltpu.SMEM(ancestors.shape, jnp.int32),
            pltpu.SMEM(lengths.shape, jnp.int32),
            pltpu.VMEM((half_rows, 2, width), jnp.bfloat16),
            pltpu.VMEM(cache_kv.shape, jnp.bfloat16),
            pltpu.SemaphoreType.DMA((4,)),
        ],
        compiler_params=params(16),
        name="pack",
    )(*(pltpu.with_memory_space_constraint(x, pltpu.HBM) for x in (ancestors, lengths, prompt_kv, cache_kv)))

    own_half = lax.all_to_all(halves, "ctx", split_axis=0, concat_axis=0, tiled=True)
    own_half = own_half.reshape(ctx_count * half_rows, 2 * width)
    other_half = lax.ppermute(own_half, "dom", [(i, i ^ 1) for i in range(dom_count)])

    incoming = lax.all_to_all(outgoing, "dom", split_axis=0, concat_axis=0, tiled=True)
    routed = pl.pallas_call(
        route_kernel,
        out_shape=shape((group, page_rows, 2 * width), jnp.bfloat16),
        in_specs=[VMEM, VMEM],
        out_specs=VMEM,
        compiler_params=params(12),
        name="route",
    )(sources, incoming)
    pages = lax.all_to_all(routed, "ctx", split_axis=0, concat_axis=0, tiled=True)
    pages = pages.reshape(ctx_count * page_rows, 2 * width)

    key_count = SPAN + own_half.shape[0]
    acc, top, total = pl.pallas_call(
        first_kernel,
        out_shape=(shape((tokens, q_width), jnp.float32),) * 3,
        in_specs=[VMEM] * 3,
        out_specs=(VMEM,) * 3,
        compiler_params=params(24),
        cost_estimate=pl.CostEstimate(
            flops=4 * tokens * q_width * key_count,
            bytes_accessed=2**23,
            transcendentals=tokens * q_width // HD * key_count,
        ),
        name="new_and_own_half",
    )(q_new, kv_new, own_half)
    return pl.pallas_call(
        last_kernel,
        out_shape=shape((tokens, q_width), jnp.bfloat16),
        in_specs=[VMEM] * 7,
        out_specs=HBM,
        scratch_shapes=[pltpu.VMEM((tokens, q_width), jnp.bfloat16), pltpu.SemaphoreType.DMA((kvh,))],
        compiler_params=params(24),
        name="other_half_and_cache",
    )(limit, q_new, other_half, pages, acc, top, total)


def solution(mesh):
    placed = (
        P(("dom", "ctx"), None),
        P(("dom", "ctx"), None, None),
        P("ctx", None, None),
        P("dom", "ctx", None, None),
        P(),
        P(),
    )
    return jax.shard_map(
        on_device, mesh=mesh, in_specs=placed, out_specs=P(("dom", "ctx"), None), check_vma=False
    )
```

```python
import functools

import jax
import jax.numpy as jnp
from jax import lax
from jax.experimental import pallas as pl
from jax.experimental.pallas import tpu as pltpu
from jax.sharding import PartitionSpec as P

HD = 128
SPAN = 128
PAGE = 8
RUN = 4
NEGATIVE = -1e30
SCALE2 = HD ** (-0.5) * 1.4426950408889634
VMEM = pl.BlockSpec(memory_space=pltpu.VMEM)
HBM = pl.BlockSpec(memory_space=pltpu.HBM)


def params(mib):
    return pltpu.CompilerParams(vmem_limit_bytes=mib * 2**20)


def pack_kernel(dom_count, anc_hbm, len_hbm, prompt_hbm, cache_hbm, halves_hbm, out_hbm, source_ref, limit_ref, anc_ref, len_ref, prompt_ref, half_ref, cache_ref, out_ref, sems):
    group = cache_ref.shape[0]
    dom = lax.axis_index("dom")
    rows, width = half_ref.shape
    from_row = pl.multiple_of((dom % 2) * rows, rows)
    prompt_in = pltpu.make_async_copy(prompt_hbm.at[pl.ds(from_row, rows)], prompt_ref, sems.at[0])
    anc_in = pltpu.make_async_copy(anc_hbm, anc_ref, sems.at[1])
    len_in = pltpu.make_async_copy(len_hbm, len_ref, sems.at[2])
    cache_in = pltpu.make_async_copy(cache_hbm, cache_ref, sems.at[3])
    anc_in.start()
    len_in.start()
    prompt_in.start()
    cache_in.start()
    prompt_in.wait()
    half_ref[...] = prompt_ref[...].reshape(rows, width)
    halves_out = [
        pltpu.make_async_copy(half_ref, halves_hbm.at[at], sems.at[5 + at]) for at in range(halves_hbm.shape[0])
    ]
    for copy in halves_out:
        copy.start()
    runs = group // RUN
    anc_in.wait()
    len_in.wait()
    for run in range(runs):
        source = anc_ref[dom * group + run * RUN] // group
        source_ref[run] = jnp.full(source_ref.shape[1:], source.astype(jnp.float32)).astype(jnp.bfloat16)
    particle = dom * group + lax.axis_index("ctx")
    limit_ref[...] = jnp.full(limit_ref.shape, len_ref[anc_ref[particle]] * PAGE)
    cache_in.wait()

    def one(step, carry):
        first = step * RUN
        anchor = anc_ref[first]

        @pl.when(anchor // group == dom)
        def _():
            for slot in range(RUN):
                local = anc_ref[first + slot] % group
                out_ref[step // runs, slot] = cache_ref[local].reshape(cache_ref.shape[1], width)

        return carry

    lax.fori_loop(0, dom_count * runs, one, 0)
    out = pltpu.make_async_copy(out_ref, out_hbm, sems.at[4])
    out.start()
    for copy in halves_out:
        copy.wait()
    out.wait()


def route_kernel(source_ref, in_ref, out_hbm, out_ref, sem):
    dom_count, _, rows, width = in_ref.shape
    for run in range(source_ref.shape[0]):
        mask = source_ref[run]
        for slot in range(RUN):
            picked = in_ref[0, slot]
            for dom in range(1, dom_count):
                here = jnp.concatenate([mask == dom] * (width // mask.shape[1]), axis=1)
                picked = jnp.where(here, in_ref[dom, slot], picked)
            out_ref[run * RUN + slot] = picked
    out = pltpu.make_async_copy(out_ref, out_hbm, sem)
    out.start()
    out.wait()


def head_rows(q_ref, g, gq):
    return jnp.concatenate(
        [q_ref[:, (g * gq + j) * HD : (g * gq + j + 1) * HD] for j in range(gq)], axis=0
    )


def dot(a, b, contract):
    return lax.dot_general(a, b, (contract, ((), ())), preferred_element_type=jnp.float32)


def first_kernel(q_ref, new_ref, half_ref, acc_ref, max_ref, sum_ref):
    width = new_ref.shape[2]
    kvh = width // HD
    gq = q_ref.shape[1] // width
    rows = gq * SPAN
    new = new_ref[...].reshape(SPAN, 2 * width)
    key = lax.broadcasted_iota(jnp.int32, (SPAN, rows), 0)
    token = lax.broadcasted_iota(jnp.int32, (SPAN, rows), 1) % SPAN
    causal = key <= token
    for g in range(kvh):
        k_at = slice(g * HD, (g + 1) * HD)
        v_at = slice(width + g * HD, width + (g + 1) * HD)
        at = slice(g * rows, (g + 1) * rows)
        keys = jnp.concatenate([new[:, k_at], half_ref[:, k_at]], axis=0)
        values = jnp.concatenate([new[:, v_at], half_ref[:, v_at]], axis=0)
        s = dot(keys, head_rows(q_ref, g, gq), ((1,), (1,)))
        s = jnp.concatenate([jnp.where(causal, s[:SPAN], NEGATIVE), s[SPAN:]], axis=0)
        top = jnp.max(s, axis=0, keepdims=True)
        weights = jnp.exp2((s - top) * SCALE2)
        acc_ref[:, at] = dot(values, weights.astype(jnp.bfloat16), ((0,), (0,)))
        sum_ref[:, at] = jnp.sum(weights, axis=0, keepdims=True)
        max_ref[:, at] = top


def last_kernel(limit_ref, q_ref, half_ref, cache_ref, acc_ref, max_ref, sum_ref, out_ref, stage, sems):
    width = cache_ref.shape[1] // 2
    gen = cache_ref.shape[0]
    other = half_ref.shape[0]
    kvh = width // HD
    gq = q_ref.shape[1] // width
    rows = gq * SPAN
    limit = jnp.concatenate([limit_ref[...]] * (rows // limit_ref.shape[1]), axis=1)
    visible = lax.broadcasted_iota(jnp.int32, (gen, rows), 0) < limit
    unit = lax.broadcasted_iota(jnp.int32, (HD, HD), 0) == lax.broadcasted_iota(jnp.int32, (HD, HD), 1)
    unit = unit.astype(jnp.float32).astype(jnp.bfloat16)
    copies = []
    for g in range(kvh):
        k_at = slice(g * HD, (g + 1) * HD)
        v_at = slice(width + g * HD, width + (g + 1) * HD)
        at = slice(g * rows, (g + 1) * rows)
        keys = jnp.concatenate([half_ref[:, k_at], cache_ref[:, k_at]], axis=0)
        values = jnp.concatenate([half_ref[:, v_at], cache_ref[:, v_at]], axis=0)
        s = dot(keys, head_rows(q_ref, g, gq), ((1,), (1,)))
        s = jnp.concatenate([s[:other], jnp.where(visible, s[other:], NEGATIVE)], axis=0)
        before = max_ref[:, at]
        top = jnp.maximum(before, jnp.max(s, axis=0, keepdims=True))
        weights = jnp.exp2((s - top) * SCALE2)
        factor = jnp.exp2((before - top) * SCALE2)
        value = acc_ref[:, at] * factor + dot(values, weights.astype(jnp.bfloat16), ((0,), (0,)))
        total = sum_ref[:, at] * factor + jnp.sum(weights, axis=0, keepdims=True)
        value = (value * (1.0 / total)).astype(jnp.bfloat16)
        for j in range(gq):
            turned = dot(unit, value[:, j * SPAN : (j + 1) * SPAN], ((1,), (1,)))
            stage[:, g * rows + j * HD : g * rows + (j + 1) * HD] = turned.astype(jnp.bfloat16)
        columns = pl.ds(g * gq * HD, gq * HD)
        copy = pltpu.make_async_copy(stage.at[:, columns], out_ref.at[:, columns], sems.at[g])
        copy.start()
        copies.append(copy)
    for copy in copies:
        copy.wait()


def on_device(q_new, kv_new, prompt_kv, cache_kv, ancestors, lengths):
    dom_count = lax.axis_size("dom")
    ctx_count = lax.axis_size("ctx")
    group, page_rows, _, width = cache_kv.shape
    tokens, q_width = q_new.shape
    kvh = width // HD
    q_rows = tokens * q_width // width
    half_rows = prompt_kv.shape[0] // 2
    shape = jax.ShapeDtypeStruct
    halves, outgoing, sources, limit = pl.pallas_call(
        functools.partial(pack_kernel, dom_count),
        out_shape=(
            pltpu.HBM((ctx_count, half_rows, 2 * width), jnp.bfloat16),
            pltpu.HBM((dom_count, RUN, page_rows, 2 * width), jnp.bfloat16),
            shape((group // RUN, page_rows, HD), jnp.bfloat16),
            shape((1, 128), jnp.int32),
        ),
        in_specs=[HBM] * 4,
        out_specs=(HBM, HBM, VMEM, VMEM),
        scratch_shapes=[
            pltpu.SMEM(ancestors.shape, jnp.int32),
            pltpu.SMEM(lengths.shape, jnp.int32),
            pltpu.VMEM((half_rows, 2, width), jnp.bfloat16),
            pltpu.VMEM((half_rows, 2 * width), jnp.bfloat16),
            pltpu.VMEM(cache_kv.shape, jnp.bfloat16),
            pltpu.VMEM((dom_count, RUN, page_rows, 2 * width), jnp.bfloat16),
            pltpu.SemaphoreType.DMA((5 + ctx_count,)),
        ],
        compiler_params=params(16),
        name="pack",
    )(*(pltpu.with_memory_space_constraint(x, pltpu.HBM) for x in (ancestors, lengths, prompt_kv, cache_kv)))

    own_half = lax.all_to_all(halves, "ctx", split_axis=0, concat_axis=0, tiled=True)
    own_half = own_half.reshape(ctx_count * half_rows, 2 * width)
    other_half = lax.ppermute(own_half, "dom", [(i, i ^ 1) for i in range(dom_count)])

    incoming = lax.all_to_all(outgoing, "dom", split_axis=0, concat_axis=0, tiled=True)
    routed = pl.pallas_call(
        route_kernel,
        out_shape=pltpu.HBM((group, page_rows, 2 * width), jnp.bfloat16),
        in_specs=[VMEM, VMEM],
        out_specs=HBM,
        scratch_shapes=[pltpu.VMEM((group, page_rows, 2 * width), jnp.bfloat16), pltpu.SemaphoreType.DMA],
        compiler_params=params(12),
        name="route",
    )(sources, incoming)
    pages = lax.all_to_all(routed, "ctx", split_axis=0, concat_axis=0, tiled=True)
    pages = pages.reshape(ctx_count * page_rows, 2 * width)

    key_count = SPAN + own_half.shape[0]
    acc, top, total = pl.pallas_call(
        first_kernel,
        out_shape=(
            shape((HD, kvh * q_rows), jnp.float32),
            shape((1, kvh * q_rows), jnp.float32),
            shape((1, kvh * q_rows), jnp.float32),
        ),
        in_specs=[VMEM] * 3,
        out_specs=(VMEM,) * 3,
        compiler_params=params(16),
        cost_estimate=pl.CostEstimate(
            flops=4 * tokens * q_width * key_count,
            bytes_accessed=2**23,
            transcendentals=tokens * q_width // HD * key_count,
        ),
        name="new_and_own_half",
    )(q_new, kv_new, own_half)
    return pl.pallas_call(
        last_kernel,
        out_shape=shape((tokens, q_width), jnp.bfloat16),
        in_specs=[VMEM] * 7,
        out_specs=HBM,
        scratch_shapes=[pltpu.VMEM((tokens, q_width), jnp.bfloat16), pltpu.SemaphoreType.DMA((kvh,))],
        compiler_params=params(16),
        name="other_half_and_cache",
    )(limit, q_new, other_half, pages, acc, top, total)


def solution(mesh):
    placed = (
        P(("dom", "ctx"), None),
        P(("dom", "ctx"), None, None),
        P("ctx", None, None),
        P("dom", "ctx", None, None),
        P(),
        P(),
    )
    return jax.shard_map(
        on_device, mesh=mesh, in_specs=placed, out_specs=P(("dom", "ctx"), None), check_vma=False
    )
```

```python
import functools

import jax
import jax.numpy as jnp
from jax import lax
from jax.experimental import pallas as pl
from jax.experimental.pallas import tpu as pltpu
from jax.sharding import PartitionSpec as P

HD = 128
SPAN = 128
PAGE = 8
RUN = 4
Z = 4
NEGATIVE = -1e30
SCALE2 = HD ** (-0.5) * 1.4426950408889634
VMEM = pl.BlockSpec(memory_space=pltpu.VMEM)
HBM = pl.BlockSpec(memory_space=pltpu.HBM)


def params(mib):
    return pltpu.CompilerParams(vmem_limit_bytes=mib * 2**20)


def pack_kernel(dom_count, anc_hbm, len_hbm, prompt_hbm, cache_hbm, half_ref, *refs):
    out_refs = refs[:dom_count]
    far_ref, limit_ref, anc_ref, len_ref, prompt_ref, cache_ref, sems = refs[dom_count:]
    group = cache_ref.shape[0]
    dom = lax.axis_index("dom")
    rows, width = half_ref.shape
    from_row = pl.multiple_of((dom % 2) * rows, rows)
    prompt_in = pltpu.make_async_copy(prompt_hbm.at[pl.ds(from_row, rows)], prompt_ref, sems.at[0])
    anc_in = pltpu.make_async_copy(anc_hbm, anc_ref, sems.at[1])
    len_in = pltpu.make_async_copy(len_hbm, len_ref, sems.at[2])
    cache_in = pltpu.make_async_copy(cache_hbm, cache_ref, sems.at[3])
    prompt_in.start()
    anc_in.start()
    len_in.start()
    cache_in.start()
    runs = group // RUN
    anc_in.wait()
    len_in.wait()
    for run in range(runs):
        far = (anc_ref[dom * group + run * RUN] // group) ^ dom
        far_ref[run] = jnp.full(far_ref.shape[1:], far.astype(jnp.float32)).astype(jnp.bfloat16)
    particle = dom * group + lax.axis_index("ctx")
    limit_ref[...] = jnp.full(limit_ref.shape, len_ref[anc_ref[particle]] * PAGE)
    prompt_in.wait()
    half_ref[...] = prompt_ref[...].reshape(rows, width)
    cache_in.wait()
    for k, out_ref in enumerate(out_refs):
        for run in range(runs):
            first = (dom ^ k) * group + run * RUN

            @pl.when(anc_ref[first] // group == dom)
            def _(first=first, out_ref=out_ref):
                for slot in range(RUN):
                    local = anc_ref[first + slot] % group
                    out_ref[slot] = cache_ref[local].reshape(cache_ref.shape[1], width)


def route_kernel(far_ref, *refs):
    *in_refs, out_hbm, out_ref, sem = refs
    width = out_ref.shape[2]
    for run in range(far_ref.shape[0]):
        far = far_ref[run]
        for slot in range(RUN):
            picked = in_refs[0][slot]
            for k in range(1, len(in_refs)):
                here = jnp.concatenate([far == k] * (width // far.shape[1]), axis=1)
                picked = jnp.where(here, in_refs[k][slot], picked)
            out_ref[run * RUN + slot] = picked
    out = pltpu.make_async_copy(out_ref, out_hbm, sem)
    out.start()
    out.wait()


def head_rows(q_ref, g, gq):
    return jnp.concatenate(
        [q_ref[:, (g * gq + j) * HD : (g * gq + j + 1) * HD] for j in range(gq)], axis=0
    )


def dot_nt(a, b):
    return lax.dot_general(a, b, (((1,), (1,)), ((), ())), preferred_element_type=jnp.float32)


def dot_nn(a, b):
    return lax.dot_general(a, b, (((1,), (0,)), ((), ())), preferred_element_type=jnp.float32)


def attend_kernel(limit_ref, q_ref, new_ref, cache_ref, *refs):
    *pieces, out_ref, stage, sems = refs
    width = new_ref.shape[2]
    gen = cache_ref.shape[0]
    kvh = width // HD
    gq = q_ref.shape[1] // width
    new = new_ref[...].reshape(SPAN, 2 * width)
    old = sum(p.shape[0] for p in pieces)
    ones = jnp.ones((SPAN + old + gen, HD), jnp.bfloat16)
    token = lax.broadcasted_iota(jnp.int32, (SPAN, SPAN), 0)
    causal = lax.broadcasted_iota(jnp.int32, (SPAN, SPAN), 1) <= token
    visible = lax.broadcasted_iota(jnp.int32, (SPAN, gen), 1) < jnp.broadcast_to(limit_ref[:1], (SPAN, gen))
    copies = []
    for g in range(kvh):
        k_at = slice(g * HD, (g + 1) * HD)
        v_at = slice(width + g * HD, width + (g + 1) * HD)
        keys = jnp.concatenate([new[:, k_at]] + [p[:, k_at] for p in pieces] + [cache_ref[:, k_at]], axis=0)
        values = jnp.concatenate([new[:, v_at]] + [p[:, v_at] for p in pieces] + [cache_ref[:, v_at]], axis=0)
        values = jnp.concatenate([values, ones], axis=1)
        scores = dot_nt(head_rows(q_ref, g, gq), keys)
        weights = []
        for j in range(gq):
            s = scores[j * SPAN : (j + 1) * SPAN]
            s_new = jnp.where(causal, s[:, :SPAN], NEGATIVE)
            s_cache = jnp.where(visible, s[:, SPAN + old :], NEGATIVE)
            s = jnp.concatenate([s_new, s[:, SPAN : SPAN + old], s_cache], axis=1)
            top = jnp.max(s, axis=1, keepdims=True)
            weights.append(jnp.exp2((s - top) * SCALE2).astype(jnp.bfloat16))
        out = dot_nn(jnp.concatenate(weights, axis=0), values)
        out = (out[:, :HD] / out[:, HD:]).astype(jnp.bfloat16)
        for j in range(gq):
            stage[:, (g * gq + j) * HD : (g * gq + j + 1) * HD] = out[j * SPAN : (j + 1) * SPAN]
        columns = pl.ds(g * gq * HD, gq * HD)
        copy = pltpu.make_async_copy(stage.at[:, columns], out_ref.at[:, columns], sems.at[g])
        copy.start()
        copies.append(copy)
    for copy in copies:
        copy.wait()


def swap(x, axis, distance):
    return lax.ppermute(x, axis, [(i, i ^ distance) for i in range(lax.axis_size(axis))])


def on_device(q_new, kv_new, prompt_kv, cache_kv, ancestors, lengths):
    dom_count = lax.axis_size("dom")
    ctx_count = lax.axis_size("ctx")
    y_count = ctx_count // Z
    group, page_rows, _, width = cache_kv.shape
    tokens, q_width = q_new.shape
    kvh = width // HD
    half_rows = prompt_kv.shape[0] // 2
    shape = jax.ShapeDtypeStruct
    half, *rest = pl.pallas_call(
        functools.partial(pack_kernel, dom_count),
        out_shape=(
            shape((half_rows, 2 * width), jnp.bfloat16),
            *[shape((RUN, page_rows, 2 * width), jnp.bfloat16)] * dom_count,
            shape((group // RUN, page_rows, HD), jnp.bfloat16),
            shape((8, ctx_count * page_rows), jnp.int32),
        ),
        in_specs=[HBM] * 4,
        out_specs=(VMEM,) * (3 + dom_count),
        scratch_shapes=[
            pltpu.SMEM(ancestors.shape, jnp.int32),
            pltpu.SMEM(lengths.shape, jnp.int32),
            pltpu.VMEM((half_rows, 2, width), jnp.bfloat16),
            pltpu.VMEM(cache_kv.shape, jnp.bfloat16),
            pltpu.SemaphoreType.DMA((4,)),
        ],
        compiler_params=params(12),
        name="pack",
    )(*(pltpu.with_memory_space_constraint(x, pltpu.HBM) for x in (ancestors, lengths, prompt_kv, cache_kv)))
    outgoing, far, limit = rest[:dom_count], rest[dom_count], rest[dom_count + 1]

    pieces = [half] + [swap(half, "ctx", k * y_count) for k in range(1, Z)]
    pieces += [swap(p, "ctx", k) for k in range(1, y_count) for p in pieces[:Z]]
    pieces += [swap(p, "dom", 1) for p in pieces]

    incoming = outgoing[:1] + [swap(outgoing[k], "dom", k) for k in range(1, dom_count)]
    routed = pl.pallas_call(
        route_kernel,
        out_shape=pltpu.HBM((group, page_rows, 2 * width), jnp.bfloat16),
        in_specs=[VMEM] * (1 + dom_count),
        out_specs=HBM,
        scratch_shapes=[pltpu.VMEM((group, page_rows, 2 * width), jnp.bfloat16), pltpu.SemaphoreType.DMA],
        compiler_params=params(12),
        name="route",
    )(far, *incoming)
    pages = lax.all_to_all(routed, "ctx", split_axis=0, concat_axis=0, tiled=True)
    pages = pages.reshape(ctx_count * page_rows, 2 * width)

    return pl.pallas_call(
        attend_kernel,
        out_shape=shape((tokens, q_width), jnp.bfloat16),
        in_specs=[VMEM] * (4 + len(pieces)),
        out_specs=HBM,
        scratch_shapes=[pltpu.VMEM((tokens, q_width), jnp.bfloat16), pltpu.SemaphoreType.DMA((kvh,))],
        compiler_params=params(40 if prompt_kv.shape[0] * ctx_count > 1024 else 24),
        name="attend",
    )(limit, q_new, kv_new, pages, *pieces)


def solution(mesh):
    placed = (
        P(("dom", "ctx"), None),
        P(("dom", "ctx"), None, None),
        P("ctx", None, None),
        P("dom", "ctx", None, None),
        P(),
        P(),
    )
    return jax.shard_map(
        on_device, mesh=mesh, in_specs=placed, out_specs=P(("dom", "ctx"), None), check_vma=False
    )
```

```python
import functools

import jax
import jax.numpy as jnp
from jax import lax
from jax.experimental import pallas as pl
from jax.experimental.pallas import tpu as pltpu
from jax.sharding import PartitionSpec as P

HD = 128
SPAN = 128
PAGE = 8
RUN = 4
Z = 4
NEGATIVE = -1e30
SCALE2 = HD ** (-0.5) * 1.4426950408889634
VMEM = pl.BlockSpec(memory_space=pltpu.VMEM)
HBM = pl.BlockSpec(memory_space=pltpu.HBM)


def params(mib):
    return pltpu.CompilerParams(vmem_limit_bytes=mib * 2**20)


def pack_kernel(dom_count, anc_hbm, len_hbm, prompt_hbm, cache_hbm, half_ref, *refs):
    out_refs = refs[:dom_count]
    far_ref, limit_ref, anc_ref, len_ref, prompt_ref, cache_ref, sems = refs[dom_count:]
    group = cache_ref.shape[0]
    dom = lax.axis_index("dom")
    rows, width = half_ref.shape
    from_row = pl.multiple_of((dom % 2) * rows, rows)
    prompt_in = pltpu.make_async_copy(prompt_hbm.at[pl.ds(from_row, rows)], prompt_ref, sems.at[0])
    anc_in = pltpu.make_async_copy(anc_hbm, anc_ref, sems.at[1])
    len_in = pltpu.make_async_copy(len_hbm, len_ref, sems.at[2])
    cache_in = pltpu.make_async_copy(cache_hbm, cache_ref, sems.at[3])
    prompt_in.start()
    anc_in.start()
    len_in.start()
    cache_in.start()
    runs = group // RUN
    anc_in.wait()
    len_in.wait()
    for run in range(runs):
        far = (anc_ref[dom * group + run * RUN] // group) ^ dom
        far_ref[run] = jnp.full(far_ref.shape[1:], far.astype(jnp.float32)).astype(jnp.bfloat16)
    particle = dom * group + lax.axis_index("ctx")
    limit_ref[...] = jnp.full(limit_ref.shape, len_ref[anc_ref[particle]] * PAGE)
    prompt_in.wait()
    half_ref[...] = prompt_ref[...].reshape(rows, width)
    cache_in.wait()
    for k, out_ref in enumerate(out_refs):
        for run in range(runs):
            first = (dom ^ k) * group + run * RUN

            @pl.when(anc_ref[first] // group == dom)
            def _(first=first, out_ref=out_ref):
                for slot in range(RUN):
                    local = anc_ref[first + slot] % group
                    out_ref[slot] = cache_ref[local].reshape(cache_ref.shape[1], width)


def route_kernel(y_count, far_ref, *refs):
    in_refs, out_refs = refs[:-Z], refs[-Z:]
    own_z = lax.axis_index("ctx") // y_count
    width = out_refs[0].shape[2]
    for k, out_ref in enumerate(out_refs):
        for y in range(y_count):
            to = (own_z ^ k) * y_count + y
            far = far_ref[to // RUN]
            picked = in_refs[0][to % RUN]
            for at in range(1, len(in_refs)):
                here = jnp.concatenate([far == at] * (width // far.shape[1]), axis=1)
                picked = jnp.where(here, in_refs[at][to % RUN], picked)
            out_ref[y] = picked


def turn_kernel(q_hbm, *refs):
    in_refs, out_refs, (q_ref, sem) = refs[:Z], refs[Z:-2], refs[-2:]
    q_in = pltpu.make_async_copy(q_hbm, q_ref, sem)
    q_in.start()
    own_y = lax.axis_index("ctx") % len(out_refs)
    for j, out_ref in enumerate(out_refs):
        for k, in_ref in enumerate(in_refs):
            out_ref[k] = in_ref[own_y ^ j]
    q_in.wait()


def head_rows(q_ref, g, gq):
    return jnp.concatenate(
        [q_ref[:, (g * gq + j) * HD : (g * gq + j + 1) * HD] for j in range(gq)], axis=0
    )


def dot_nt(a, b):
    return lax.dot_general(a, b, (((1,), (1,)), ((), ())), preferred_element_type=jnp.float32)


def dot_nn(a, b):
    return lax.dot_general(a, b, (((1,), (0,)), ((), ())), preferred_element_type=jnp.float32)


def attend_kernel(y_count, limit_ref, q_ref, new_ref, *refs):
    pages, pieces, (out_ref, stage, sems) = refs[:y_count], refs[y_count:-3], refs[-3:]
    width = new_ref.shape[2]
    page_rows = pages[0].shape[0] // Z
    gen = page_rows * Z * y_count
    kvh = width // HD
    gq = q_ref.shape[1] // width
    new = new_ref[...].reshape(SPAN, 2 * width)
    old = sum(p.shape[0] for p in pieces)
    ones = jnp.ones((SPAN + old + gen, HD), jnp.bfloat16)
    token = lax.broadcasted_iota(jnp.int32, (SPAN, SPAN), 0)
    causal = lax.broadcasted_iota(jnp.int32, (SPAN, SPAN), 1) <= token
    at = lax.broadcasted_iota(jnp.int32, (SPAN, gen), 1)
    ctx = lax.axis_index("ctx")
    page_z = (at // page_rows % Z) ^ (ctx // y_count)
    page_y = (at // (page_rows * Z)) ^ (ctx % y_count)
    at = (page_z * y_count + page_y) * page_rows + at % page_rows
    visible = at < jnp.broadcast_to(limit_ref[:1], (SPAN, gen))
    copies = []
    for g in range(kvh):
        k_at = slice(g * HD, (g + 1) * HD)
        v_at = slice(width + g * HD, width + (g + 1) * HD)
        keys = jnp.concatenate([new[:, k_at]] + [p[:, k_at] for p in (*pieces, *pages)], axis=0)
        values = jnp.concatenate([new[:, v_at]] + [p[:, v_at] for p in (*pieces, *pages)], axis=0)
        values = jnp.concatenate([values, ones], axis=1)
        scores = dot_nt(head_rows(q_ref, g, gq), keys)
        weights = []
        for j in range(gq):
            s = scores[j * SPAN : (j + 1) * SPAN]
            s_new = jnp.where(causal, s[:, :SPAN], NEGATIVE)
            s_cache = jnp.where(visible, s[:, SPAN + old :], NEGATIVE)
            s = jnp.concatenate([s_new, s[:, SPAN : SPAN + old], s_cache], axis=1)
            top = jnp.max(s, axis=1, keepdims=True)
            weights.append(jnp.exp2((s - top) * SCALE2).astype(jnp.bfloat16))
        out = dot_nn(jnp.concatenate(weights, axis=0), values)
        out = (out[:, :HD] / out[:, HD:]).astype(jnp.bfloat16)
        for j in range(gq):
            stage[:, (g * gq + j) * HD : (g * gq + j + 1) * HD] = out[j * SPAN : (j + 1) * SPAN]
        columns = pl.ds(g * gq * HD, gq * HD)
        copy = pltpu.make_async_copy(stage.at[:, columns], out_ref.at[:, columns], sems.at[g])
        copy.start()
        copies.append(copy)
    for copy in copies:
        copy.wait()


def swap(x, axis, distance):
    return lax.ppermute(x, axis, [(i, i ^ distance) for i in range(lax.axis_size(axis))])


def on_device(q_new, kv_new, prompt_kv, cache_kv, ancestors, lengths):
    dom_count = lax.axis_size("dom")
    ctx_count = lax.axis_size("ctx")
    y_count = ctx_count // Z
    group, page_rows, _, width = cache_kv.shape
    tokens, q_width = q_new.shape
    kvh = width // HD
    half_rows = prompt_kv.shape[0] // 2
    shape = jax.ShapeDtypeStruct
    half, *rest = pl.pallas_call(
        functools.partial(pack_kernel, dom_count),
        out_shape=(
            shape((half_rows, 2 * width), jnp.bfloat16),
            *[shape((RUN, page_rows, 2 * width), jnp.bfloat16)] * dom_count,
            shape((group // RUN, page_rows, HD), jnp.bfloat16),
            shape((8, ctx_count * page_rows), jnp.int32),
        ),
        in_specs=[HBM] * 4,
        out_specs=(VMEM,) * (3 + dom_count),
        scratch_shapes=[
            pltpu.SMEM(ancestors.shape, jnp.int32),
            pltpu.SMEM(lengths.shape, jnp.int32),
            pltpu.VMEM((half_rows, 2, width), jnp.bfloat16),
            pltpu.VMEM(cache_kv.shape, jnp.bfloat16),
            pltpu.SemaphoreType.DMA((4,)),
        ],
        compiler_params=params(12),
        name="pack",
    )(*(pltpu.with_memory_space_constraint(x, pltpu.HBM) for x in (ancestors, lengths, prompt_kv, cache_kv)))
    outgoing, far, limit = rest[:dom_count], rest[dom_count], rest[dom_count + 1]

    pieces = [half] + [swap(half, "ctx", k * y_count) for k in range(1, Z)]
    pieces += [swap(p, "ctx", k) for k in range(1, y_count) for p in pieces[:Z]]
    pieces += [swap(p, "dom", 1) for p in pieces]

    incoming = outgoing[:1] + [swap(outgoing[k], "dom", k) for k in range(1, dom_count)]
    routed = pl.pallas_call(
        functools.partial(route_kernel, y_count),
        out_shape=(shape((y_count, page_rows, 2 * width), jnp.bfloat16),) * Z,
        in_specs=[VMEM] * (1 + dom_count),
        out_specs=(VMEM,) * Z,
        compiler_params=params(12),
        name="route",
    )(far, *incoming)
    routed = routed[:1] + tuple(swap(routed[k], "ctx", k * y_count) for k in range(1, Z))
    *pages, q_new = pl.pallas_call(
        turn_kernel,
        out_shape=(shape((Z, page_rows, 2 * width), jnp.bfloat16),) * y_count + (shape(q_new.shape, q_new.dtype),),
        in_specs=[HBM] + [VMEM] * Z,
        out_specs=(VMEM,) * (y_count + 1),
        scratch_shapes=[pltpu.SemaphoreType.DMA],
        compiler_params=params(12),
        name="turn",
    )(pltpu.with_memory_space_constraint(q_new, pltpu.HBM), *routed)
    pages = pages[:1] + [swap(pages[j], "ctx", j) for j in range(1, y_count)]
    pages = [page.reshape(Z * page_rows, 2 * width) for page in pages]

    return pl.pallas_call(
        functools.partial(attend_kernel, y_count),
        out_shape=shape((tokens, q_width), jnp.bfloat16),
        in_specs=[VMEM] * (3 + len(pages) + len(pieces)),
        out_specs=HBM,
        scratch_shapes=[pltpu.VMEM((tokens, q_width), jnp.bfloat16), pltpu.SemaphoreType.DMA((kvh,))],
        compiler_params=params(40 if prompt_kv.shape[0] * ctx_count > 1024 else 24),
        name="attend",
    )(limit, q_new, kv_new, *pages, *pieces)


def solution(mesh):
    placed = (
        P(("dom", "ctx"), None),
        P(("dom", "ctx"), None, None),
        P("ctx", None, None),
        P("dom", "ctx", None, None),
        P(),
        P(),
    )
    return jax.shard_map(
        on_device, mesh=mesh, in_specs=placed, out_specs=P(("dom", "ctx"), None), check_vma=False
    )
```

```python
import functools

import jax
import jax.numpy as jnp
from jax import lax
from jax.experimental import pallas as pl
from jax.experimental.pallas import tpu as pltpu
from jax.sharding import PartitionSpec as P

HD = 128
SPAN = 128
PAGE = 8
RUN = 4
Z = 4
NEGATIVE = -1e30
SCALE2 = HD ** (-0.5) * 1.4426950408889634
VMEM = pl.BlockSpec(memory_space=pltpu.VMEM)
HBM = pl.BlockSpec(memory_space=pltpu.HBM)


def params(mib):
    return pltpu.CompilerParams(vmem_limit_bytes=mib * 2**20)


def pack_kernel(dom_count, anc_hbm, len_hbm, prompt_hbm, cache_hbm, half_ref, *refs):
    out_refs = refs[:dom_count]
    far_ref, limit_ref, anc_ref, len_ref, prompt_ref, cache_ref, sems = refs[dom_count:]
    group = cache_ref.shape[0]
    dom = lax.axis_index("dom")
    _, rows, width = half_ref.shape
    from_row = pl.multiple_of((dom % 2) * rows, rows)
    prompt_in = pltpu.make_async_copy(prompt_hbm.at[pl.ds(from_row, rows)], prompt_ref, sems.at[0])
    anc_in = pltpu.make_async_copy(anc_hbm, anc_ref, sems.at[1])
    len_in = pltpu.make_async_copy(len_hbm, len_ref, sems.at[2])
    cache_in = pltpu.make_async_copy(cache_hbm, cache_ref, sems.at[3])
    prompt_in.start()
    anc_in.start()
    len_in.start()
    cache_in.start()
    runs = group // RUN
    anc_in.wait()
    len_in.wait()
    for run in range(runs):
        far = (anc_ref[dom * group + run * RUN] // group) ^ dom
        far_ref[run] = jnp.full(far_ref.shape[1:], far.astype(jnp.float32)).astype(jnp.bfloat16)
    particle = dom * group + lax.axis_index("ctx")
    limit_ref[...] = jnp.full(limit_ref.shape, len_ref[anc_ref[particle]] * PAGE)
    prompt_in.wait()
    half = prompt_ref[...].reshape(rows, width)
    for to in range(half_ref.shape[0]):
        half_ref[to] = half
    cache_in.wait()
    for k, out_ref in enumerate(out_refs):
        for run in range(runs):
            first = (dom ^ k) * group + run * RUN

            @pl.when(anc_ref[first] // group == dom)
            def _(first=first, out_ref=out_ref):
                for slot in range(RUN):
                    local = anc_ref[first + slot] % group
                    out_ref[slot] = cache_ref[local].reshape(cache_ref.shape[1], width)


def route_kernel(y_count, far_ref, *refs):
    in_refs, out_refs = refs[:-Z], refs[-Z:]
    own_z = lax.axis_index("ctx") // y_count
    width = out_refs[0].shape[2]
    for k, out_ref in enumerate(out_refs):
        for y in range(y_count):
            to = (own_z ^ k) * y_count + y
            far = far_ref[to // RUN]
            picked = in_refs[0][to % RUN]
            for at in range(1, len(in_refs)):
                here = jnp.concatenate([far == at] * (width // far.shape[1]), axis=1)
                picked = jnp.where(here, in_refs[at][to % RUN], picked)
            out_ref[y] = picked


def turn_kernel(q_hbm, *refs):
    in_refs, out_refs, (q_ref, sem) = refs[:Z], refs[Z:-2], refs[-2:]
    q_in = pltpu.make_async_copy(q_hbm, q_ref, sem)
    q_in.start()
    own_y = lax.axis_index("ctx") % len(out_refs)
    for j, out_ref in enumerate(out_refs):
        for k, in_ref in enumerate(in_refs):
            out_ref[k] = in_ref[own_y ^ j]
    q_in.wait()


def head_rows(q_ref, g, gq):
    return jnp.concatenate(
        [q_ref[:, (g * gq + j) * HD : (g * gq + j + 1) * HD] for j in range(gq)], axis=0
    )


def dot_nt(a, b):
    return lax.dot_general(a, b, (((1,), (1,)), ((), ())), preferred_element_type=jnp.float32)


def dot_nn(a, b):
    return lax.dot_general(a, b, (((1,), (0,)), ((), ())), preferred_element_type=jnp.float32)


def attend_kernel(y_count, limit_ref, q_ref, new_ref, *refs):
    pages, pieces, (out_ref, stage, sems) = refs[:y_count], refs[y_count:-3], refs[-3:]
    width = new_ref.shape[2]
    page_rows = pages[0].shape[0] // Z
    gen = page_rows * Z * y_count
    kvh = width // HD
    gq = q_ref.shape[1] // width
    new = new_ref[...].reshape(SPAN, 2 * width)
    old = sum(p.shape[0] for p in pieces)
    ones = jnp.ones((SPAN + old + gen, HD), jnp.bfloat16)
    token = lax.broadcasted_iota(jnp.int32, (SPAN, SPAN), 0)
    causal = lax.broadcasted_iota(jnp.int32, (SPAN, SPAN), 1) <= token
    at = lax.broadcasted_iota(jnp.int32, (SPAN, gen), 1)
    ctx = lax.axis_index("ctx")
    page_z = (at // page_rows % Z) ^ (ctx // y_count)
    page_y = (at // (page_rows * Z)) ^ (ctx % y_count)
    at = (page_z * y_count + page_y) * page_rows + at % page_rows
    visible = at < jnp.broadcast_to(limit_ref[:1], (SPAN, gen))
    copies = []
    for g in range(kvh):
        k_at = slice(g * HD, (g + 1) * HD)
        v_at = slice(width + g * HD, width + (g + 1) * HD)
        keys = jnp.concatenate([new[:, k_at]] + [p[:, k_at] for p in (*pieces, *pages)], axis=0)
        values = jnp.concatenate([new[:, v_at]] + [p[:, v_at] for p in (*pieces, *pages)], axis=0)
        values = jnp.concatenate([values, ones], axis=1)
        scores = dot_nt(head_rows(q_ref, g, gq), keys)
        weights = []
        for j in range(gq):
            s = scores[j * SPAN : (j + 1) * SPAN]
            s_new = jnp.where(causal, s[:, :SPAN], NEGATIVE)
            s_cache = jnp.where(visible, s[:, SPAN + old :], NEGATIVE)
            s = jnp.concatenate([s_new, s[:, SPAN : SPAN + old], s_cache], axis=1)
            top = jnp.max(s, axis=1, keepdims=True)
            weights.append(jnp.exp2((s - top) * SCALE2).astype(jnp.bfloat16))
        out = dot_nn(jnp.concatenate(weights, axis=0), values)
        out = (out[:, :HD] / out[:, HD:]).astype(jnp.bfloat16)
        for j in range(gq):
            stage[:, (g * gq + j) * HD : (g * gq + j + 1) * HD] = out[j * SPAN : (j + 1) * SPAN]
        columns = pl.ds(g * gq * HD, gq * HD)
        copy = pltpu.make_async_copy(stage.at[:, columns], out_ref.at[:, columns], sems.at[g])
        copy.start()
        copies.append(copy)
    for copy in copies:
        copy.wait()


def swap(x, axis, distance):
    return lax.ppermute(x, axis, [(i, i ^ distance) for i in range(lax.axis_size(axis))])


def on_device(q_new, kv_new, prompt_kv, cache_kv, ancestors, lengths):
    dom_count = lax.axis_size("dom")
    ctx_count = lax.axis_size("ctx")
    y_count = ctx_count // Z
    group, page_rows, _, width = cache_kv.shape
    tokens, q_width = q_new.shape
    kvh = width // HD
    half_rows = prompt_kv.shape[0] // 2
    shape = jax.ShapeDtypeStruct
    half, *rest = pl.pallas_call(
        functools.partial(pack_kernel, dom_count),
        out_shape=(
            shape((ctx_count, half_rows, 2 * width), jnp.bfloat16),
            *[shape((RUN, page_rows, 2 * width), jnp.bfloat16)] * dom_count,
            shape((group // RUN, page_rows, HD), jnp.bfloat16),
            shape((8, ctx_count * page_rows), jnp.int32),
        ),
        in_specs=[HBM] * 4,
        out_specs=(VMEM,) * (3 + dom_count),
        scratch_shapes=[
            pltpu.SMEM(ancestors.shape, jnp.int32),
            pltpu.SMEM(lengths.shape, jnp.int32),
            pltpu.VMEM((half_rows, 2, width), jnp.bfloat16),
            pltpu.VMEM(cache_kv.shape, jnp.bfloat16),
            pltpu.SemaphoreType.DMA((4,)),
        ],
        compiler_params=params(12),
        name="pack",
    )(*(pltpu.with_memory_space_constraint(x, pltpu.HBM) for x in (ancestors, lengths, prompt_kv, cache_kv)))
    outgoing, far, limit = rest[:dom_count], rest[dom_count], rest[dom_count + 1]

    own_half = lax.all_to_all(half, "ctx", split_axis=0, concat_axis=0, tiled=True)
    own_half = own_half.reshape(ctx_count * half_rows, 2 * width)

    incoming = outgoing[:1] + [swap(outgoing[k], "dom", k) for k in range(1, dom_count)]
    routed = pl.pallas_call(
        functools.partial(route_kernel, y_count),
        out_shape=(shape((y_count, page_rows, 2 * width), jnp.bfloat16),) * Z,
        in_specs=[VMEM] * (1 + dom_count),
        out_specs=(VMEM,) * Z,
        compiler_params=params(12),
        name="route",
    )(far, *incoming)
    routed = routed[:1] + tuple(swap(routed[k], "ctx", k * y_count) for k in range(1, Z))
    *pages, q_new = pl.pallas_call(
        turn_kernel,
        out_shape=(shape((Z, page_rows, 2 * width), jnp.bfloat16),) * y_count + (shape(q_new.shape, q_new.dtype),),
        in_specs=[HBM] + [VMEM] * Z,
        out_specs=(VMEM,) * (y_count + 1),
        scratch_shapes=[pltpu.SemaphoreType.DMA],
        compiler_params=params(12),
        name="turn",
    )(pltpu.with_memory_space_constraint(q_new, pltpu.HBM), *routed)
    own_half, pages[0] = lax.optimization_barrier((own_half, pages[0]))
    pieces = [own_half, swap(own_half, "dom", 1)]
    pages = pages[:1] + [swap(pages[j], "ctx", j) for j in range(1, y_count)]
    pages = [page.reshape(Z * page_rows, 2 * width) for page in pages]

    return pl.pallas_call(
        functools.partial(attend_kernel, y_count),
        out_shape=shape((tokens, q_width), jnp.bfloat16),
        in_specs=[VMEM] * (3 + len(pages) + len(pieces)),
        out_specs=HBM,
        scratch_shapes=[pltpu.VMEM((tokens, q_width), jnp.bfloat16), pltpu.SemaphoreType.DMA((kvh,))],
        compiler_params=params(40 if prompt_kv.shape[0] * ctx_count > 1024 else 24),
        name="attend",
    )(limit, q_new, kv_new, *pages, *pieces)


def solution(mesh):
    placed = (
        P(("dom", "ctx"), None),
        P(("dom", "ctx"), None, None),
        P("ctx", None, None),
        P("dom", "ctx", None, None),
        P(),
        P(),
    )
    return jax.shard_map(
        on_device, mesh=mesh, in_specs=placed, out_specs=P(("dom", "ctx"), None), check_vma=False
    )
```

```python
import functools

import jax
import jax.numpy as jnp
from jax import lax
from jax.experimental import pallas as pl
from jax.experimental.pallas import tpu as pltpu
from jax.sharding import PartitionSpec as P

HD = 128
SPAN = 128
PAGE = 8
RUN = 4
PARTS = 4
Z = 4
CHUNK = 4
NEGATIVE = -1e30
SCALE2 = HD ** (-0.5) * 1.4426950408889634
VMEM = pl.BlockSpec(memory_space=pltpu.VMEM)
HBM = pl.BlockSpec(memory_space=pltpu.HBM)


def params(mib):
    return pltpu.CompilerParams(vmem_limit_bytes=mib * 2**20)


def pack_kernel(dom_count, anc_hbm, len_hbm, prompt_hbm, cache_hbm, part_ref, *refs):
    out_refs = refs[:dom_count]
    far_ref, limit_ref, anc_ref, len_ref, prompt_ref, cache_ref, sems = refs[dom_count:]
    group = cache_ref.shape[0]
    dom = lax.axis_index("dom")
    _, rows, width = part_ref.shape
    from_row = pl.multiple_of((dom % PARTS) * rows, rows)
    prompt_in = pltpu.make_async_copy(prompt_hbm.at[pl.ds(from_row, rows)], prompt_ref, sems.at[0])
    anc_in = pltpu.make_async_copy(anc_hbm, anc_ref, sems.at[1])
    len_in = pltpu.make_async_copy(len_hbm, len_ref, sems.at[2])
    cache_in = pltpu.make_async_copy(cache_hbm, cache_ref, sems.at[3])
    prompt_in.start()
    anc_in.start()
    len_in.start()
    cache_in.start()
    runs = group // RUN
    anc_in.wait()
    len_in.wait()
    for run in range(runs):
        far = (anc_ref[dom * group + run * RUN] // group) ^ dom
        far_ref[run] = jnp.full(far_ref.shape[1:], far.astype(jnp.float32)).astype(jnp.bfloat16)
    particle = dom * group + lax.axis_index("ctx")
    limit_ref[...] = jnp.full(limit_ref.shape, len_ref[anc_ref[particle]] * PAGE)
    prompt_in.wait()
    part = prompt_ref[...].reshape(rows, width)
    for to in range(part_ref.shape[0]):
        part_ref[to] = part
    cache_in.wait()
    for k, out_ref in enumerate(out_refs):
        for run in range(runs):
            first = (dom ^ k) * group + run * RUN

            @pl.when(anc_ref[first] // group == dom)
            def _(first=first, out_ref=out_ref):
                for slot in range(RUN):
                    local = anc_ref[first + slot] % group
                    out_ref[slot] = cache_ref[local].reshape(cache_ref.shape[1], width)


def route_kernel(y_count, far_ref, *refs):
    in_refs, out_refs = refs[:-Z], refs[-Z:]
    own_z = lax.axis_index("ctx") // y_count
    width = out_refs[0].shape[2]
    for k, out_ref in enumerate(out_refs):
        for y in range(y_count):
            to = (own_z ^ k) * y_count + y
            far = far_ref[to // RUN]
            picked = in_refs[0][to % RUN]
            for at in range(1, len(in_refs)):
                here = jnp.concatenate([far == at] * (width // far.shape[1]), axis=1)
                picked = jnp.where(here, in_refs[at][to % RUN], picked)
            out_ref[y] = picked


def turn_kernel(q_hbm, *refs):
    in_refs, out_refs, (q_ref, sem) = refs[:Z], refs[Z:-2], refs[-2:]
    q_in = pltpu.make_async_copy(q_hbm, q_ref, sem)
    q_in.start()
    own_y = lax.axis_index("ctx") % len(out_refs)
    for j, out_ref in enumerate(out_refs):
        for k, in_ref in enumerate(in_refs):
            out_ref[k] = in_ref[own_y ^ j]
    q_in.wait()


def head_rows(q_ref, g, gq):
    return jnp.concatenate(
        [q_ref[:, (g * gq + j) * HD : (g * gq + j + 1) * HD] for j in range(gq)], axis=0
    )


def dot_nt(a, b):
    return lax.dot_general(a, b, (((1,), (1,)), ((), ())), preferred_element_type=jnp.float32)


def dot_nn(a, b):
    return lax.dot_general(a, b, (((1,), (0,)), ((), ())), preferred_element_type=jnp.float32)


def attend_kernel(y_count, limit_ref, q_ref, new_ref, *refs):
    pages, pieces, (out_ref, stage, sems) = refs[:y_count], refs[y_count:-3], refs[-3:]
    width = new_ref.shape[2]
    page_rows = pages[0].shape[0] // Z
    gen = page_rows * Z * y_count
    kvh = width // HD
    gq = q_ref.shape[1] // width
    new = new_ref[...].reshape(SPAN, 2 * width)
    old = sum(p.shape[0] for p in pieces)
    ones = jnp.ones((SPAN + old + gen, HD), jnp.bfloat16)
    token = lax.broadcasted_iota(jnp.int32, (SPAN, SPAN), 0)
    causal = lax.broadcasted_iota(jnp.int32, (SPAN, SPAN), 1) <= token
    at = lax.broadcasted_iota(jnp.int32, (SPAN, gen), 1)
    ctx = lax.axis_index("ctx")
    page_z = (at // page_rows % Z) ^ (ctx // y_count)
    page_y = (at // (page_rows * Z)) ^ (ctx % y_count)
    at = (page_z * y_count + page_y) * page_rows + at % page_rows
    visible = at < jnp.broadcast_to(limit_ref[:1], (SPAN, gen))
    keys, values = [], []
    for g in range(kvh):
        k_at = slice(g * HD, (g + 1) * HD)
        v_at = slice(width + g * HD, width + (g + 1) * HD)
        keys.append(jnp.concatenate([new[:, k_at]] + [p[:, k_at] for p in (*pieces, *pages)], axis=0))
        value = jnp.concatenate([new[:, v_at]] + [p[:, v_at] for p in (*pieces, *pages)], axis=0)
        values.append(jnp.concatenate([value, ones], axis=1))
    chunk = CHUNK * HD
    per_group = gq // CHUNK
    count = q_ref.shape[1] // chunk

    def scores_of(c):
        return dot_nt(head_rows(q_ref, c, CHUNK), keys[c // per_group])

    copies = []
    ahead = scores_of(0)
    for c in range(count):
        scores = ahead
        if c + 1 < count:
            ahead = scores_of(c + 1)
        weights = []
        for j in range(CHUNK):
            s = scores[j * SPAN : (j + 1) * SPAN]
            s_new = jnp.where(causal, s[:, :SPAN], NEGATIVE)
            s_cache = jnp.where(visible, s[:, SPAN + old :], NEGATIVE)
            s = jnp.concatenate([s_new, s[:, SPAN : SPAN + old], s_cache], axis=1)
            top = jnp.max(s, axis=1, keepdims=True)
            weights.append(jnp.exp2((s - top) * SCALE2).astype(jnp.bfloat16))
        out = dot_nn(jnp.concatenate(weights, axis=0), values[c // per_group])
        out = (out[:, :HD] / out[:, HD:]).astype(jnp.bfloat16)
        for j in range(CHUNK):
            stage[:, (c * CHUNK + j) * HD : (c * CHUNK + j + 1) * HD] = out[j * SPAN : (j + 1) * SPAN]
        columns = pl.ds(c * chunk, chunk)
        copy = pltpu.make_async_copy(stage.at[:, columns], out_ref.at[:, columns], sems.at[c])
        copy.start()
        copies.append(copy)
    for copy in copies:
        copy.wait()


def swap(x, axis, distance):
    return lax.ppermute(x, axis, [(i, i ^ distance) for i in range(lax.axis_size(axis))])


def on_device(q_new, kv_new, prompt_kv, cache_kv, ancestors, lengths):
    dom_count = lax.axis_size("dom")
    ctx_count = lax.axis_size("ctx")
    y_count = ctx_count // Z
    group, page_rows, _, width = cache_kv.shape
    tokens, q_width = q_new.shape
    kvh = width // HD
    part_rows = prompt_kv.shape[0] // PARTS
    shape = jax.ShapeDtypeStruct
    parts, *rest = pl.pallas_call(
        functools.partial(pack_kernel, dom_count),
        out_shape=(
            shape((ctx_count, part_rows, 2 * width), jnp.bfloat16),
            *[shape((RUN, page_rows, 2 * width), jnp.bfloat16)] * dom_count,
            shape((group // RUN, page_rows, HD), jnp.bfloat16),
            shape((8, ctx_count * page_rows), jnp.int32),
        ),
        in_specs=[HBM] * 4,
        out_specs=(VMEM,) * (3 + dom_count),
        scratch_shapes=[
            pltpu.SMEM(ancestors.shape, jnp.int32),
            pltpu.SMEM(lengths.shape, jnp.int32),
            pltpu.VMEM((part_rows, 2, width), jnp.bfloat16),
            pltpu.VMEM(cache_kv.shape, jnp.bfloat16),
            pltpu.SemaphoreType.DMA((4,)),
        ],
        compiler_params=params(12),
        name="pack",
    )(*(pltpu.with_memory_space_constraint(x, pltpu.HBM) for x in (ancestors, lengths, prompt_kv, cache_kv)))
    outgoing, far, limit = rest[:dom_count], rest[dom_count], rest[dom_count + 1]

    own_part = lax.all_to_all(parts, "ctx", split_axis=0, concat_axis=0, tiled=True)
    own_part = own_part.reshape(ctx_count * part_rows, 2 * width)

    incoming = outgoing[:1] + [swap(outgoing[k], "dom", k) for k in range(1, dom_count)]
    routed = pl.pallas_call(
        functools.partial(route_kernel, y_count),
        out_shape=(shape((y_count, page_rows, 2 * width), jnp.bfloat16),) * Z,
        in_specs=[VMEM] * (1 + dom_count),
        out_specs=(VMEM,) * Z,
        compiler_params=params(12),
        name="route",
    )(far, *incoming)
    own_part, own_route = lax.optimization_barrier((own_part, routed[0]))
    routed = (own_route,) + tuple(routed[1:])
    pieces = [own_part, swap(own_part, "dom", 2)]
    routed = routed[:1] + tuple(swap(routed[k], "ctx", k * y_count) for k in range(1, Z))
    *pages, q_new = pl.pallas_call(
        turn_kernel,
        out_shape=(shape((Z, page_rows, 2 * width), jnp.bfloat16),) * y_count + (shape(q_new.shape, q_new.dtype),),
        in_specs=[HBM] + [VMEM] * Z,
        out_specs=(VMEM,) * (y_count + 1),
        scratch_shapes=[pltpu.SemaphoreType.DMA],
        compiler_params=params(12),
        name="turn",
    )(pltpu.with_memory_space_constraint(q_new, pltpu.HBM), *routed)
    pieces[1], pages[0] = lax.optimization_barrier((pieces[1], pages[0]))
    pieces += [swap(piece, "dom", 1) for piece in pieces]
    pages = pages[:1] + [swap(pages[j], "ctx", j) for j in range(1, y_count)]
    pages = [page.reshape(Z * page_rows, 2 * width) for page in pages]

    return pl.pallas_call(
        functools.partial(attend_kernel, y_count),
        out_shape=shape((tokens, q_width), jnp.bfloat16),
        in_specs=[VMEM] * (3 + len(pages) + len(pieces)),
        out_specs=HBM,
        scratch_shapes=[pltpu.VMEM((tokens, q_width), jnp.bfloat16), pltpu.SemaphoreType.DMA((q_width // (CHUNK * HD),))],
        compiler_params=params(40 if prompt_kv.shape[0] * ctx_count > 1024 else 24),
        name="attend",
    )(limit, q_new, kv_new, *pages, *pieces)


def solution(mesh):
    placed = (
        P(("dom", "ctx"), None),
        P(("dom", "ctx"), None, None),
        P("ctx", None, None),
        P("dom", "ctx", None, None),
        P(),
        P(),
    )
    return jax.shard_map(
        on_device, mesh=mesh, in_specs=placed, out_specs=P(("dom", "ctx"), None), check_vma=False
    )
```

```python
import functools

import jax
import jax.numpy as jnp
from jax import lax
from jax.experimental import pallas as pl
from jax.experimental.pallas import tpu as pltpu
from jax.sharding import PartitionSpec as P

HD = 128
SPAN = 128
PAGE = 8
RUN = 4
Z = 4
CHUNK = 4
NEGATIVE = -1e30
SCALE2 = HD ** (-0.5) * 1.4426950408889634
VMEM = pl.BlockSpec(memory_space=pltpu.VMEM)
HBM = pl.BlockSpec(memory_space=pltpu.HBM)


def params(mib):
    return pltpu.CompilerParams(vmem_limit_bytes=mib * 2**20)


def pack_kernel(dom_count, anc_hbm, len_hbm, prompt_hbm, cache_hbm, half_ref, *refs):
    out_refs = refs[:dom_count]
    far_ref, limit_ref, anc_ref, len_ref, prompt_ref, cache_ref, sems = refs[dom_count:]
    group = cache_ref.shape[0]
    dom = lax.axis_index("dom")
    rows, width = half_ref.shape
    from_row = pl.multiple_of((dom % 2) * rows, rows)
    prompt_in = pltpu.make_async_copy(prompt_hbm.at[pl.ds(from_row, rows)], prompt_ref, sems.at[0])
    anc_in = pltpu.make_async_copy(anc_hbm, anc_ref, sems.at[1])
    len_in = pltpu.make_async_copy(len_hbm, len_ref, sems.at[2])
    cache_in = pltpu.make_async_copy(cache_hbm, cache_ref, sems.at[3])
    prompt_in.start()
    anc_in.start()
    len_in.start()
    cache_in.start()
    runs = group // RUN
    anc_in.wait()
    len_in.wait()
    for run in range(runs):
        far = (anc_ref[dom * group + run * RUN] // group) ^ dom
        far_ref[run] = jnp.full(far_ref.shape[1:], far.astype(jnp.float32)).astype(jnp.bfloat16)
    particle = dom * group + lax.axis_index("ctx")
    limit_ref[...] = jnp.full(limit_ref.shape, len_ref[anc_ref[particle]] * PAGE)
    prompt_in.wait()
    half_ref[...] = prompt_ref[...].reshape(rows, width)
    cache_in.wait()
    for k, out_ref in enumerate(out_refs):
        for run in range(runs):
            first = (dom ^ k) * group + run * RUN

            @pl.when(anc_ref[first] // group == dom)
            def _(first=first, out_ref=out_ref):
                for slot in range(RUN):
                    local = anc_ref[first + slot] % group
                    out_ref[slot] = cache_ref[local].reshape(cache_ref.shape[1], width)


def route_kernel(dom_count, far_ref, *refs):
    in_refs, (out_hbm, out_ref, sem) = refs[:dom_count], refs[-3:]
    width = out_ref.shape[2]
    for run in range(far_ref.shape[0]):
        far = far_ref[run]
        for slot in range(RUN):
            picked = in_refs[0][slot]
            for k in range(1, len(in_refs)):
                here = jnp.concatenate([far == k] * (width // far.shape[1]), axis=1)
                picked = jnp.where(here, in_refs[k][slot], picked)
            out_ref[run * RUN + slot] = picked
    out = pltpu.make_async_copy(out_ref, out_hbm, sem)
    out.start()
    out.wait()


def head_rows(q_ref, g, gq):
    return jnp.concatenate(
        [q_ref[:, (g * gq + j) * HD : (g * gq + j + 1) * HD] for j in range(gq)], axis=0
    )


def dot_nt(a, b):
    return lax.dot_general(a, b, (((1,), (1,)), ((), ())), preferred_element_type=jnp.float32)


def dot_nn(a, b):
    return lax.dot_general(a, b, (((1,), (0,)), ((), ())), preferred_element_type=jnp.float32)


def attend_kernel(limit_ref, q_hbm, new_ref, cache_ref, *refs):
    pieces, (out_ref, q_ref, stage, sems) = refs[:-4], refs[-4:]
    chunk = CHUNK * HD
    count = q_ref.shape[1] // chunk
    q_copies = []
    for c in range(count):
        columns = pl.ds(c * chunk, chunk)
        q_copies.append(pltpu.make_async_copy(q_hbm.at[:, columns], q_ref.at[:, columns], sems.at[count + c]))
        q_copies[c].start()
    width = new_ref.shape[2]
    gen = cache_ref.shape[0]
    kvh = width // HD
    gq = q_ref.shape[1] // width
    new = new_ref[...].reshape(SPAN, 2 * width)
    old = sum(p.shape[0] for p in pieces)
    ones = jnp.ones((SPAN + old + gen, HD), jnp.bfloat16)
    token = lax.broadcasted_iota(jnp.int32, (SPAN, SPAN), 0)
    causal = lax.broadcasted_iota(jnp.int32, (SPAN, SPAN), 1) <= token
    visible = lax.broadcasted_iota(jnp.int32, (SPAN, gen), 1) < jnp.broadcast_to(limit_ref[:1], (SPAN, gen))
    keys, values = [], []
    for g in range(kvh):
        k_at = slice(g * HD, (g + 1) * HD)
        v_at = slice(width + g * HD, width + (g + 1) * HD)
        keys.append(jnp.concatenate([new[:, k_at]] + [p[:, k_at] for p in (*pieces, cache_ref)], axis=0))
        value = jnp.concatenate([new[:, v_at]] + [p[:, v_at] for p in (*pieces, cache_ref)], axis=0)
        values.append(jnp.concatenate([value, ones], axis=1))
    per_group = gq // CHUNK

    def scores_of(c):
        q_copies[c].wait()
        return dot_nt(head_rows(q_ref, c, CHUNK), keys[c // per_group])

    copies = []
    ahead = scores_of(0)
    for c in range(count):
        scores = ahead
        if c + 1 < count:
            ahead = scores_of(c + 1)
        weights = []
        for j in range(CHUNK):
            s = scores[j * SPAN : (j + 1) * SPAN]
            s_new = jnp.where(causal, s[:, :SPAN], NEGATIVE)
            s_cache = jnp.where(visible, s[:, SPAN + old :], NEGATIVE)
            s = jnp.concatenate([s_new, s[:, SPAN : SPAN + old], s_cache], axis=1)
            top = jnp.max(s, axis=1, keepdims=True)
            weights.append(jnp.exp2((s - top) * SCALE2).astype(jnp.bfloat16))
        out = dot_nn(jnp.concatenate(weights, axis=0), values[c // per_group])
        out = (out[:, :HD] / out[:, HD:]).astype(jnp.bfloat16)
        for j in range(CHUNK):
            stage[:, (c * CHUNK + j) * HD : (c * CHUNK + j + 1) * HD] = out[j * SPAN : (j + 1) * SPAN]
        columns = pl.ds(c * chunk, chunk)
        copy = pltpu.make_async_copy(stage.at[:, columns], out_ref.at[:, columns], sems.at[c])
        copy.start()
        copies.append(copy)
    for copy in copies:
        copy.wait()


def swap(x, axis, distance):
    return lax.ppermute(x, axis, [(i, i ^ distance) for i in range(lax.axis_size(axis))])


def on_device(q_new, kv_new, prompt_kv, cache_kv, ancestors, lengths):
    dom_count = lax.axis_size("dom")
    ctx_count = lax.axis_size("ctx")
    y_count = ctx_count // Z
    group, page_rows, _, width = cache_kv.shape
    tokens, q_width = q_new.shape
    half_rows = prompt_kv.shape[0] // 2
    shape = jax.ShapeDtypeStruct
    half, *rest = pl.pallas_call(
        functools.partial(pack_kernel, dom_count),
        out_shape=(
            shape((half_rows, 2 * width), jnp.bfloat16),
            *[shape((RUN, page_rows, 2 * width), jnp.bfloat16)] * dom_count,
            shape((group // RUN, page_rows, HD), jnp.bfloat16),
            shape((8, ctx_count * page_rows), jnp.int32),
        ),
        in_specs=[HBM] * 4,
        out_specs=(VMEM,) * (3 + dom_count),
        scratch_shapes=[
            pltpu.SMEM(ancestors.shape, jnp.int32),
            pltpu.SMEM(lengths.shape, jnp.int32),
            pltpu.VMEM((half_rows, 2, width), jnp.bfloat16),
            pltpu.VMEM(cache_kv.shape, jnp.bfloat16),
            pltpu.SemaphoreType.DMA((4,)),
        ],
        compiler_params=params(12),
        name="pack",
    )(*(pltpu.with_memory_space_constraint(x, pltpu.HBM) for x in (ancestors, lengths, prompt_kv, cache_kv)))
    outgoing, far, limit = rest[:dom_count], rest[dom_count], rest[dom_count + 1]

    pieces = [half] + [swap(half, "ctx", k * y_count) for k in range(1, Z)]
    pieces += [swap(p, "ctx", k) for k in range(1, y_count) for p in pieces[:Z]]
    underway = pieces[1 : Z + 2]
    pieces += [swap(p, "dom", 1) for p in pieces]

    incoming = outgoing[:1] + [swap(outgoing[k], "dom", k) for k in range(1, dom_count)]
    routed = pl.pallas_call(
        functools.partial(route_kernel, dom_count),
        out_shape=pltpu.HBM((group, page_rows, 2 * width), jnp.bfloat16),
        in_specs=[VMEM] * (1 + dom_count) + [pl.BlockSpec(memory_space=pl.ANY)] * len(underway),
        out_specs=HBM,
        scratch_shapes=[pltpu.VMEM((group, page_rows, 2 * width), jnp.bfloat16), pltpu.SemaphoreType.DMA],
        compiler_params=params(12),
        name="route",
    )(far, *incoming, *underway)
    pages = lax.all_to_all(routed, "ctx", split_axis=0, concat_axis=0, tiled=True)
    pages = pages.reshape(ctx_count * page_rows, 2 * width)

    return pl.pallas_call(
        attend_kernel,
        out_shape=shape((tokens, q_width), jnp.bfloat16),
        in_specs=[VMEM, HBM] + [VMEM] * (2 + len(pieces)),
        out_specs=HBM,
        scratch_shapes=[
            pltpu.VMEM((tokens, q_width), jnp.bfloat16),
            pltpu.VMEM((tokens, q_width), jnp.bfloat16),
            pltpu.SemaphoreType.DMA((2 * q_width // (CHUNK * HD),)),
        ],
        compiler_params=params(40 if prompt_kv.shape[0] * ctx_count > 1024 else 24),
        name="attend",
    )(limit, pltpu.with_memory_space_constraint(q_new, pltpu.HBM), kv_new, pages, *pieces)


def solution(mesh):
    placed = (
        P(("dom", "ctx"), None),
        P(("dom", "ctx"), None, None),
        P("ctx", None, None),
        P("dom", "ctx", None, None),
        P(),
        P(),
    )
    return jax.shard_map(
        on_device, mesh=mesh, in_specs=placed, out_specs=P(("dom", "ctx"), None), check_vma=False
    )
```

```python
import functools

import jax
import jax.numpy as jnp
from jax import lax
from jax.experimental import pallas as pl
from jax.experimental.pallas import tpu as pltpu
from jax.sharding import PartitionSpec as P

HD = 128
SPAN = 128
PAGE = 8
RUN = 4
Z = 4
CHUNK = 4
Q_COPIES = 4
NEGATIVE = -1e30
SCALE2 = HD ** (-0.5) * 1.4426950408889634
VMEM = pl.BlockSpec(memory_space=pltpu.VMEM)
HBM = pl.BlockSpec(memory_space=pltpu.HBM)


def params(mib):
    return pltpu.CompilerParams(vmem_limit_bytes=mib * 2**20)


def pack_kernel(dom_count, anc_hbm, len_hbm, prompt_hbm, cache_hbm, q_hbm, half_ref, *refs):
    out_refs = refs[:dom_count]
    far_ref, limit_ref, q_ref, anc_ref, len_ref, prompt_ref, cache_ref, sems = refs[dom_count:]
    group = cache_ref.shape[0]
    dom = lax.axis_index("dom")
    rows, width = half_ref.shape
    from_row = pl.multiple_of((dom % 2) * rows, rows)
    prompt_in = pltpu.make_async_copy(prompt_hbm.at[pl.ds(from_row, rows)], prompt_ref, sems.at[0])
    anc_in = pltpu.make_async_copy(anc_hbm, anc_ref, sems.at[1])
    len_in = pltpu.make_async_copy(len_hbm, len_ref, sems.at[2])
    cache_in = pltpu.make_async_copy(cache_hbm, cache_ref, sems.at[3])
    prompt_in.start()
    anc_in.start()
    len_in.start()
    cache_in.start()
    q_rows = q_ref.shape[0] // Q_COPIES
    q_in = []
    for at in range(Q_COPIES):
        rows_at = pl.ds(at * q_rows, q_rows)
        q_in.append(pltpu.make_async_copy(q_hbm.at[rows_at], q_ref.at[rows_at], sems.at[4 + at]))
        q_in[at].start()
    runs = group // RUN
    anc_in.wait()
    len_in.wait()
    for run in range(runs):
        far = (anc_ref[dom * group + run * RUN] // group) ^ dom
        far_ref[run] = jnp.full(far_ref.shape[1:], far.astype(jnp.float32)).astype(jnp.bfloat16)
    particle = dom * group + lax.axis_index("ctx")
    limit_ref[...] = jnp.full(limit_ref.shape, len_ref[anc_ref[particle]] * PAGE)
    prompt_in.wait()
    half_ref[...] = prompt_ref[...].reshape(rows, width)
    cache_in.wait()
    for k, out_ref in enumerate(out_refs):
        for run in range(runs):
            first = (dom ^ k) * group + run * RUN

            @pl.when(anc_ref[first] // group == dom)
            def _(first=first, out_ref=out_ref):
                for slot in range(RUN):
                    local = anc_ref[first + slot] % group
                    out_ref[slot] = cache_ref[local].reshape(cache_ref.shape[1], width)

    for copy in q_in:
        copy.wait()


def route_kernel(dom_count, far_ref, *refs):
    in_refs, out_refs = refs[:dom_count], refs[dom_count:]
    ctx = lax.axis_index("ctx")
    width = out_refs[0].shape[1]
    for k, out_ref in enumerate(out_refs):
        to = ctx ^ k
        far = far_ref[to // RUN]
        picked = in_refs[0][to % RUN]
        for at in range(1, dom_count):
            here = jnp.concatenate([far == at] * (width // far.shape[1]), axis=1)
            picked = jnp.where(here, in_refs[at][to % RUN], picked)
        out_ref[...] = picked


def head_rows(q_ref, g, gq):
    return jnp.concatenate(
        [q_ref[:, (g * gq + j) * HD : (g * gq + j + 1) * HD] for j in range(gq)], axis=0
    )


def dot_nt(a, b):
    return lax.dot_general(a, b, (((1,), (1,)), ((), ())), preferred_element_type=jnp.float32)


def dot_nn(a, b):
    return lax.dot_general(a, b, (((1,), (0,)), ((), ())), preferred_element_type=jnp.float32)


def gather_kernel(new_ref, *refs):
    pieces, (key_ref, value_ref) = refs[:-2], refs[-2:]
    width = new_ref.shape[2]
    new = new_ref[...].reshape(SPAN, 2 * width)
    at = 0
    for piece in (new, *pieces):
        rows = slice(at, at + piece.shape[0])
        at += piece.shape[0]
        key_ref[rows, :] = piece[:, :width]
        for g in range(width // HD):
            value_ref[rows, 2 * g * HD : (2 * g + 1) * HD] = piece[:, width + g * HD : width + (g + 1) * HD]
            value_ref[rows, (2 * g + 1) * HD : (2 * g + 2) * HD] = jnp.ones((piece.shape[0], HD), jnp.bfloat16)


def attend_kernel(limit_ref, q_ref, key_ref, value_ref, *refs):
    pages, (out_ref, stage, sems) = refs[:-3], refs[-3:]
    width = key_ref.shape[1]
    page_rows = pages[0].shape[0]
    gen = page_rows * len(pages)
    kvh = width // HD
    gq = q_ref.shape[1] // width
    old = key_ref.shape[0] - SPAN
    token = lax.broadcasted_iota(jnp.int32, (SPAN, SPAN), 0)
    causal = lax.broadcasted_iota(jnp.int32, (SPAN, SPAN), 1) <= token
    at = lax.broadcasted_iota(jnp.int32, (SPAN, gen), 1)
    at = ((at // page_rows) ^ lax.axis_index("ctx")) * page_rows + at % page_rows
    visible = at < jnp.broadcast_to(limit_ref[:1], (SPAN, gen))
    pages = jnp.concatenate([page[...] for page in pages], axis=0)
    ones = jnp.ones((gen, HD), jnp.bfloat16)
    keys, values = [], []
    for g in range(kvh):
        keys.append(jnp.concatenate([key_ref[:, g * HD : (g + 1) * HD], pages[:, g * HD : (g + 1) * HD]], axis=0))
        value = jnp.concatenate([pages[:, width + g * HD : width + (g + 1) * HD], ones], axis=1)
        values.append(jnp.concatenate([value_ref[:, 2 * g * HD : (2 * g + 2) * HD], value], axis=0))
    chunk = CHUNK * HD
    per_group = gq // CHUNK
    count = q_ref.shape[1] // chunk

    def scores_of(c):
        return dot_nt(head_rows(q_ref, c, CHUNK), keys[c // per_group])

    copies = []
    ahead = scores_of(0)
    for c in range(count):
        scores = ahead
        if c + 1 < count:
            ahead = scores_of(c + 1)
        weights = []
        for j in range(CHUNK):
            s = scores[j * SPAN : (j + 1) * SPAN]
            s_new = jnp.where(causal, s[:, :SPAN], NEGATIVE)
            s_cache = jnp.where(visible, s[:, SPAN + old :], NEGATIVE)
            s = jnp.concatenate([s_new, s[:, SPAN : SPAN + old], s_cache], axis=1)
            top = jnp.max(s, axis=1, keepdims=True)
            weights.append(jnp.exp2((s - top) * SCALE2).astype(jnp.bfloat16))
        out = dot_nn(jnp.concatenate(weights, axis=0), values[c // per_group])
        out = (out[:, :HD] / out[:, HD:]).astype(jnp.bfloat16)
        for j in range(CHUNK):
            stage[:, (c * CHUNK + j) * HD : (c * CHUNK + j + 1) * HD] = out[j * SPAN : (j + 1) * SPAN]
        columns = pl.ds(c * chunk, chunk)
        copy = pltpu.make_async_copy(stage.at[:, columns], out_ref.at[:, columns], sems.at[c])
        copy.start()
        copies.append(copy)
    for copy in copies:
        copy.wait()


def swap(x, axis, distance):
    return lax.ppermute(x, axis, [(i, i ^ distance) for i in range(lax.axis_size(axis))])


def on_device(q_new, kv_new, prompt_kv, cache_kv, ancestors, lengths):
    dom_count = lax.axis_size("dom")
    ctx_count = lax.axis_size("ctx")
    y_count = ctx_count // Z
    group, page_rows, _, width = cache_kv.shape
    tokens, q_width = q_new.shape
    half_rows = prompt_kv.shape[0] // 2
    shape = jax.ShapeDtypeStruct
    half, *rest = pl.pallas_call(
        functools.partial(pack_kernel, dom_count),
        out_shape=(
            shape((half_rows, 2 * width), jnp.bfloat16),
            *[shape((RUN, page_rows, 2 * width), jnp.bfloat16)] * dom_count,
            shape((group // RUN, page_rows, HD), jnp.bfloat16),
            shape((8, ctx_count * page_rows), jnp.int32),
            shape(q_new.shape, q_new.dtype),
        ),
        in_specs=[HBM] * 5,
        out_specs=(VMEM,) * (4 + dom_count),
        scratch_shapes=[
            pltpu.SMEM(ancestors.shape, jnp.int32),
            pltpu.SMEM(lengths.shape, jnp.int32),
            pltpu.VMEM((half_rows, 2, width), jnp.bfloat16),
            pltpu.VMEM(cache_kv.shape, jnp.bfloat16),
            pltpu.SemaphoreType.DMA((4 + Q_COPIES,)),
        ],
        compiler_params=params(12),
        name="pack",
    )(*(pltpu.with_memory_space_constraint(x, pltpu.HBM) for x in (ancestors, lengths, prompt_kv, cache_kv, q_new)))
    outgoing, (far, limit, queries) = rest[:dom_count], rest[dom_count:]

    pieces = [half] + [swap(half, "ctx", k * y_count) for k in range(1, Z)]
    pieces += [swap(p, "ctx", k) for k in range(1, y_count) for p in pieces[:Z]]
    pieces += [swap(p, "dom", 1) for p in pieces]

    incoming = outgoing[:1] + [swap(outgoing[k], "dom", k) for k in range(1, dom_count)]
    routed = pl.pallas_call(
        functools.partial(route_kernel, dom_count),
        out_shape=(shape((page_rows, 2 * width), jnp.bfloat16),) * ctx_count,
        in_specs=[VMEM] * (1 + dom_count),
        out_specs=(VMEM,) * ctx_count,
        compiler_params=params(12),
        name="route",
    )(far, *incoming)
    pages = [routed[0]] + [swap(routed[k], "ctx", k) for k in range(1, ctx_count)]

    key_count = SPAN + sum(piece.shape[0] for piece in pieces)
    keys, values = pl.pallas_call(
        gather_kernel,
        out_shape=(shape((key_count, width), jnp.bfloat16), shape((key_count, 2 * width), jnp.bfloat16)),
        in_specs=[VMEM] * (1 + len(pieces)),
        out_specs=(VMEM, VMEM),
        compiler_params=params(16),
        cost_estimate=pl.CostEstimate(flops=10**10, bytes_accessed=2**22, transcendentals=0),
        name="gather",
    )(kv_new, *pieces)
    return pl.pallas_call(
        attend_kernel,
        out_shape=shape((tokens, q_width), jnp.bfloat16),
        in_specs=[VMEM] * (4 + len(pages)),
        out_specs=HBM,
        scratch_shapes=[pltpu.VMEM((tokens, q_width), jnp.bfloat16), pltpu.SemaphoreType.DMA((q_width // (CHUNK * HD),))],
        compiler_params=params(40 if prompt_kv.shape[0] * ctx_count > 1024 else 24),
        name="attend",
    )(limit, queries, keys, values, *pages)


def solution(mesh):
    placed = (
        P(("dom", "ctx"), None),
        P(("dom", "ctx"), None, None),
        P("ctx", None, None),
        P("dom", "ctx", None, None),
        P(),
        P(),
    )
    return jax.shard_map(
        on_device, mesh=mesh, in_specs=placed, out_specs=P(("dom", "ctx"), None), check_vma=False
    )
```

```python
import functools

import jax
import jax.numpy as jnp
from jax import lax
from jax.experimental import pallas as pl
from jax.experimental.pallas import tpu as pltpu
from jax.sharding import PartitionSpec as P

HD = 128
SPAN = 128
PAGE = 8
RUN = 4
Z = 4
CHUNK = 4
Q_COPIES = 4
NEGATIVE = -1e30
SCALE2 = HD ** (-0.5) * 1.4426950408889634
VMEM = pl.BlockSpec(memory_space=pltpu.VMEM)
HBM = pl.BlockSpec(memory_space=pltpu.HBM)


def params(mib):
    return pltpu.CompilerParams(vmem_limit_bytes=mib * 2**20)


def pack_kernel(dom_count, anc_hbm, len_hbm, prompt_hbm, cache_hbm, q_hbm, half_ref, *refs):
    out_refs = refs[:dom_count]
    far_ref, limit_ref, q_ref, anc_ref, len_ref, prompt_ref, cache_ref, sems = refs[dom_count:]
    group = cache_ref.shape[0]
    dom = lax.axis_index("dom")
    rows, width = half_ref.shape
    from_row = pl.multiple_of((dom % 2) * rows, rows)
    prompt_in = pltpu.make_async_copy(prompt_hbm.at[pl.ds(from_row, rows)], prompt_ref, sems.at[0])
    anc_in = pltpu.make_async_copy(anc_hbm, anc_ref, sems.at[1])
    len_in = pltpu.make_async_copy(len_hbm, len_ref, sems.at[2])
    cache_in = pltpu.make_async_copy(cache_hbm, cache_ref, sems.at[3])
    prompt_in.start()
    anc_in.start()
    len_in.start()
    cache_in.start()
    q_rows = q_ref.shape[0] // Q_COPIES
    q_in = []
    for at in range(Q_COPIES):
        rows_at = pl.ds(at * q_rows, q_rows)
        q_in.append(pltpu.make_async_copy(q_hbm.at[rows_at], q_ref.at[rows_at], sems.at[4 + at]))
        q_in[at].start()
    runs = group // RUN
    anc_in.wait()
    len_in.wait()
    for run in range(runs):
        far = (anc_ref[dom * group + run * RUN] // group) ^ dom
        far_ref[run] = jnp.full(far_ref.shape[1:], far.astype(jnp.float32)).astype(jnp.bfloat16)
    particle = dom * group + lax.axis_index("ctx")
    limit_ref[...] = jnp.full(limit_ref.shape, len_ref[anc_ref[particle]] * PAGE)
    prompt_in.wait()
    half_ref[...] = prompt_ref[...].reshape(rows, width)
    cache_in.wait()
    for k, out_ref in enumerate(out_refs):
        for run in range(runs):
            first = (dom ^ k) * group + run * RUN

            @pl.when(anc_ref[first] // group == dom)
            def _(first=first, out_ref=out_ref):
                for slot in range(RUN):
                    local = anc_ref[first + slot] % group
                    out_ref[slot] = cache_ref[local].reshape(cache_ref.shape[1], width)

    for copy in q_in:
        copy.wait()


def route_kernel(far_ref, *refs):
    *in_refs, out_hbm, out_ref, sem = refs
    width = out_ref.shape[2]
    for run in range(far_ref.shape[0]):
        far = far_ref[run]
        for slot in range(RUN):
            picked = in_refs[0][slot]
            for k in range(1, len(in_refs)):
                here = jnp.concatenate([far == k] * (width // far.shape[1]), axis=1)
                picked = jnp.where(here, in_refs[k][slot], picked)
            out_ref[run * RUN + slot] = picked
    out = pltpu.make_async_copy(out_ref, out_hbm, sem)
    out.start()
    out.wait()


def head_rows(q_ref, g, gq):
    return jnp.concatenate(
        [q_ref[:, (g * gq + j) * HD : (g * gq + j + 1) * HD] for j in range(gq)], axis=0
    )


def dot_nt(a, b):
    return lax.dot_general(a, b, (((1,), (1,)), ((), ())), preferred_element_type=jnp.float32)


def dot_nn(a, b):
    return lax.dot_general(a, b, (((1,), (0,)), ((), ())), preferred_element_type=jnp.float32)


def gather_kernel(new_ref, *refs):
    pieces, (key_ref, value_ref) = refs[:-2], refs[-2:]
    width = new_ref.shape[2]
    new = new_ref[...].reshape(SPAN, 2 * width)
    at = 0
    for piece in (new, *pieces):
        rows = slice(at, at + piece.shape[0])
        at += piece.shape[0]
        key_ref[rows, :] = piece[:, :width]
        for g in range(width // HD):
            value_ref[rows, 2 * g * HD : (2 * g + 1) * HD] = piece[:, width + g * HD : width + (g + 1) * HD]
            value_ref[rows, (2 * g + 1) * HD : (2 * g + 2) * HD] = jnp.ones((piece.shape[0], HD), jnp.bfloat16)


def attend_kernel(limit_ref, q_ref, key_ref, value_ref, cache_ref, out_ref, stage, sems):
    width = key_ref.shape[1]
    gen = cache_ref.shape[0]
    kvh = width // HD
    gq = q_ref.shape[1] // width
    old = key_ref.shape[0] - SPAN
    token = lax.broadcasted_iota(jnp.int32, (SPAN, SPAN), 0)
    causal = lax.broadcasted_iota(jnp.int32, (SPAN, SPAN), 1) <= token
    visible = lax.broadcasted_iota(jnp.int32, (SPAN, gen), 1) < jnp.broadcast_to(limit_ref[:1], (SPAN, gen))
    ones = jnp.ones((gen, HD), jnp.bfloat16)
    keys, values = [], []
    for g in range(kvh):
        keys.append(jnp.concatenate([key_ref[:, g * HD : (g + 1) * HD], cache_ref[:, g * HD : (g + 1) * HD]], axis=0))
        value = jnp.concatenate([cache_ref[:, width + g * HD : width + (g + 1) * HD], ones], axis=1)
        values.append(jnp.concatenate([value_ref[:, 2 * g * HD : (2 * g + 2) * HD], value], axis=0))
    chunk = CHUNK * HD
    per_group = gq // CHUNK
    count = q_ref.shape[1] // chunk

    def scores_of(c):
        return dot_nt(head_rows(q_ref, c, CHUNK), keys[c // per_group])

    copies = []
    ahead = scores_of(0)
    for c in range(count):
        scores = ahead
        if c + 1 < count:
            ahead = scores_of(c + 1)
        weights = []
        for j in range(CHUNK):
            s = scores[j * SPAN : (j + 1) * SPAN]
            s_new = jnp.where(causal, s[:, :SPAN], NEGATIVE)
            s_cache = jnp.where(visible, s[:, SPAN + old :], NEGATIVE)
            s = jnp.concatenate([s_new, s[:, SPAN : SPAN + old], s_cache], axis=1)
            top = jnp.max(s, axis=1, keepdims=True)
            weights.append(jnp.exp2((s - top) * SCALE2).astype(jnp.bfloat16))
        out = dot_nn(jnp.concatenate(weights, axis=0), values[c // per_group])
        out = (out[:, :HD] / out[:, HD:]).astype(jnp.bfloat16)
        for j in range(CHUNK):
            stage[:, (c * CHUNK + j) * HD : (c * CHUNK + j + 1) * HD] = out[j * SPAN : (j + 1) * SPAN]
        columns = pl.ds(c * chunk, chunk)
        copy = pltpu.make_async_copy(stage.at[:, columns], out_ref.at[:, columns], sems.at[c])
        copy.start()
        copies.append(copy)
    for copy in copies:
        copy.wait()


def swap(x, axis, distance):
    return lax.ppermute(x, axis, [(i, i ^ distance) for i in range(lax.axis_size(axis))])


def on_device(q_new, kv_new, prompt_kv, cache_kv, ancestors, lengths):
    dom_count = lax.axis_size("dom")
    ctx_count = lax.axis_size("ctx")
    y_count = ctx_count // Z
    group, page_rows, _, width = cache_kv.shape
    tokens, q_width = q_new.shape
    half_rows = prompt_kv.shape[0] // 2
    shape = jax.ShapeDtypeStruct
    half, *rest = pl.pallas_call(
        functools.partial(pack_kernel, dom_count),
        out_shape=(
            shape((half_rows, 2 * width), jnp.bfloat16),
            *[shape((RUN, page_rows, 2 * width), jnp.bfloat16)] * dom_count,
            shape((group // RUN, page_rows, HD), jnp.bfloat16),
            shape((8, ctx_count * page_rows), jnp.int32),
            shape(q_new.shape, q_new.dtype),
        ),
        in_specs=[HBM] * 5,
        out_specs=(VMEM,) * (4 + dom_count),
        scratch_shapes=[
            pltpu.SMEM(ancestors.shape, jnp.int32),
            pltpu.SMEM(lengths.shape, jnp.int32),
            pltpu.VMEM((half_rows, 2, width), jnp.bfloat16),
            pltpu.VMEM(cache_kv.shape, jnp.bfloat16),
            pltpu.SemaphoreType.DMA((4 + Q_COPIES,)),
        ],
        compiler_params=params(12),
        name="pack",
    )(*(pltpu.with_memory_space_constraint(x, pltpu.HBM) for x in (ancestors, lengths, prompt_kv, cache_kv, q_new)))
    outgoing, (far, limit, queries) = rest[:dom_count], rest[dom_count:]

    pieces = [half] + [swap(half, "ctx", k * y_count) for k in range(1, Z)]
    pieces += [swap(p, "ctx", k) for k in range(1, y_count) for p in pieces[:Z]]
    pieces += [swap(p, "dom", 1) for p in pieces]

    incoming = outgoing[:1] + [swap(outgoing[k], "dom", k) for k in range(1, dom_count)]
    routed = pl.pallas_call(
        route_kernel,
        out_shape=pltpu.HBM((group, page_rows, 2 * width), jnp.bfloat16),
        in_specs=[VMEM] * (1 + dom_count),
        out_specs=HBM,
        scratch_shapes=[pltpu.VMEM((group, page_rows, 2 * width), jnp.bfloat16), pltpu.SemaphoreType.DMA],
        compiler_params=params(12),
        name="route",
    )(far, *incoming)
    pages = lax.all_to_all(routed, "ctx", split_axis=0, concat_axis=0, tiled=True)
    pages = pages.reshape(ctx_count * page_rows, 2 * width)

    key_count = SPAN + sum(piece.shape[0] for piece in pieces)
    keys, values = pl.pallas_call(
        gather_kernel,
        out_shape=(shape((key_count, width), jnp.bfloat16), shape((key_count, 2 * width), jnp.bfloat16)),
        in_specs=[VMEM] * (1 + len(pieces)),
        out_specs=(VMEM, VMEM),
        compiler_params=params(16),
        cost_estimate=pl.CostEstimate(flops=10**10, bytes_accessed=2**22, transcendentals=0),
        name="gather",
    )(kv_new, *pieces)
    return pl.pallas_call(
        attend_kernel,
        out_shape=shape((tokens, q_width), jnp.bfloat16),
        in_specs=[VMEM] * 5,
        out_specs=HBM,
        scratch_shapes=[pltpu.VMEM((tokens, q_width), jnp.bfloat16), pltpu.SemaphoreType.DMA((q_width // (CHUNK * HD),))],
        compiler_params=params(40 if prompt_kv.shape[0] * ctx_count > 1024 else 24),
        name="attend",
    )(limit, queries, keys, values, pages)


def solution(mesh):
    placed = (
        P(("dom", "ctx"), None),
        P(("dom", "ctx"), None, None),
        P("ctx", None, None),
        P("dom", "ctx", None, None),
        P(),
        P(),
    )
    return jax.shard_map(
        on_device, mesh=mesh, in_specs=placed, out_specs=P(("dom", "ctx"), None), check_vma=False
    )
```

```python
import functools

import jax
import jax.numpy as jnp
from jax import lax
from jax.experimental import pallas as pl
from jax.experimental.pallas import tpu as pltpu
from jax.sharding import PartitionSpec as P

HD = 128
SPAN = 128
PAGE = 8
RUN = 4
Z = 4
CHUNK = 4
Q_COPIES = 4
NEGATIVE = -1e30
SCALE2 = HD ** (-0.5) * 1.4426950408889634
VMEM = pl.BlockSpec(memory_space=pltpu.VMEM)
HBM = pl.BlockSpec(memory_space=pltpu.HBM)


def params(mib):
    return pltpu.CompilerParams(vmem_limit_bytes=mib * 2**20)


def pack_kernel(dom_count, anc_hbm, len_hbm, prompt_hbm, cache_hbm, half_ref, *refs):
    out_refs = refs[:dom_count]
    far_ref, limit_ref, anc_ref, len_ref, prompt_ref, cache_ref, sems = refs[dom_count:]
    group = cache_ref.shape[0]
    dom = lax.axis_index("dom")
    rows, width = half_ref.shape
    from_row = pl.multiple_of((dom % 2) * rows, rows)
    prompt_in = pltpu.make_async_copy(prompt_hbm.at[pl.ds(from_row, rows)], prompt_ref, sems.at[0])
    anc_in = pltpu.make_async_copy(anc_hbm, anc_ref, sems.at[1])
    len_in = pltpu.make_async_copy(len_hbm, len_ref, sems.at[2])
    cache_in = pltpu.make_async_copy(cache_hbm, cache_ref, sems.at[3])
    prompt_in.start()
    anc_in.start()
    len_in.start()
    cache_in.start()
    runs = group // RUN
    anc_in.wait()
    len_in.wait()
    for run in range(runs):
        far = (anc_ref[dom * group + run * RUN] // group) ^ dom
        far_ref[run] = jnp.full(far_ref.shape[1:], far.astype(jnp.float32)).astype(jnp.bfloat16)
    particle = dom * group + lax.axis_index("ctx")
    limit_ref[...] = jnp.full(limit_ref.shape, len_ref[anc_ref[particle]] * PAGE)
    prompt_in.wait()
    half_ref[...] = prompt_ref[...].reshape(rows, width)
    cache_in.wait()
    for k, out_ref in enumerate(out_refs):
        for run in range(runs):
            first = (dom ^ k) * group + run * RUN

            @pl.when(anc_ref[first] // group == dom)
            def _(first=first, out_ref=out_ref):
                for slot in range(RUN):
                    local = anc_ref[first + slot] % group
                    out_ref[slot] = cache_ref[local].reshape(cache_ref.shape[1], width)


def route_kernel(far_ref, *refs):
    *in_refs, out_hbm, out_ref, sem = refs
    width = out_ref.shape[2]
    for run in range(far_ref.shape[0]):
        far = far_ref[run]
        for slot in range(RUN):
            picked = in_refs[0][slot]
            for k in range(1, len(in_refs)):
                here = jnp.concatenate([far == k] * (width // far.shape[1]), axis=1)
                picked = jnp.where(here, in_refs[k][slot], picked)
            out_ref[run * RUN + slot] = picked
    out = pltpu.make_async_copy(out_ref, out_hbm, sem)
    out.start()
    out.wait()


def head_rows(q_ref, g, gq):
    return jnp.concatenate(
        [q_ref[:, (g * gq + j) * HD : (g * gq + j + 1) * HD] for j in range(gq)], axis=0
    )


def dot_nt(a, b):
    return lax.dot_general(a, b, (((1,), (1,)), ((), ())), preferred_element_type=jnp.float32)


def dot_nn(a, b):
    return lax.dot_general(a, b, (((1,), (0,)), ((), ())), preferred_element_type=jnp.float32)


def gather_kernel(q_hbm, new_ref, *refs):
    pieces, (kv_ref, q_ref, sems) = refs[:-3], refs[-3:]
    q_rows = q_ref.shape[0] // Q_COPIES
    copies = []
    for number in range(Q_COPIES):
        rows_at = pl.ds(number * q_rows, q_rows)
        copies.append(pltpu.make_async_copy(q_hbm.at[rows_at], q_ref.at[rows_at], sems.at[number]))
        copies[number].start()
    kv_ref[:SPAN, :] = new_ref[...].reshape(SPAN, kv_ref.shape[1])
    at = SPAN
    for piece in pieces:
        kv_ref[at : at + piece.shape[0], :] = piece[...]
        at += piece.shape[0]
    for copy in copies:
        copy.wait()


def attend_kernel(limit_ref, q_ref, kv_ref, *refs):
    late, (cache_ref, out_ref, stage, sems) = refs[:-4], refs[-4:]
    width = kv_ref.shape[1] // 2
    gen = cache_ref.shape[0]
    kvh = width // HD
    gq = q_ref.shape[1] // width
    old = kv_ref.shape[0] - SPAN + sum(piece.shape[0] for piece in late)
    token = lax.broadcasted_iota(jnp.int32, (SPAN, SPAN), 0)
    causal = lax.broadcasted_iota(jnp.int32, (SPAN, SPAN), 1) <= token
    visible = lax.broadcasted_iota(jnp.int32, (SPAN, gen), 1) < jnp.broadcast_to(limit_ref[:1], (SPAN, gen))
    ones = jnp.ones((SPAN + old + gen, HD), jnp.bfloat16)
    keys, values = [], []
    for g in range(kvh):
        k_at = slice(g * HD, (g + 1) * HD)
        v_at = slice(width + g * HD, width + (g + 1) * HD)
        keys.append(jnp.concatenate([ref[:, k_at] for ref in (kv_ref, *late, cache_ref)], axis=0))
        value = jnp.concatenate([ref[:, v_at] for ref in (kv_ref, *late, cache_ref)], axis=0)
        values.append(jnp.concatenate([value, ones], axis=1))
    chunk = CHUNK * HD
    per_group = gq // CHUNK
    count = q_ref.shape[1] // chunk

    def scores_of(c):
        return dot_nt(head_rows(q_ref, c, CHUNK), keys[c // per_group])

    copies = []
    ahead = scores_of(0)
    for c in range(count):
        scores = ahead
        if c + 1 < count:
            ahead = scores_of(c + 1)
        weights = []
        for j in range(CHUNK):
            s = scores[j * SPAN : (j + 1) * SPAN]
            s_new = jnp.where(causal, s[:, :SPAN], NEGATIVE)
            s_cache = jnp.where(visible, s[:, SPAN + old :], NEGATIVE)
            s = jnp.concatenate([s_new, s[:, SPAN : SPAN + old], s_cache], axis=1)
            top = jnp.max(s, axis=1, keepdims=True)
            weights.append(jnp.exp2((s - top) * SCALE2).astype(jnp.bfloat16))
        out = dot_nn(jnp.concatenate(weights, axis=0), values[c // per_group])
        out = (out[:, :HD] / out[:, HD:]).astype(jnp.bfloat16)
        for j in range(CHUNK):
            stage[:, (c * CHUNK + j) * HD : (c * CHUNK + j + 1) * HD] = out[j * SPAN : (j + 1) * SPAN]
        columns = pl.ds(c * chunk, chunk)
        copy = pltpu.make_async_copy(stage.at[:, columns], out_ref.at[:, columns], sems.at[c])
        copy.start()
        copies.append(copy)
    for copy in copies:
        copy.wait()


def swap(x, axis, distance):
    return lax.ppermute(x, axis, [(i, i ^ distance) for i in range(lax.axis_size(axis))])


def on_device(q_new, kv_new, prompt_kv, cache_kv, ancestors, lengths):
    dom_count = lax.axis_size("dom")
    ctx_count = lax.axis_size("ctx")
    y_count = ctx_count // Z
    group, page_rows, _, width = cache_kv.shape
    tokens, q_width = q_new.shape
    half_rows = prompt_kv.shape[0] // 2
    shape = jax.ShapeDtypeStruct
    half, *rest = pl.pallas_call(
        functools.partial(pack_kernel, dom_count),
        out_shape=(
            shape((half_rows, 2 * width), jnp.bfloat16),
            *[shape((RUN, page_rows, 2 * width), jnp.bfloat16)] * dom_count,
            shape((group // RUN, page_rows, HD), jnp.bfloat16),
            shape((8, ctx_count * page_rows), jnp.int32),
        ),
        in_specs=[HBM] * 4,
        out_specs=(VMEM,) * (3 + dom_count),
        scratch_shapes=[
            pltpu.SMEM(ancestors.shape, jnp.int32),
            pltpu.SMEM(lengths.shape, jnp.int32),
            pltpu.VMEM((half_rows, 2, width), jnp.bfloat16),
            pltpu.VMEM(cache_kv.shape, jnp.bfloat16),
            pltpu.SemaphoreType.DMA((4,)),
        ],
        compiler_params=params(12),
        name="pack",
    )(*(pltpu.with_memory_space_constraint(x, pltpu.HBM) for x in (ancestors, lengths, prompt_kv, cache_kv)))
    outgoing, (far, limit) = rest[:dom_count], rest[dom_count:]

    pieces = [half] + [swap(half, "ctx", k * y_count) for k in range(1, Z)]
    pieces += [swap(p, "ctx", k) for k in range(1, y_count) for p in pieces[:Z]]
    pieces += [swap(p, "dom", 1) for p in pieces]

    incoming = outgoing[:1] + [swap(outgoing[k], "dom", k) for k in range(1, dom_count)]
    routed = pl.pallas_call(
        route_kernel,
        out_shape=pltpu.HBM((group, page_rows, 2 * width), jnp.bfloat16),
        in_specs=[VMEM] * (1 + dom_count),
        out_specs=HBM,
        scratch_shapes=[pltpu.VMEM((group, page_rows, 2 * width), jnp.bfloat16), pltpu.SemaphoreType.DMA],
        compiler_params=params(12),
        name="route",
    )(far, *incoming)
    pages = lax.all_to_all(routed, "ctx", split_axis=0, concat_axis=0, tiled=True)
    pages = pages.reshape(ctx_count * page_rows, 2 * width)

    late = [pieces.pop(at) for at in sorted((*range(Z + 2, 2 * Z), *range(len(pieces) - Z + 2, len(pieces))), reverse=True)]
    key_count = SPAN + sum(piece.shape[0] for piece in pieces)
    kv, queries = pl.pallas_call(
        gather_kernel,
        out_shape=(shape((key_count, 2 * width), jnp.bfloat16), shape(q_new.shape, q_new.dtype)),
        in_specs=[HBM] + [VMEM] * (1 + len(pieces)),
        out_specs=(VMEM, VMEM),
        scratch_shapes=[pltpu.SemaphoreType.DMA((Q_COPIES,))],
        compiler_params=params(16),
        cost_estimate=pl.CostEstimate(flops=10**9, bytes_accessed=2**22, transcendentals=0),
        name="gather",
    )(pltpu.with_memory_space_constraint(q_new, pltpu.HBM), kv_new, *pieces)
    return pl.pallas_call(
        attend_kernel,
        out_shape=shape((tokens, q_width), jnp.bfloat16),
        in_specs=[VMEM] * (4 + len(late)),
        out_specs=HBM,
        scratch_shapes=[pltpu.VMEM((tokens, q_width), jnp.bfloat16), pltpu.SemaphoreType.DMA((q_width // (CHUNK * HD),))],
        compiler_params=params(40 if prompt_kv.shape[0] * ctx_count > 1024 else 24),
        name="attend",
    )(limit, queries, kv, *late, pages)


def solution(mesh):
    placed = (
        P(("dom", "ctx"), None),
        P(("dom", "ctx"), None, None),
        P("ctx", None, None),
        P("dom", "ctx", None, None),
        P(),
        P(),
    )
    return jax.shard_map(
        on_device, mesh=mesh, in_specs=placed, out_specs=P(("dom", "ctx"), None), check_vma=False
    )
```

```python
import functools

import jax
import jax.numpy as jnp
from jax import lax
from jax.experimental import pallas as pl
from jax.experimental.pallas import tpu as pltpu
from jax.sharding import PartitionSpec as P

HD = 128
SPAN = 128
PAGE = 8
RUN = 4
Z = 4
CHUNK = 4
Q_COPIES = 4
NEGATIVE = -1e30
SCALE2 = HD ** (-0.5) * 1.4426950408889634
VMEM = pl.BlockSpec(memory_space=pltpu.VMEM)
HBM = pl.BlockSpec(memory_space=pltpu.HBM)


def params(mib):
    return pltpu.CompilerParams(vmem_limit_bytes=mib * 2**20)


def pack_kernel(dom_count, anc_hbm, len_hbm, prompt_hbm, cache_hbm, half_ref, *refs):
    out_refs = refs[:dom_count]
    far_ref, limit_ref, anc_ref, len_ref, prompt_ref, cache_ref, sems = refs[dom_count:]
    group = cache_ref.shape[0]
    dom = lax.axis_index("dom")
    rows, width = half_ref.shape
    from_row = pl.multiple_of((dom % 2) * rows, rows)
    prompt_in = pltpu.make_async_copy(prompt_hbm.at[pl.ds(from_row, rows)], prompt_ref, sems.at[0])
    anc_in = pltpu.make_async_copy(anc_hbm, anc_ref, sems.at[1])
    len_in = pltpu.make_async_copy(len_hbm, len_ref, sems.at[2])
    cache_in = pltpu.make_async_copy(cache_hbm, cache_ref, sems.at[3])
    prompt_in.start()
    anc_in.start()
    len_in.start()
    cache_in.start()
    runs = group // RUN
    anc_in.wait()
    len_in.wait()
    for run in range(runs):
        far = (anc_ref[dom * group + run * RUN] // group) ^ dom
        far_ref[run] = jnp.full(far_ref.shape[1:], far.astype(jnp.float32)).astype(jnp.bfloat16)
    particle = dom * group + lax.axis_index("ctx")
    limit_ref[...] = jnp.full(limit_ref.shape, len_ref[anc_ref[particle]] * PAGE)
    prompt_in.wait()
    half_ref[...] = prompt_ref[...].reshape(rows, width)
    cache_in.wait()
    for k, out_ref in enumerate(out_refs):
        for run in range(runs):
            first = (dom ^ k) * group + run * RUN

            @pl.when(anc_ref[first] // group == dom)
            def _(first=first, out_ref=out_ref):
                for slot in range(RUN):
                    local = anc_ref[first + slot] % group
                    out_ref[slot] = cache_ref[local].reshape(cache_ref.shape[1], width)


def route_kernel(far_ref, *refs):
    *in_refs, out_hbm, out_ref, sem = refs
    width = out_ref.shape[2]
    for run in range(far_ref.shape[0]):
        far = far_ref[run]
        for slot in range(RUN):
            picked = in_refs[0][slot]
            for k in range(1, len(in_refs)):
                here = jnp.concatenate([far == k] * (width // far.shape[1]), axis=1)
                picked = jnp.where(here, in_refs[k][slot], picked)
            out_ref[run * RUN + slot] = picked
    out = pltpu.make_async_copy(out_ref, out_hbm, sem)
    out.start()
    out.wait()


def head_rows(q_ref, g, gq):
    return jnp.concatenate(
        [q_ref[:, (g * gq + j) * HD : (g * gq + j + 1) * HD] for j in range(gq)], axis=0
    )


def dot_nt(a, b):
    return lax.dot_general(a, b, (((1,), (1,)), ((), ())), preferred_element_type=jnp.float32)


def dot_nn(a, b):
    return lax.dot_general(a, b, (((1,), (0,)), ((), ())), preferred_element_type=jnp.float32)


def gather_kernel(q_hbm, new_ref, *refs):
    pieces, (kv_ref, q_ref, sems) = refs[:-3], refs[-3:]
    q_rows = q_ref.shape[0] // Q_COPIES
    copies = []
    for number in range(Q_COPIES):
        rows_at = pl.ds(number * q_rows, q_rows)
        copies.append(pltpu.make_async_copy(q_hbm.at[rows_at], q_ref.at[rows_at], sems.at[number]))
        copies[number].start()
    kv_ref[:SPAN, :] = new_ref[...].reshape(SPAN, kv_ref.shape[1])
    at = SPAN
    for piece in pieces:
        kv_ref[at : at + piece.shape[0], :] = piece[...]
        at += piece.shape[0]
    for copy in copies:
        copy.wait()


def attend_kernel(limit_ref, q_ref, kv_ref, *refs):
    late, (cache_ref, out_ref, stage, sems) = refs[:-4], refs[-4:]
    width = kv_ref.shape[1] // 2
    gen = cache_ref.shape[0]
    kvh = width // HD
    gq = q_ref.shape[1] // width
    old = kv_ref.shape[0] - SPAN + sum(piece.shape[0] for piece in late)
    token = lax.broadcasted_iota(jnp.int32, (SPAN, SPAN), 0)
    causal = lax.broadcasted_iota(jnp.int32, (SPAN, SPAN), 1) <= token
    visible = lax.broadcasted_iota(jnp.int32, (SPAN, gen), 1) < jnp.broadcast_to(limit_ref[:1], (SPAN, gen))
    ones = jnp.ones((SPAN + old + gen, HD), jnp.bfloat16)
    keys, values = [], []
    for g in range(kvh):
        k_at = slice(g * HD, (g + 1) * HD)
        v_at = slice(width + g * HD, width + (g + 1) * HD)
        keys.append(jnp.concatenate([ref[:, k_at] for ref in (kv_ref, *late, cache_ref)], axis=0))
        value = jnp.concatenate([ref[:, v_at] for ref in (kv_ref, *late, cache_ref)], axis=0)
        values.append(jnp.concatenate([value, ones], axis=1))
    chunk = CHUNK * HD
    per_group = gq // CHUNK
    count = q_ref.shape[1] // chunk

    def scores_of(c):
        return dot_nt(head_rows(q_ref, c, CHUNK), keys[c // per_group])

    copies = []
    ahead = scores_of(0)
    for c in range(count):
        scores = ahead
        if c + 1 < count:
            ahead = scores_of(c + 1)
        weights = []
        for j in range(CHUNK):
            s = scores[j * SPAN : (j + 1) * SPAN]
            s_new = jnp.where(causal, s[:, :SPAN], NEGATIVE)
            s_cache = jnp.where(visible, s[:, SPAN + old :], NEGATIVE)
            s = jnp.concatenate([s_new, s[:, SPAN : SPAN + old], s_cache], axis=1)
            top = jnp.max(s, axis=1, keepdims=True)
            weights.append(jnp.exp2((s - top) * SCALE2).astype(jnp.bfloat16))
        out = dot_nn(jnp.concatenate(weights, axis=0), values[c // per_group])
        out = (out[:, :HD] / out[:, HD:]).astype(jnp.bfloat16)
        for j in range(CHUNK):
            stage[:, (c * CHUNK + j) * HD : (c * CHUNK + j + 1) * HD] = out[j * SPAN : (j + 1) * SPAN]
        columns = pl.ds(c * chunk, chunk)
        copy = pltpu.make_async_copy(stage.at[:, columns], out_ref.at[:, columns], sems.at[c])
        copy.start()
        copies.append(copy)
    for copy in copies:
        copy.wait()


def swap(x, axis, distance):
    return lax.ppermute(x, axis, [(i, i ^ distance) for i in range(lax.axis_size(axis))])


def on_device(q_new, kv_new, prompt_kv, cache_kv, ancestors, lengths):
    dom_count = lax.axis_size("dom")
    ctx_count = lax.axis_size("ctx")
    y_count = ctx_count // Z
    group, page_rows, _, width = cache_kv.shape
    tokens, q_width = q_new.shape
    half_rows = prompt_kv.shape[0] // 2
    shape = jax.ShapeDtypeStruct
    half, *rest = pl.pallas_call(
        functools.partial(pack_kernel, dom_count),
        out_shape=(
            shape((half_rows, 2 * width), jnp.bfloat16),
            *[shape((RUN, page_rows, 2 * width), jnp.bfloat16)] * dom_count,
            shape((group // RUN, page_rows, HD), jnp.bfloat16),
            shape((8, ctx_count * page_rows), jnp.int32),
        ),
        in_specs=[HBM] * 4,
        out_specs=(VMEM,) * (3 + dom_count),
        scratch_shapes=[
            pltpu.SMEM(ancestors.shape, jnp.int32),
            pltpu.SMEM(lengths.shape, jnp.int32),
            pltpu.VMEM((half_rows, 2, width), jnp.bfloat16),
            pltpu.VMEM(cache_kv.shape, jnp.bfloat16),
            pltpu.SemaphoreType.DMA((4,)),
        ],
        compiler_params=params(12),
        name="pack",
    )(*(pltpu.with_memory_space_constraint(x, pltpu.HBM) for x in (ancestors, lengths, prompt_kv, cache_kv)))
    outgoing, (far, limit) = rest[:dom_count], rest[dom_count:]

    pieces = [half] + [swap(half, "ctx", k * y_count) for k in range(1, Z)]
    pieces += [swap(p, "ctx", k) for k in range(1, y_count) for p in pieces[:Z]]
    pieces += [swap(p, "dom", 1) for p in pieces]

    incoming = outgoing[:1] + [swap(outgoing[k], "dom", k) for k in range(1, dom_count)]
    routed = pl.pallas_call(
        route_kernel,
        out_shape=pltpu.HBM((group, page_rows, 2 * width), jnp.bfloat16),
        in_specs=[VMEM] * (1 + dom_count),
        out_specs=HBM,
        scratch_shapes=[pltpu.VMEM((group, page_rows, 2 * width), jnp.bfloat16), pltpu.SemaphoreType.DMA],
        compiler_params=params(12),
        name="route",
    )(far, *incoming)
    pages = lax.all_to_all(routed, "ctx", split_axis=0, concat_axis=0, tiled=True)
    pages = pages.reshape(ctx_count * page_rows, 2 * width)

    late = [pieces.pop(at) for at in sorted((Z, *range(Z + 2, 2 * Z), len(pieces) - Z, *range(len(pieces) - Z + 2, len(pieces))), reverse=True)]
    key_count = SPAN + sum(piece.shape[0] for piece in pieces)
    kv, queries = pl.pallas_call(
        gather_kernel,
        out_shape=(shape((key_count, 2 * width), jnp.bfloat16), shape(q_new.shape, q_new.dtype)),
        in_specs=[HBM] + [VMEM] * (1 + len(pieces)),
        out_specs=(VMEM, VMEM),
        scratch_shapes=[pltpu.SemaphoreType.DMA((Q_COPIES,))],
        compiler_params=params(16),
        cost_estimate=pl.CostEstimate(flops=3 * 10**9, bytes_accessed=2**22, transcendentals=0),
        name="gather",
    )(pltpu.with_memory_space_constraint(q_new, pltpu.HBM), kv_new, *pieces)
    return pl.pallas_call(
        attend_kernel,
        out_shape=shape((tokens, q_width), jnp.bfloat16),
        in_specs=[VMEM] * (4 + len(late)),
        out_specs=HBM,
        scratch_shapes=[pltpu.VMEM((tokens, q_width), jnp.bfloat16), pltpu.SemaphoreType.DMA((q_width // (CHUNK * HD),))],
        compiler_params=params(40 if prompt_kv.shape[0] * ctx_count > 1024 else 24),
        name="attend",
    )(limit, queries, kv, *late, pages)


def solution(mesh):
    placed = (
        P(("dom", "ctx"), None),
        P(("dom", "ctx"), None, None),
        P("ctx", None, None),
        P("dom", "ctx", None, None),
        P(),
        P(),
    )
    return jax.shard_map(
        on_device, mesh=mesh, in_specs=placed, out_specs=P(("dom", "ctx"), None), check_vma=False
    )
```

```python
import functools

import jax
import jax.numpy as jnp
from jax import lax
from jax.experimental import pallas as pl
from jax.experimental.pallas import tpu as pltpu
from jax.sharding import PartitionSpec as P

HD = 128
SPAN = 128
PAGE = 8
RUN = 4
Z = 4
CHUNK = 4
Q_COPIES = 4
NEGATIVE = -1e30
SCALE2 = HD ** (-0.5) * 1.4426950408889634
VMEM = pl.BlockSpec(memory_space=pltpu.VMEM)
HBM = pl.BlockSpec(memory_space=pltpu.HBM)


def params(mib):
    return pltpu.CompilerParams(vmem_limit_bytes=mib * 2**20)


def pack_kernel(dom_count, anc_hbm, len_hbm, prompt_hbm, cache_hbm, half_ref, *refs):
    out_refs = refs[:dom_count]
    far_ref, limit_ref, anc_ref, len_ref, prompt_ref, cache_ref, sems = refs[dom_count:]
    group = cache_ref.shape[0]
    dom = lax.axis_index("dom")
    rows, width = half_ref.shape
    from_row = pl.multiple_of((dom % 2) * rows, rows)
    prompt_in = pltpu.make_async_copy(prompt_hbm.at[pl.ds(from_row, rows)], prompt_ref, sems.at[0])
    anc_in = pltpu.make_async_copy(anc_hbm, anc_ref, sems.at[1])
    len_in = pltpu.make_async_copy(len_hbm, len_ref, sems.at[2])
    cache_in = pltpu.make_async_copy(cache_hbm, cache_ref, sems.at[3])
    prompt_in.start()
    anc_in.start()
    len_in.start()
    cache_in.start()
    runs = group // RUN
    anc_in.wait()
    len_in.wait()
    for run in range(runs):
        far = (anc_ref[dom * group + run * RUN] // group) ^ dom
        far_ref[run] = jnp.full(far_ref.shape[1:], far.astype(jnp.float32)).astype(jnp.bfloat16)
    particle = dom * group + lax.axis_index("ctx")
    limit_ref[...] = jnp.full(limit_ref.shape, len_ref[anc_ref[particle]] * PAGE)
    prompt_in.wait()
    half_ref[...] = prompt_ref[...].reshape(rows, width)
    cache_in.wait()
    for k, out_ref in enumerate(out_refs):
        for run in range(runs):
            first = (dom ^ k) * group + run * RUN

            @pl.when(anc_ref[first] // group == dom)
            def _(first=first, out_ref=out_ref):
                for slot in range(RUN):
                    local = anc_ref[first + slot] % group
                    out_ref[slot] = cache_ref[local].reshape(cache_ref.shape[1], width)


def route_kernel(dom_count, far_ref, *refs):
    in_refs, (out_hbm, out_ref, sem) = refs[:dom_count], refs[-3:]
    width = out_ref.shape[2]
    for run in range(far_ref.shape[0]):
        far = far_ref[run]
        for slot in range(RUN):
            picked = in_refs[0][slot]
            for k in range(1, len(in_refs)):
                here = jnp.concatenate([far == k] * (width // far.shape[1]), axis=1)
                picked = jnp.where(here, in_refs[k][slot], picked)
            out_ref[run * RUN + slot] = picked
    out = pltpu.make_async_copy(out_ref, out_hbm, sem)
    out.start()
    out.wait()


def head_rows(q_ref, g, gq):
    return jnp.concatenate(
        [q_ref[:, (g * gq + j) * HD : (g * gq + j + 1) * HD] for j in range(gq)], axis=0
    )


def dot_nt(a, b):
    return lax.dot_general(a, b, (((1,), (1,)), ((), ())), preferred_element_type=jnp.float32)


def dot_nn(a, b):
    return lax.dot_general(a, b, (((1,), (0,)), ((), ())), preferred_element_type=jnp.float32)


def gather_kernel(q_hbm, new_ref, *refs):
    pieces, (kv_ref, q_ref, sems) = refs[:-3], refs[-3:]
    q_rows = q_ref.shape[0] // Q_COPIES
    copies = []
    for number in range(Q_COPIES):
        rows_at = pl.ds(number * q_rows, q_rows)
        copies.append(pltpu.make_async_copy(q_hbm.at[rows_at], q_ref.at[rows_at], sems.at[number]))
        copies[number].start()
    kv_ref[:SPAN, :] = new_ref[...].reshape(SPAN, kv_ref.shape[1])
    at = SPAN
    for piece in pieces:
        kv_ref[at : at + piece.shape[0], :] = piece[...]
        at += piece.shape[0]
    for copy in copies:
        copy.wait()


def attend_kernel(limit_ref, q_ref, kv_ref, *refs):
    late, (cache_ref, out_ref, stage, sems) = refs[:-4], refs[-4:]
    width = kv_ref.shape[1] // 2
    gen = cache_ref.shape[0]
    kvh = width // HD
    gq = q_ref.shape[1] // width
    old = kv_ref.shape[0] - SPAN + sum(piece.shape[0] for piece in late)
    token = lax.broadcasted_iota(jnp.int32, (SPAN, SPAN), 0)
    causal = lax.broadcasted_iota(jnp.int32, (SPAN, SPAN), 1) <= token
    visible = lax.broadcasted_iota(jnp.int32, (SPAN, gen), 1) < jnp.broadcast_to(limit_ref[:1], (SPAN, gen))
    ones = jnp.ones((SPAN + old + gen, HD), jnp.bfloat16)
    keys, values = [], []
    for g in range(kvh):
        k_at = slice(g * HD, (g + 1) * HD)
        v_at = slice(width + g * HD, width + (g + 1) * HD)
        keys.append(jnp.concatenate([ref[:, k_at] for ref in (kv_ref, *late, cache_ref)], axis=0))
        value = jnp.concatenate([ref[:, v_at] for ref in (kv_ref, *late, cache_ref)], axis=0)
        values.append(jnp.concatenate([value, ones], axis=1))
    chunk = CHUNK * HD
    per_group = gq // CHUNK
    count = q_ref.shape[1] // chunk

    def scores_of(c):
        return dot_nt(head_rows(q_ref, c, CHUNK), keys[c // per_group])

    copies = []
    ahead = scores_of(0)
    for c in range(count):
        scores = ahead
        if c + 1 < count:
            ahead = scores_of(c + 1)
        weights = []
        for j in range(CHUNK):
            s = scores[j * SPAN : (j + 1) * SPAN]
            s_new = jnp.where(causal, s[:, :SPAN], NEGATIVE)
            s_cache = jnp.where(visible, s[:, SPAN + old :], NEGATIVE)
            s = jnp.concatenate([s_new, s[:, SPAN : SPAN + old], s_cache], axis=1)
            top = jnp.max(s, axis=1, keepdims=True)
            weights.append(jnp.exp2((s - top) * SCALE2).astype(jnp.bfloat16))
        out = dot_nn(jnp.concatenate(weights, axis=0), values[c // per_group])
        out = (out[:, :HD] / out[:, HD:]).astype(jnp.bfloat16)
        for j in range(CHUNK):
            stage[:, (c * CHUNK + j) * HD : (c * CHUNK + j + 1) * HD] = out[j * SPAN : (j + 1) * SPAN]
        columns = pl.ds(c * chunk, chunk)
        copy = pltpu.make_async_copy(stage.at[:, columns], out_ref.at[:, columns], sems.at[c])
        copy.start()
        copies.append(copy)
    for copy in copies:
        copy.wait()


def swap(x, axis, distance):
    return lax.ppermute(x, axis, [(i, i ^ distance) for i in range(lax.axis_size(axis))])


def on_device(q_new, kv_new, prompt_kv, cache_kv, ancestors, lengths):
    dom_count = lax.axis_size("dom")
    ctx_count = lax.axis_size("ctx")
    y_count = ctx_count // Z
    group, page_rows, _, width = cache_kv.shape
    tokens, q_width = q_new.shape
    half_rows = prompt_kv.shape[0] // 2
    shape = jax.ShapeDtypeStruct
    half, *rest = pl.pallas_call(
        functools.partial(pack_kernel, dom_count),
        out_shape=(
            shape((half_rows, 2 * width), jnp.bfloat16),
            *[shape((RUN, page_rows, 2 * width), jnp.bfloat16)] * dom_count,
            shape((group // RUN, page_rows, HD), jnp.bfloat16),
            shape((8, ctx_count * page_rows), jnp.int32),
        ),
        in_specs=[HBM] * 4,
        out_specs=(VMEM,) * (3 + dom_count),
        scratch_shapes=[
            pltpu.SMEM(ancestors.shape, jnp.int32),
            pltpu.SMEM(lengths.shape, jnp.int32),
            pltpu.VMEM((half_rows, 2, width), jnp.bfloat16),
            pltpu.VMEM(cache_kv.shape, jnp.bfloat16),
            pltpu.SemaphoreType.DMA((4,)),
        ],
        compiler_params=params(12),
        name="pack",
    )(*(pltpu.with_memory_space_constraint(x, pltpu.HBM) for x in (ancestors, lengths, prompt_kv, cache_kv)))
    outgoing, (far, limit) = rest[:dom_count], rest[dom_count:]

    pieces = [half] + [swap(half, "ctx", k * y_count) for k in range(1, Z)]
    pieces += [swap(p, "ctx", k) for k in range(1, y_count) for p in pieces[:Z]]
    pieces += [swap(p, "dom", 1) for p in pieces]

    incoming = outgoing[:1] + [swap(outgoing[k], "dom", k) for k in range(1, dom_count)]
    routed = pl.pallas_call(
        functools.partial(route_kernel, dom_count),
        out_shape=pltpu.HBM((group, page_rows, 2 * width), jnp.bfloat16),
        in_specs=[VMEM] * (1 + dom_count) + [pl.BlockSpec(memory_space=pl.ANY)] * (Z - 1),
        out_specs=HBM,
        scratch_shapes=[pltpu.VMEM((group, page_rows, 2 * width), jnp.bfloat16), pltpu.SemaphoreType.DMA],
        compiler_params=params(12),
        name="route",
    )(far, *incoming, *pieces[1:Z])
    pages = lax.all_to_all(routed, "ctx", split_axis=0, concat_axis=0, tiled=True)
    pages = pages.reshape(ctx_count * page_rows, 2 * width)

    late = [pieces.pop(at) for at in sorted((*range(Z + 2, 2 * Z), *range(len(pieces) - Z + 2, len(pieces))), reverse=True)]
    key_count = SPAN + sum(piece.shape[0] for piece in pieces)
    kv, queries = pl.pallas_call(
        gather_kernel,
        out_shape=(shape((key_count, 2 * width), jnp.bfloat16), shape(q_new.shape, q_new.dtype)),
        in_specs=[HBM] + [VMEM] * (1 + len(pieces)),
        out_specs=(VMEM, VMEM),
        scratch_shapes=[pltpu.SemaphoreType.DMA((Q_COPIES,))],
        compiler_params=params(16),
        cost_estimate=pl.CostEstimate(flops=10**9, bytes_accessed=2**22, transcendentals=0),
        name="gather",
    )(pltpu.with_memory_space_constraint(q_new, pltpu.HBM), kv_new, *pieces)
    return pl.pallas_call(
        attend_kernel,
        out_shape=shape((tokens, q_width), jnp.bfloat16),
        in_specs=[VMEM] * (4 + len(late)),
        out_specs=HBM,
        scratch_shapes=[pltpu.VMEM((tokens, q_width), jnp.bfloat16), pltpu.SemaphoreType.DMA((q_width // (CHUNK * HD),))],
        compiler_params=params(40 if prompt_kv.shape[0] * ctx_count > 1024 else 24),
        name="attend",
    )(limit, queries, kv, *late, pages)


def solution(mesh):
    placed = (
        P(("dom", "ctx"), None),
        P(("dom", "ctx"), None, None),
        P("ctx", None, None),
        P("dom", "ctx", None, None),
        P(),
        P(),
    )
    return jax.shard_map(
        on_device, mesh=mesh, in_specs=placed, out_specs=P(("dom", "ctx"), None), check_vma=False
    )
```

```python
import functools

import jax
import jax.numpy as jnp
from jax import lax
from jax.experimental import pallas as pl
from jax.experimental.pallas import tpu as pltpu
from jax.sharding import PartitionSpec as P

HD = 128
SPAN = 128
PAGE = 8
RUN = 4
Z = 4
CHUNK = 4
Q_COPIES = 4
NEGATIVE = -1e30
SCALE2 = HD ** (-0.5) * 1.4426950408889634
VMEM = pl.BlockSpec(memory_space=pltpu.VMEM)
HBM = pl.BlockSpec(memory_space=pltpu.HBM)


def params(mib):
    return pltpu.CompilerParams(vmem_limit_bytes=mib * 2**20)


def pack_kernel(dom_count, anc_hbm, len_hbm, prompt_hbm, cache_hbm, half_ref, *refs):
    out_refs = refs[:dom_count]
    far_ref, limit_ref, anc_ref, len_ref, prompt_ref, cache_ref, sems = refs[dom_count:]
    group = cache_ref.shape[0]
    dom = lax.axis_index("dom")
    rows, width = half_ref.shape
    from_row = pl.multiple_of((dom % 2) * rows, rows)
    prompt_in = pltpu.make_async_copy(prompt_hbm.at[pl.ds(from_row, rows)], prompt_ref, sems.at[0])
    anc_in = pltpu.make_async_copy(anc_hbm, anc_ref, sems.at[1])
    len_in = pltpu.make_async_copy(len_hbm, len_ref, sems.at[2])
    cache_in = pltpu.make_async_copy(cache_hbm, cache_ref, sems.at[3])
    prompt_in.start()
    anc_in.start()
    len_in.start()
    cache_in.start()
    runs = group // RUN
    anc_in.wait()
    len_in.wait()
    for run in range(runs):
        far = (anc_ref[dom * group + run * RUN] // group) ^ dom
        far_ref[run] = jnp.full(far_ref.shape[1:], far.astype(jnp.float32)).astype(jnp.bfloat16)
    particle = dom * group + lax.axis_index("ctx")
    limit_ref[...] = jnp.full(limit_ref.shape, len_ref[anc_ref[particle]] * PAGE)
    prompt_in.wait()
    half_ref[...] = prompt_ref[...].reshape(rows, width)
    cache_in.wait()
    for k, out_ref in enumerate(out_refs):
        for run in range(runs):
            first = (dom ^ k) * group + run * RUN

            @pl.when(anc_ref[first] // group == dom)
            def _(first=first, out_ref=out_ref):
                for slot in range(RUN):
                    local = anc_ref[first + slot] % group
                    out_ref[slot] = cache_ref[local].reshape(cache_ref.shape[1], width)


def route_kernel(dom_count, far_ref, *refs):
    in_refs, pieces, (out_hbm, rows_ref, out_ref, sem) = refs[:dom_count], refs[dom_count:-4], refs[-4:]
    width = out_ref.shape[2]
    for run in range(far_ref.shape[0]):
        far = far_ref[run]
        for slot in range(RUN):
            picked = in_refs[0][slot]
            for k in range(1, len(in_refs)):
                here = jnp.concatenate([far == k] * (width // far.shape[1]), axis=1)
                picked = jnp.where(here, in_refs[k][slot], picked)
            out_ref[run * RUN + slot] = picked
    out = pltpu.make_async_copy(out_ref, out_hbm, sem)
    out.start()
    for number, piece in enumerate(pieces):
        rows_ref[number * piece.shape[0] : (number + 1) * piece.shape[0], :] = piece[...]
    out.wait()


def head_rows(q_ref, g, gq):
    return jnp.concatenate(
        [q_ref[:, (g * gq + j) * HD : (g * gq + j + 1) * HD] for j in range(gq)], axis=0
    )


def dot_nt(a, b):
    return lax.dot_general(a, b, (((1,), (1,)), ((), ())), preferred_element_type=jnp.float32)


def dot_nn(a, b):
    return lax.dot_general(a, b, (((1,), (0,)), ((), ())), preferred_element_type=jnp.float32)


def gather_kernel(q_hbm, new_ref, *refs):
    pieces, (kv_ref, q_ref, sems) = refs[:-3], refs[-3:]
    q_rows = q_ref.shape[0] // Q_COPIES
    copies = []
    for number in range(Q_COPIES):
        rows_at = pl.ds(number * q_rows, q_rows)
        copies.append(pltpu.make_async_copy(q_hbm.at[rows_at], q_ref.at[rows_at], sems.at[number]))
        copies[number].start()
    kv_ref[:SPAN, :] = new_ref[...].reshape(SPAN, kv_ref.shape[1])
    at = SPAN
    for piece in pieces:
        kv_ref[at : at + piece.shape[0], :] = piece[...]
        at += piece.shape[0]
    for copy in copies:
        copy.wait()


def attend_kernel(limit_ref, q_ref, kv_ref, *refs):
    late, (cache_ref, out_ref, stage, sems) = refs[:-4], refs[-4:]
    width = kv_ref.shape[1] // 2
    gen = cache_ref.shape[0]
    kvh = width // HD
    gq = q_ref.shape[1] // width
    old = kv_ref.shape[0] - SPAN + sum(piece.shape[0] for piece in late)
    token = lax.broadcasted_iota(jnp.int32, (SPAN, SPAN), 0)
    causal = lax.broadcasted_iota(jnp.int32, (SPAN, SPAN), 1) <= token
    visible = lax.broadcasted_iota(jnp.int32, (SPAN, gen), 1) < jnp.broadcast_to(limit_ref[:1], (SPAN, gen))
    ones = jnp.ones((SPAN + old + gen, HD), jnp.bfloat16)
    keys, values = [], []
    for g in range(kvh):
        k_at = slice(g * HD, (g + 1) * HD)
        v_at = slice(width + g * HD, width + (g + 1) * HD)
        keys.append(jnp.concatenate([ref[:, k_at] for ref in (kv_ref, *late, cache_ref)], axis=0))
        value = jnp.concatenate([ref[:, v_at] for ref in (kv_ref, *late, cache_ref)], axis=0)
        values.append(jnp.concatenate([value, ones], axis=1))
    chunk = CHUNK * HD
    per_group = gq // CHUNK
    count = q_ref.shape[1] // chunk

    def scores_of(c):
        return dot_nt(head_rows(q_ref, c, CHUNK), keys[c // per_group])

    copies = []
    ahead = scores_of(0)
    for c in range(count):
        scores = ahead
        if c + 1 < count:
            ahead = scores_of(c + 1)
        weights = []
        for j in range(CHUNK):
            s = scores[j * SPAN : (j + 1) * SPAN]
            s_new = jnp.where(causal, s[:, :SPAN], NEGATIVE)
            s_cache = jnp.where(visible, s[:, SPAN + old :], NEGATIVE)
            s = jnp.concatenate([s_new, s[:, SPAN : SPAN + old], s_cache], axis=1)
            top = jnp.max(s, axis=1, keepdims=True)
            weights.append(jnp.exp2((s - top) * SCALE2).astype(jnp.bfloat16))
        out = dot_nn(jnp.concatenate(weights, axis=0), values[c // per_group])
        out = (out[:, :HD] / out[:, HD:]).astype(jnp.bfloat16)
        for j in range(CHUNK):
            stage[:, (c * CHUNK + j) * HD : (c * CHUNK + j + 1) * HD] = out[j * SPAN : (j + 1) * SPAN]
        columns = pl.ds(c * chunk, chunk)
        copy = pltpu.make_async_copy(stage.at[:, columns], out_ref.at[:, columns], sems.at[c])
        copy.start()
        copies.append(copy)
    for copy in copies:
        copy.wait()


def swap(x, axis, distance):
    return lax.ppermute(x, axis, [(i, i ^ distance) for i in range(lax.axis_size(axis))])


def on_device(q_new, kv_new, prompt_kv, cache_kv, ancestors, lengths):
    dom_count = lax.axis_size("dom")
    ctx_count = lax.axis_size("ctx")
    y_count = ctx_count // Z
    group, page_rows, _, width = cache_kv.shape
    tokens, q_width = q_new.shape
    half_rows = prompt_kv.shape[0] // 2
    shape = jax.ShapeDtypeStruct
    half, *rest = pl.pallas_call(
        functools.partial(pack_kernel, dom_count),
        out_shape=(
            shape((half_rows, 2 * width), jnp.bfloat16),
            *[shape((RUN, page_rows, 2 * width), jnp.bfloat16)] * dom_count,
            shape((group // RUN, page_rows, HD), jnp.bfloat16),
            shape((8, ctx_count * page_rows), jnp.int32),
        ),
        in_specs=[HBM] * 4,
        out_specs=(VMEM,) * (3 + dom_count),
        scratch_shapes=[
            pltpu.SMEM(ancestors.shape, jnp.int32),
            pltpu.SMEM(lengths.shape, jnp.int32),
            pltpu.VMEM((half_rows, 2, width), jnp.bfloat16),
            pltpu.VMEM(cache_kv.shape, jnp.bfloat16),
            pltpu.SemaphoreType.DMA((4,)),
        ],
        compiler_params=params(12),
        name="pack",
    )(*(pltpu.with_memory_space_constraint(x, pltpu.HBM) for x in (ancestors, lengths, prompt_kv, cache_kv)))
    outgoing, (far, limit) = rest[:dom_count], rest[dom_count:]

    pieces = [half] + [swap(half, "ctx", k * y_count) for k in range(1, Z)]

    incoming = outgoing[:1] + [swap(outgoing[k], "dom", k) for k in range(1, dom_count)]
    routed, rows = pl.pallas_call(
        functools.partial(route_kernel, dom_count),
        out_shape=(
            pltpu.HBM((group, page_rows, 2 * width), jnp.bfloat16),
            shape((Z * half_rows, 2 * width), jnp.bfloat16),
        ),
        in_specs=[VMEM] * (1 + dom_count + Z),
        out_specs=(HBM, VMEM),
        scratch_shapes=[pltpu.VMEM((group, page_rows, 2 * width), jnp.bfloat16), pltpu.SemaphoreType.DMA],
        compiler_params=params(12),
        name="route",
    )(far, *incoming, *pieces)
    over_y = [swap(rows, "ctx", k) for k in range(1, y_count)]
    pieces = [rows, swap(rows, "dom", 1), *over_y]
    late = [swap(piece, "dom", 1) for piece in over_y]
    pages = lax.all_to_all(routed, "ctx", split_axis=0, concat_axis=0, tiled=True)
    pages = pages.reshape(ctx_count * page_rows, 2 * width)

    key_count = SPAN + sum(piece.shape[0] for piece in pieces)
    kv, queries = pl.pallas_call(
        gather_kernel,
        out_shape=(shape((key_count, 2 * width), jnp.bfloat16), shape(q_new.shape, q_new.dtype)),
        in_specs=[HBM] + [VMEM] * (1 + len(pieces)),
        out_specs=(VMEM, VMEM),
        scratch_shapes=[pltpu.SemaphoreType.DMA((Q_COPIES,))],
        compiler_params=params(16),
        cost_estimate=pl.CostEstimate(flops=10**10, bytes_accessed=2**22, transcendentals=0),
        name="gather",
    )(pltpu.with_memory_space_constraint(q_new, pltpu.HBM), kv_new, *pieces)
    return pl.pallas_call(
        attend_kernel,
        out_shape=shape((tokens, q_width), jnp.bfloat16),
        in_specs=[VMEM] * (4 + len(late)),
        out_specs=HBM,
        scratch_shapes=[pltpu.VMEM((tokens, q_width), jnp.bfloat16), pltpu.SemaphoreType.DMA((q_width // (CHUNK * HD),))],
        compiler_params=params(40 if prompt_kv.shape[0] * ctx_count > 1024 else 24),
        name="attend",
    )(limit, queries, kv, *late, pages)


def solution(mesh):
    placed = (
        P(("dom", "ctx"), None),
        P(("dom", "ctx"), None, None),
        P("ctx", None, None),
        P("dom", "ctx", None, None),
        P(),
        P(),
    )
    return jax.shard_map(
        on_device, mesh=mesh, in_specs=placed, out_specs=P(("dom", "ctx"), None), check_vma=False
    )
```

```python
import functools

import jax
import jax.numpy as jnp
from jax import lax
from jax.experimental import pallas as pl
from jax.experimental.pallas import tpu as pltpu
from jax.sharding import PartitionSpec as P

HD = 128
SPAN = 128
PAGE = 8
RUN = 4
Z = 4
CHUNK = 4
Q_COPIES = 4
NEGATIVE = -1e30
SCALE2 = HD ** (-0.5) * 1.4426950408889634
VMEM = pl.BlockSpec(memory_space=pltpu.VMEM)
HBM = pl.BlockSpec(memory_space=pltpu.HBM)


def params(mib):
    return pltpu.CompilerParams(vmem_limit_bytes=mib * 2**20)


def pack_kernel(dom_count, anc_hbm, len_hbm, prompt_hbm, cache_hbm, half_ref, *refs):
    out_refs = refs[:dom_count]
    far_ref, limit_ref, anc_ref, len_ref, prompt_ref, cache_ref, sems = refs[dom_count:]
    group = cache_ref.shape[0]
    dom = lax.axis_index("dom")
    rows, width = half_ref.shape
    from_row = pl.multiple_of((dom % 2) * rows, rows)
    prompt_in = pltpu.make_async_copy(prompt_hbm.at[pl.ds(from_row, rows)], prompt_ref, sems.at[0])
    anc_in = pltpu.make_async_copy(anc_hbm, anc_ref, sems.at[1])
    len_in = pltpu.make_async_copy(len_hbm, len_ref, sems.at[2])
    cache_in = pltpu.make_async_copy(cache_hbm, cache_ref, sems.at[3])
    prompt_in.start()
    anc_in.start()
    len_in.start()
    cache_in.start()
    runs = group // RUN
    anc_in.wait()
    len_in.wait()
    for run in range(runs):
        far = (anc_ref[dom * group + run * RUN] // group) ^ dom
        far_ref[run] = jnp.full(far_ref.shape[1:], far.astype(jnp.float32)).astype(jnp.bfloat16)
    particle = dom * group + lax.axis_index("ctx")
    limit_ref[...] = jnp.full(limit_ref.shape, len_ref[anc_ref[particle]] * PAGE)
    prompt_in.wait()
    half_ref[...] = prompt_ref[...].reshape(rows, width)
    cache_in.wait()
    for k, out_ref in enumerate(out_refs):
        for run in range(runs):
            first = (dom ^ k) * group + run * RUN

            @pl.when(anc_ref[first] // group == dom)
            def _(first=first, out_ref=out_ref):
                for slot in range(RUN):
                    local = anc_ref[first + slot] % group
                    out_ref[slot] = cache_ref[local].reshape(cache_ref.shape[1], width)


def route_kernel(y_count, far_ref, *refs):
    in_refs, out_refs = refs[:-Z], refs[-Z:]
    own_z = lax.axis_index("ctx") // y_count
    width = out_refs[0].shape[2]
    for k, out_ref in enumerate(out_refs):
        for y in range(y_count):
            to = (own_z ^ k) * y_count + y
            far = far_ref[to // RUN]
            picked = in_refs[0][to % RUN]
            for at in range(1, len(in_refs)):
                here = jnp.concatenate([far == at] * (width // far.shape[1]), axis=1)
                picked = jnp.where(here, in_refs[at][to % RUN], picked)
            out_ref[y] = picked


def turn_kernel(*refs):
    in_refs, out_refs = refs[:Z], refs[Z:]
    own_y = lax.axis_index("ctx") % len(out_refs)
    for j, out_ref in enumerate(out_refs):
        for k, in_ref in enumerate(in_refs):
            out_ref[k] = in_ref[own_y ^ j]


def stack_kernel(*refs):
    *pieces, rows_ref = refs
    for number, piece in enumerate(pieces):
        rows_ref[number * piece.shape[0] : (number + 1) * piece.shape[0], :] = piece[...]


def head_rows(q_ref, g, gq):
    return jnp.concatenate(
        [q_ref[:, (g * gq + j) * HD : (g * gq + j + 1) * HD] for j in range(gq)], axis=0
    )


def dot_nt(a, b):
    return lax.dot_general(a, b, (((1,), (1,)), ((), ())), preferred_element_type=jnp.float32)


def dot_nn(a, b):
    return lax.dot_general(a, b, (((1,), (0,)), ((), ())), preferred_element_type=jnp.float32)


def gather_kernel(q_hbm, new_ref, *refs):
    pieces, (kv_ref, q_ref, sems) = refs[:-3], refs[-3:]
    q_rows = q_ref.shape[0] // Q_COPIES
    copies = []
    for number in range(Q_COPIES):
        rows_at = pl.ds(number * q_rows, q_rows)
        copies.append(pltpu.make_async_copy(q_hbm.at[rows_at], q_ref.at[rows_at], sems.at[number]))
        copies[number].start()
    kv_ref[:SPAN, :] = new_ref[...].reshape(SPAN, kv_ref.shape[1])
    at = SPAN
    for piece in pieces:
        kv_ref[at : at + piece.shape[0], :] = piece[...]
        at += piece.shape[0]
    for copy in copies:
        copy.wait()


def attend_kernel(y_count, limit_ref, q_ref, kv_ref, *refs):
    late, pages, (out_ref, stage, sems) = refs[: -3 - y_count], refs[-3 - y_count : -3], refs[-3:]
    width = kv_ref.shape[1] // 2
    page_rows = pages[0].shape[0] // Z
    gen = page_rows * Z * y_count
    kvh = width // HD
    gq = q_ref.shape[1] // width
    old = kv_ref.shape[0] - SPAN + sum(piece.shape[0] for piece in late)
    token = lax.broadcasted_iota(jnp.int32, (SPAN, SPAN), 0)
    causal = lax.broadcasted_iota(jnp.int32, (SPAN, SPAN), 1) <= token
    at = lax.broadcasted_iota(jnp.int32, (SPAN, gen), 1)
    ctx = lax.axis_index("ctx")
    page_z = (at // page_rows % Z) ^ (ctx // y_count)
    page_y = (at // (page_rows * Z)) ^ (ctx % y_count)
    at = (page_z * y_count + page_y) * page_rows + at % page_rows
    visible = at < jnp.broadcast_to(limit_ref[:1], (SPAN, gen))
    ones = jnp.ones((SPAN + old + gen, HD), jnp.bfloat16)
    keys, values = [], []
    for g in range(kvh):
        k_at = slice(g * HD, (g + 1) * HD)
        v_at = slice(width + g * HD, width + (g + 1) * HD)
        keys.append(jnp.concatenate([ref[:, k_at] for ref in (kv_ref, *late, *pages)], axis=0))
        value = jnp.concatenate([ref[:, v_at] for ref in (kv_ref, *late, *pages)], axis=0)
        values.append(jnp.concatenate([value, ones], axis=1))
    chunk = CHUNK * HD
    per_group = gq // CHUNK
    count = q_ref.shape[1] // chunk

    def scores_of(c):
        return dot_nt(head_rows(q_ref, c, CHUNK), keys[c // per_group])

    copies = []
    ahead = scores_of(0)
    for c in range(count):
        scores = ahead
        if c + 1 < count:
            ahead = scores_of(c + 1)
        weights = []
        for j in range(CHUNK):
            s = scores[j * SPAN : (j + 1) * SPAN]
            s_new = jnp.where(causal, s[:, :SPAN], NEGATIVE)
            s_cache = jnp.where(visible, s[:, SPAN + old :], NEGATIVE)
            s = jnp.concatenate([s_new, s[:, SPAN : SPAN + old], s_cache], axis=1)
            top = jnp.max(s, axis=1, keepdims=True)
            weights.append(jnp.exp2((s - top) * SCALE2).astype(jnp.bfloat16))
        out = dot_nn(jnp.concatenate(weights, axis=0), values[c // per_group])
        out = (out[:, :HD] * pl.reciprocal(out[:, HD:], approx=True)).astype(jnp.bfloat16)
        for j in range(CHUNK):
            stage[:, (c * CHUNK + j) * HD : (c * CHUNK + j + 1) * HD] = out[j * SPAN : (j + 1) * SPAN]
        columns = pl.ds(c * chunk, chunk)
        copy = pltpu.make_async_copy(stage.at[:, columns], out_ref.at[:, columns], sems.at[c])
        copy.start()
        copies.append(copy)
    for copy in copies:
        copy.wait()


def swap(x, axis, distance):
    return lax.ppermute(x, axis, [(i, i ^ distance) for i in range(lax.axis_size(axis))])


def on_device(q_new, kv_new, prompt_kv, cache_kv, ancestors, lengths):
    dom_count = lax.axis_size("dom")
    ctx_count = lax.axis_size("ctx")
    y_count = ctx_count // Z
    group, page_rows, _, width = cache_kv.shape
    tokens, q_width = q_new.shape
    half_rows = prompt_kv.shape[0] // 2
    shape = jax.ShapeDtypeStruct
    half, *rest = pl.pallas_call(
        functools.partial(pack_kernel, dom_count),
        out_shape=(
            shape((half_rows, 2 * width), jnp.bfloat16),
            *[shape((RUN, page_rows, 2 * width), jnp.bfloat16)] * dom_count,
            shape((group // RUN, page_rows, HD), jnp.bfloat16),
            shape((8, ctx_count * page_rows), jnp.int32),
        ),
        in_specs=[HBM] * 4,
        out_specs=(VMEM,) * (3 + dom_count),
        scratch_shapes=[
            pltpu.SMEM(ancestors.shape, jnp.int32),
            pltpu.SMEM(lengths.shape, jnp.int32),
            pltpu.VMEM((half_rows, 2, width), jnp.bfloat16),
            pltpu.VMEM(cache_kv.shape, jnp.bfloat16),
            pltpu.SemaphoreType.DMA((4,)),
        ],
        compiler_params=params(12),
        name="pack",
    )(*(pltpu.with_memory_space_constraint(x, pltpu.HBM) for x in (ancestors, lengths, prompt_kv, cache_kv)))
    outgoing, (far, limit) = rest[:dom_count], rest[dom_count:]

    pieces = [half] + [swap(half, "ctx", k * y_count) for k in range(1, Z)]

    incoming = outgoing[:1] + [swap(outgoing[k], "dom", k) for k in range(1, dom_count)]
    routed = pl.pallas_call(
        functools.partial(route_kernel, y_count),
        out_shape=(shape((y_count, page_rows, 2 * width), jnp.bfloat16),) * Z,
        in_specs=[VMEM] * (1 + dom_count),
        out_specs=(VMEM,) * Z,
        compiler_params=params(12),
        name="route",
    )(far, *incoming)
    routed = routed[:1] + tuple(swap(routed[k], "ctx", k * y_count) for k in range(1, Z))
    pages = pl.pallas_call(
        turn_kernel,
        out_shape=(shape((Z, page_rows, 2 * width), jnp.bfloat16),) * y_count,
        in_specs=[VMEM] * Z,
        out_specs=(VMEM,) * y_count,
        compiler_params=params(12),
        name="turn",
    )(*routed)
    pages = pages[:1] + tuple(swap(pages[j], "ctx", j) for j in range(1, y_count))
    pages = [page.reshape(Z * page_rows, 2 * width) for page in pages]
    rows = pl.pallas_call(
        stack_kernel,
        out_shape=shape((Z * half_rows, 2 * width), jnp.bfloat16),
        in_specs=[VMEM] * Z,
        out_specs=VMEM,
        compiler_params=params(12),
        name="stack",
    )(*pieces)
    over_y = [swap(rows, "ctx", k) for k in range(1, y_count)]
    pieces = [rows, swap(rows, "dom", 1), *over_y]
    late = [swap(piece, "dom", 1) for piece in over_y]
    key_count = SPAN + sum(piece.shape[0] for piece in pieces)
    kv, queries = pl.pallas_call(
        gather_kernel,
        out_shape=(shape((key_count, 2 * width), jnp.bfloat16), shape(q_new.shape, q_new.dtype)),
        in_specs=[HBM] + [VMEM] * (1 + len(pieces)),
        out_specs=(VMEM, VMEM),
        scratch_shapes=[pltpu.SemaphoreType.DMA((Q_COPIES,))],
        compiler_params=params(16),
        cost_estimate=pl.CostEstimate(flops=10**10, bytes_accessed=2**22, transcendentals=0),
        name="gather",
    )(pltpu.with_memory_space_constraint(q_new, pltpu.HBM), kv_new, *pieces)
    return pl.pallas_call(
        functools.partial(attend_kernel, y_count),
        out_shape=shape((tokens, q_width), jnp.bfloat16),
        in_specs=[VMEM] * (3 + len(late) + len(pages)),
        out_specs=HBM,
        scratch_shapes=[pltpu.VMEM((tokens, q_width), jnp.bfloat16), pltpu.SemaphoreType.DMA((q_width // (CHUNK * HD),))],
        compiler_params=params(40 if prompt_kv.shape[0] * ctx_count > 1024 else 24),
        name="attend",
    )(limit, queries, kv, *late, *pages)


def solution(mesh):
    placed = (
        P(("dom", "ctx"), None),
        P(("dom", "ctx"), None, None),
        P("ctx", None, None),
        P("dom", "ctx", None, None),
        P(),
        P(),
    )
    return jax.shard_map(
        on_device, mesh=mesh, in_specs=placed, out_specs=P(("dom", "ctx"), None), check_vma=False
    )
```

```python
import functools

import jax
import jax.numpy as jnp
from jax import lax
from jax.experimental import pallas as pl
from jax.experimental.pallas import tpu as pltpu
from jax.sharding import PartitionSpec as P

HD = 128
SPAN = 128
PAGE = 8
RUN = 4
Z = 4
CHUNK = 4
Q_COPIES = 4
NEGATIVE = -1e30
SCALE2 = HD ** (-0.5) * 1.4426950408889634
VMEM = pl.BlockSpec(memory_space=pltpu.VMEM)
HBM = pl.BlockSpec(memory_space=pltpu.HBM)


def params(mib):
    return pltpu.CompilerParams(vmem_limit_bytes=mib * 2**20)


def pack_kernel(dom_count, anc_hbm, len_hbm, prompt_hbm, cache_hbm, half_ref, *refs):
    out_refs = refs[:dom_count]
    far_ref, limit_ref, anc_ref, len_ref, prompt_ref, cache_ref, sems = refs[dom_count:]
    group = cache_ref.shape[0]
    dom = lax.axis_index("dom")
    rows, width = half_ref.shape
    from_row = pl.multiple_of((dom % 2) * rows, rows)
    prompt_in = pltpu.make_async_copy(prompt_hbm.at[pl.ds(from_row, rows)], prompt_ref, sems.at[0])
    anc_in = pltpu.make_async_copy(anc_hbm, anc_ref, sems.at[1])
    len_in = pltpu.make_async_copy(len_hbm, len_ref, sems.at[2])
    cache_in = pltpu.make_async_copy(cache_hbm, cache_ref, sems.at[3])
    prompt_in.start()
    anc_in.start()
    len_in.start()
    cache_in.start()
    runs = group // RUN
    anc_in.wait()
    len_in.wait()
    for run in range(runs):
        far = (anc_ref[dom * group + run * RUN] // group) ^ dom
        far_ref[run] = jnp.full(far_ref.shape[1:], far.astype(jnp.float32)).astype(jnp.bfloat16)
    particle = dom * group + lax.axis_index("ctx")
    limit_ref[...] = jnp.full(limit_ref.shape, len_ref[anc_ref[particle]] * PAGE)
    prompt_in.wait()
    half_ref[...] = prompt_ref[...].reshape(rows, width)
    cache_in.wait()
    for k, out_ref in enumerate(out_refs):
        for run in range(runs):
            first = (dom ^ k) * group + run * RUN

            @pl.when(anc_ref[first] // group == dom)
            def _(first=first, out_ref=out_ref):
                for slot in range(RUN):
                    local = anc_ref[first + slot] % group
                    out_ref[slot] = cache_ref[local].reshape(cache_ref.shape[1], width)


def route_kernel(dom_count, far_ref, *refs):
    in_refs, pieces, (out_hbm, rows_ref, out_ref, sem) = refs[:dom_count], refs[dom_count:-4], refs[-4:]
    width = out_ref.shape[2]
    for run in range(far_ref.shape[0]):
        far = far_ref[run]
        for slot in range(RUN):
            picked = in_refs[0][slot]
            for k in range(1, len(in_refs)):
                here = jnp.concatenate([far == k] * (width // far.shape[1]), axis=1)
                picked = jnp.where(here, in_refs[k][slot], picked)
            out_ref[run * RUN + slot] = picked
    out = pltpu.make_async_copy(out_ref, out_hbm, sem)
    out.start()
    for number, piece in enumerate(pieces):
        rows_ref[number * piece.shape[0] : (number + 1) * piece.shape[0], :] = piece[...]
    out.wait()


def head_rows(q_ref, g, gq):
    return jnp.concatenate(
        [q_ref[:, (g * gq + j) * HD : (g * gq + j + 1) * HD] for j in range(gq)], axis=0
    )


def dot_nt(a, b):
    return lax.dot_general(a, b, (((1,), (1,)), ((), ())), preferred_element_type=jnp.float32)


def dot_nn(a, b):
    return lax.dot_general(a, b, (((1,), (0,)), ((), ())), preferred_element_type=jnp.float32)


def gather_kernel(q_hbm, new_ref, *refs):
    pieces, (kv_ref, q_ref, sems) = refs[:-3], refs[-3:]
    q_rows = q_ref.shape[0] // Q_COPIES
    copies = []
    for number in range(Q_COPIES):
        rows_at = pl.ds(number * q_rows, q_rows)
        copies.append(pltpu.make_async_copy(q_hbm.at[rows_at], q_ref.at[rows_at], sems.at[number]))
        copies[number].start()
    kv_ref[:SPAN, :] = new_ref[...].reshape(SPAN, kv_ref.shape[1])
    at = SPAN
    for piece in pieces:
        kv_ref[at : at + piece.shape[0], :] = piece[...]
        at += piece.shape[0]
    for copy in copies:
        copy.wait()


def attend_kernel(limit_ref, q_ref, kv_ref, *refs):
    late, (cache_ref, out_ref, stage, sems) = refs[:-4], refs[-4:]
    width = kv_ref.shape[1] // 2
    gen = cache_ref.shape[0]
    kvh = width // HD
    gq = q_ref.shape[1] // width
    old = kv_ref.shape[0] - SPAN + sum(piece.shape[0] for piece in late)
    token = lax.broadcasted_iota(jnp.int32, (SPAN, SPAN), 0)
    causal = lax.broadcasted_iota(jnp.int32, (SPAN, SPAN), 1) <= token
    visible = lax.broadcasted_iota(jnp.int32, (SPAN, gen), 1) < jnp.broadcast_to(limit_ref[:1], (SPAN, gen))
    ones = jnp.ones((SPAN + old + gen, HD), jnp.bfloat16)
    keys, values = [], []
    for g in range(kvh):
        k_at = slice(g * HD, (g + 1) * HD)
        v_at = slice(width + g * HD, width + (g + 1) * HD)
        keys.append(jnp.concatenate([ref[:, k_at] for ref in (kv_ref, *late, cache_ref)], axis=0))
        value = jnp.concatenate([ref[:, v_at] for ref in (kv_ref, *late, cache_ref)], axis=0)
        values.append(jnp.concatenate([value, ones], axis=1))
    chunk = CHUNK * HD
    per_group = gq // CHUNK
    count = q_ref.shape[1] // chunk

    def scores_of(c):
        return dot_nt(head_rows(q_ref, c, CHUNK), keys[c // per_group])

    copies = []
    ahead = scores_of(0)
    for c in range(count):
        scores = ahead
        if c + 1 < count:
            ahead = scores_of(c + 1)
        weights = []
        for j in range(CHUNK):
            s = scores[j * SPAN : (j + 1) * SPAN]
            s_new = jnp.where(causal, s[:, :SPAN], NEGATIVE)
            s_cache = jnp.where(visible, s[:, SPAN + old :], NEGATIVE)
            s = jnp.concatenate([s_new, s[:, SPAN : SPAN + old], s_cache], axis=1)
            top = jnp.max(s, axis=1, keepdims=True)
            weights.append(jnp.exp2(((s - top) * SCALE2).astype(jnp.bfloat16)))
        out = dot_nn(jnp.concatenate(weights, axis=0), values[c // per_group])
        out = (out[:, :HD] * pl.reciprocal(out[:, HD:], approx=True)).astype(jnp.bfloat16)
        for j in range(CHUNK):
            stage[:, (c * CHUNK + j) * HD : (c * CHUNK + j + 1) * HD] = out[j * SPAN : (j + 1) * SPAN]
        columns = pl.ds(c * chunk, chunk)
        copy = pltpu.make_async_copy(stage.at[:, columns], out_ref.at[:, columns], sems.at[c])
        copy.start()
        copies.append(copy)
    for copy in copies:
        copy.wait()


def swap(x, axis, distance):
    return lax.ppermute(x, axis, [(i, i ^ distance) for i in range(lax.axis_size(axis))])


def on_device(q_new, kv_new, prompt_kv, cache_kv, ancestors, lengths):
    dom_count = lax.axis_size("dom")
    ctx_count = lax.axis_size("ctx")
    y_count = ctx_count // Z
    group, page_rows, _, width = cache_kv.shape
    tokens, q_width = q_new.shape
    half_rows = prompt_kv.shape[0] // 2
    shape = jax.ShapeDtypeStruct
    half, *rest = pl.pallas_call(
        functools.partial(pack_kernel, dom_count),
        out_shape=(
            shape((half_rows, 2 * width), jnp.bfloat16),
            *[shape((RUN, page_rows, 2 * width), jnp.bfloat16)] * dom_count,
            shape((group // RUN, page_rows, HD), jnp.bfloat16),
            shape((8, ctx_count * page_rows), jnp.int32),
        ),
        in_specs=[HBM] * 4,
        out_specs=(VMEM,) * (3 + dom_count),
        scratch_shapes=[
            pltpu.SMEM(ancestors.shape, jnp.int32),
            pltpu.SMEM(lengths.shape, jnp.int32),
            pltpu.VMEM((half_rows, 2, width), jnp.bfloat16),
            pltpu.VMEM(cache_kv.shape, jnp.bfloat16),
            pltpu.SemaphoreType.DMA((4,)),
        ],
        compiler_params=params(12),
        name="pack",
    )(*(pltpu.with_memory_space_constraint(x, pltpu.HBM) for x in (ancestors, lengths, prompt_kv, cache_kv)))
    outgoing, (far, limit) = rest[:dom_count], rest[dom_count:]

    pieces = [half] + [swap(half, "ctx", k * y_count) for k in range(1, Z)]

    incoming = outgoing[:1] + [swap(outgoing[k], "dom", k) for k in range(1, dom_count)]
    routed, rows = pl.pallas_call(
        functools.partial(route_kernel, dom_count),
        out_shape=(
            pltpu.HBM((group, page_rows, 2 * width), jnp.bfloat16),
            shape((Z * half_rows, 2 * width), jnp.bfloat16),
        ),
        in_specs=[VMEM] * (1 + dom_count + Z),
        out_specs=(HBM, VMEM),
        scratch_shapes=[pltpu.VMEM((group, page_rows, 2 * width), jnp.bfloat16), pltpu.SemaphoreType.DMA],
        compiler_params=params(12),
        name="route",
    )(far, *incoming, *pieces)
    over_y = [swap(rows, "ctx", k) for k in range(1, y_count)]
    pieces = [rows, swap(rows, "dom", 1), *over_y]
    late = [swap(piece, "dom", 1) for piece in over_y]
    pages = lax.all_to_all(routed, "ctx", split_axis=0, concat_axis=0, tiled=True)
    pages = pages.reshape(ctx_count * page_rows, 2 * width)

    key_count = SPAN + sum(piece.shape[0] for piece in pieces)
    kv, queries = pl.pallas_call(
        gather_kernel,
        out_shape=(shape((key_count, 2 * width), jnp.bfloat16), shape(q_new.shape, q_new.dtype)),
        in_specs=[HBM] + [VMEM] * (1 + len(pieces)),
        out_specs=(VMEM, VMEM),
        scratch_shapes=[pltpu.SemaphoreType.DMA((Q_COPIES,))],
        compiler_params=params(16),
        cost_estimate=pl.CostEstimate(flops=10**10, bytes_accessed=2**22, transcendentals=0),
        name="gather",
    )(pltpu.with_memory_space_constraint(q_new, pltpu.HBM), kv_new, *pieces)
    return pl.pallas_call(
        attend_kernel,
        out_shape=shape((tokens, q_width), jnp.bfloat16),
        in_specs=[VMEM] * (4 + len(late)),
        out_specs=HBM,
        scratch_shapes=[pltpu.VMEM((tokens, q_width), jnp.bfloat16), pltpu.SemaphoreType.DMA((q_width // (CHUNK * HD),))],
        compiler_params=params(40 if prompt_kv.shape[0] * ctx_count > 1024 else 24),
        name="attend",
    )(limit, queries, kv, *late, pages)


def solution(mesh):
    placed = (
        P(("dom", "ctx"), None),
        P(("dom", "ctx"), None, None),
        P("ctx", None, None),
        P("dom", "ctx", None, None),
        P(),
        P(),
    )
    return jax.shard_map(
        on_device, mesh=mesh, in_specs=placed, out_specs=P(("dom", "ctx"), None), check_vma=False
    )
```

```python
import functools

import jax
import jax.numpy as jnp
from jax import lax
from jax.experimental import pallas as pl
from jax.experimental.pallas import tpu as pltpu
from jax.sharding import PartitionSpec as P

HD = 128
SPAN = 128
PAGE = 8
RUN = 4
Z = 4
CHUNK = 4
Q_COPIES = 4
NEGATIVE = -1e30
SCALE2 = HD ** (-0.5) * 1.4426950408889634
VMEM = pl.BlockSpec(memory_space=pltpu.VMEM)
HBM = pl.BlockSpec(memory_space=pltpu.HBM)


def params(mib):
    return pltpu.CompilerParams(vmem_limit_bytes=mib * 2**20)


def pack_kernel(dom_count, anc_hbm, len_hbm, prompt_hbm, cache_hbm, half_ref, *refs):
    out_refs = refs[:dom_count]
    far_ref, limit_ref, anc_ref, len_ref, prompt_ref, cache_ref, sems = refs[dom_count:]
    group = cache_ref.shape[0]
    dom = lax.axis_index("dom")
    rows, width = half_ref.shape
    from_row = pl.multiple_of((dom % 2) * rows, rows)
    prompt_in = pltpu.make_async_copy(prompt_hbm.at[pl.ds(from_row, rows)], prompt_ref, sems.at[0])
    anc_in = pltpu.make_async_copy(anc_hbm, anc_ref, sems.at[1])
    len_in = pltpu.make_async_copy(len_hbm, len_ref, sems.at[2])
    cache_in = pltpu.make_async_copy(cache_hbm, cache_ref, sems.at[3])
    prompt_in.start()
    anc_in.start()
    len_in.start()
    cache_in.start()
    runs = group // RUN
    anc_in.wait()
    len_in.wait()
    for run in range(runs):
        far = (anc_ref[dom * group + run * RUN] // group) ^ dom
        far_ref[run] = jnp.full(far_ref.shape[1:], far.astype(jnp.float32)).astype(jnp.bfloat16)
    particle = dom * group + lax.axis_index("ctx")
    limit_ref[...] = jnp.full(limit_ref.shape, len_ref[anc_ref[particle]] * PAGE)
    prompt_in.wait()
    half_ref[...] = prompt_ref[...].reshape(rows, width)
    cache_in.wait()
    for k, out_ref in enumerate(out_refs):
        for run in range(runs):
            first = (dom ^ k) * group + run * RUN

            @pl.when(anc_ref[first] // group == dom)
            def _(first=first, out_ref=out_ref):
                for slot in range(RUN):
                    local = anc_ref[first + slot] % group
                    out_ref[slot] = cache_ref[local].reshape(cache_ref.shape[1], width)


def route_kernel(dom_count, far_ref, *refs):
    in_refs, (out_hbm, out_ref, sem) = refs[:dom_count], refs[-3:]
    width = out_ref.shape[2]
    for run in range(far_ref.shape[0]):
        far = far_ref[run]
        for slot in range(RUN):
            picked = in_refs[0][slot]
            for k in range(1, len(in_refs)):
                here = jnp.concatenate([far == k] * (width // far.shape[1]), axis=1)
                picked = jnp.where(here, in_refs[k][slot], picked)
            out_ref[run * RUN + slot] = picked
    out = pltpu.make_async_copy(out_ref, out_hbm, sem)
    out.start()
    out.wait()


def stack_kernel(*refs):
    pieces, out_refs = refs[:Z], refs[-2:]
    half = len(pieces) // 2
    for number, piece in enumerate(pieces):
        at = number % half * piece.shape[0]
        out_refs[number // half][at : at + piece.shape[0], :] = piece[...]


def head_rows(q_ref, g, gq):
    return jnp.concatenate(
        [q_ref[:, (g * gq + j) * HD : (g * gq + j + 1) * HD] for j in range(gq)], axis=0
    )


def dot_nt(a, b):
    return lax.dot_general(a, b, (((1,), (1,)), ((), ())), preferred_element_type=jnp.float32)


def dot_nn(a, b):
    return lax.dot_general(a, b, (((1,), (0,)), ((), ())), preferred_element_type=jnp.float32)


def gather_kernel(q_hbm, new_ref, *refs):
    pieces, (kv_ref, q_ref, sems) = refs[:-3], refs[-3:]
    q_rows = q_ref.shape[0] // Q_COPIES
    copies = []
    for number in range(Q_COPIES):
        rows_at = pl.ds(number * q_rows, q_rows)
        copies.append(pltpu.make_async_copy(q_hbm.at[rows_at], q_ref.at[rows_at], sems.at[number]))
        copies[number].start()
    kv_ref[:SPAN, :] = new_ref[...].reshape(SPAN, kv_ref.shape[1])
    at = SPAN
    for piece in pieces:
        kv_ref[at : at + piece.shape[0], :] = piece[...]
        at += piece.shape[0]
    for copy in copies:
        copy.wait()


def attend_kernel(limit_ref, q_ref, kv_ref, *refs):
    late, (cache_ref, out_ref, stage, sems) = refs[:-4], refs[-4:]
    width = kv_ref.shape[1] // 2
    gen = cache_ref.shape[0]
    kvh = width // HD
    gq = q_ref.shape[1] // width
    old = kv_ref.shape[0] - SPAN + sum(piece.shape[0] for piece in late)
    token = lax.broadcasted_iota(jnp.int32, (SPAN, SPAN), 0)
    causal = lax.broadcasted_iota(jnp.int32, (SPAN, SPAN), 1) <= token
    visible = lax.broadcasted_iota(jnp.int32, (SPAN, gen), 1) < jnp.broadcast_to(limit_ref[:1], (SPAN, gen))
    ones = jnp.ones((SPAN + old + gen, HD), jnp.bfloat16)
    keys, values = [], []
    for g in range(kvh):
        k_at = slice(g * HD, (g + 1) * HD)
        v_at = slice(width + g * HD, width + (g + 1) * HD)
        keys.append(jnp.concatenate([ref[:, k_at] for ref in (kv_ref, *late, cache_ref)], axis=0))
        value = jnp.concatenate([ref[:, v_at] for ref in (kv_ref, *late, cache_ref)], axis=0)
        values.append(jnp.concatenate([value, ones], axis=1))
    chunk = CHUNK * HD
    per_group = gq // CHUNK
    count = q_ref.shape[1] // chunk

    def scores_of(c):
        return dot_nt(head_rows(q_ref, c, CHUNK), keys[c // per_group])

    copies = []
    ahead = scores_of(0)
    for c in range(count):
        scores = ahead
        if c + 1 < count:
            ahead = scores_of(c + 1)
        weights = []
        for j in range(CHUNK):
            s = scores[j * SPAN : (j + 1) * SPAN]
            s_new = jnp.where(causal, s[:, :SPAN], NEGATIVE)
            s_cache = jnp.where(visible, s[:, SPAN + old :], NEGATIVE)
            s = jnp.concatenate([s_new, s[:, SPAN : SPAN + old], s_cache], axis=1)
            top = jnp.max(s, axis=1, keepdims=True)
            weights.append(jnp.exp2((s - top) * SCALE2).astype(jnp.bfloat16))
        out = dot_nn(jnp.concatenate(weights, axis=0), values[c // per_group])
        out = (out[:, :HD] / out[:, HD:]).astype(jnp.bfloat16)
        for j in range(CHUNK):
            stage[:, (c * CHUNK + j) * HD : (c * CHUNK + j + 1) * HD] = out[j * SPAN : (j + 1) * SPAN]
        columns = pl.ds(c * chunk, chunk)
        copy = pltpu.make_async_copy(stage.at[:, columns], out_ref.at[:, columns], sems.at[c])
        copy.start()
        copies.append(copy)
    for copy in copies:
        copy.wait()


def swap(x, axis, distance):
    return lax.ppermute(x, axis, [(i, i ^ distance) for i in range(lax.axis_size(axis))])


def on_device(q_new, kv_new, prompt_kv, cache_kv, ancestors, lengths):
    dom_count = lax.axis_size("dom")
    ctx_count = lax.axis_size("ctx")
    y_count = ctx_count // Z
    group, page_rows, _, width = cache_kv.shape
    tokens, q_width = q_new.shape
    half_rows = prompt_kv.shape[0] // 2
    shape = jax.ShapeDtypeStruct
    half, *rest = pl.pallas_call(
        functools.partial(pack_kernel, dom_count),
        out_shape=(
            shape((half_rows, 2 * width), jnp.bfloat16),
            *[shape((RUN, page_rows, 2 * width), jnp.bfloat16)] * dom_count,
            shape((group // RUN, page_rows, HD), jnp.bfloat16),
            shape((8, ctx_count * page_rows), jnp.int32),
        ),
        in_specs=[HBM] * 4,
        out_specs=(VMEM,) * (3 + dom_count),
        scratch_shapes=[
            pltpu.SMEM(ancestors.shape, jnp.int32),
            pltpu.SMEM(lengths.shape, jnp.int32),
            pltpu.VMEM((half_rows, 2, width), jnp.bfloat16),
            pltpu.VMEM(cache_kv.shape, jnp.bfloat16),
            pltpu.SemaphoreType.DMA((4,)),
        ],
        compiler_params=params(12),
        name="pack",
    )(*(pltpu.with_memory_space_constraint(x, pltpu.HBM) for x in (ancestors, lengths, prompt_kv, cache_kv)))
    outgoing, (far, limit) = rest[:dom_count], rest[dom_count:]

    pieces = [half] + [swap(half, "ctx", k * y_count) for k in range(1, Z)]

    incoming = outgoing[:1] + [swap(outgoing[k], "dom", k) for k in range(1, dom_count)]
    routed = pl.pallas_call(
        functools.partial(route_kernel, dom_count),
        out_shape=pltpu.HBM((group, page_rows, 2 * width), jnp.bfloat16),
        in_specs=[VMEM] * (1 + dom_count),
        out_specs=HBM,
        scratch_shapes=[pltpu.VMEM((group, page_rows, 2 * width), jnp.bfloat16), pltpu.SemaphoreType.DMA],
        compiler_params=params(12),
        name="route",
    )(far, *incoming)
    stacks = pl.pallas_call(
        stack_kernel,
        out_shape=(shape((Z // 2 * half_rows, 2 * width), jnp.bfloat16),) * 2,
        in_specs=[VMEM] * Z + [pl.BlockSpec(memory_space=pl.ANY)] * (dom_count - 1),
        out_specs=(VMEM, VMEM),
        compiler_params=params(12),
        name="stack",
    )(*pieces, *incoming[1:])
    pieces = [*stacks, *(swap(rows, "dom", 1) for rows in stacks)]
    late = [swap(rows, "ctx", k) for k in range(1, y_count) for rows in stacks]
    late += [swap(rows, "dom", 1) for rows in late]
    pages = lax.all_to_all(routed, "ctx", split_axis=0, concat_axis=0, tiled=True)
    pages = pages.reshape(ctx_count * page_rows, 2 * width)

    key_count = SPAN + sum(piece.shape[0] for piece in pieces)
    kv, queries = pl.pallas_call(
        gather_kernel,
        out_shape=(shape((key_count, 2 * width), jnp.bfloat16), shape(q_new.shape, q_new.dtype)),
        in_specs=[HBM] + [VMEM] * (1 + len(pieces)),
        out_specs=(VMEM, VMEM),
        scratch_shapes=[pltpu.SemaphoreType.DMA((Q_COPIES,))],
        compiler_params=params(16),
        cost_estimate=pl.CostEstimate(flops=10**9, bytes_accessed=2**22, transcendentals=0),
        name="gather",
    )(pltpu.with_memory_space_constraint(q_new, pltpu.HBM), kv_new, *pieces)
    return pl.pallas_call(
        attend_kernel,
        out_shape=shape((tokens, q_width), jnp.bfloat16),
        in_specs=[VMEM] * (4 + len(late)),
        out_specs=HBM,
        scratch_shapes=[pltpu.VMEM((tokens, q_width), jnp.bfloat16), pltpu.SemaphoreType.DMA((q_width // (CHUNK * HD),))],
        compiler_params=params(40 if prompt_kv.shape[0] * ctx_count > 1024 else 24),
        name="attend",
    )(limit, queries, kv, *late, pages)


def solution(mesh):
    placed = (
        P(("dom", "ctx"), None),
        P(("dom", "ctx"), None, None),
        P("ctx", None, None),
        P("dom", "ctx", None, None),
        P(),
        P(),
    )
    return jax.shard_map(
        on_device, mesh=mesh, in_specs=placed, out_specs=P(("dom", "ctx"), None), check_vma=False
    )
```

```python
import functools

import jax
import jax.numpy as jnp
from jax import lax
from jax.experimental import pallas as pl
from jax.experimental.pallas import tpu as pltpu
from jax.sharding import PartitionSpec as P

HD = 128
SPAN = 128
PAGE = 8
RUN = 4
Z = 4
CHUNK = 4
Q_COPIES = 4
NEGATIVE = -1e30
SCALE2 = HD ** (-0.5) * 1.4426950408889634
VMEM = pl.BlockSpec(memory_space=pltpu.VMEM)
HBM = pl.BlockSpec(memory_space=pltpu.HBM)


def params(mib):
    return pltpu.CompilerParams(vmem_limit_bytes=mib * 2**20)


def pack_kernel(dom_count, anc_hbm, len_hbm, prompt_hbm, cache_hbm, half_ref, *refs):
    out_refs = refs[:dom_count]
    far_ref, limit_ref, anc_ref, len_ref, prompt_ref, cache_ref, sems = refs[dom_count:]
    group = cache_ref.shape[0]
    dom = lax.axis_index("dom")
    rows, width = half_ref.shape
    from_row = pl.multiple_of((dom % 2) * rows, rows)
    prompt_in = pltpu.make_async_copy(prompt_hbm.at[pl.ds(from_row, rows)], prompt_ref, sems.at[0])
    anc_in = pltpu.make_async_copy(anc_hbm, anc_ref, sems.at[1])
    len_in = pltpu.make_async_copy(len_hbm, len_ref, sems.at[2])
    cache_in = pltpu.make_async_copy(cache_hbm, cache_ref, sems.at[3])
    prompt_in.start()
    anc_in.start()
    len_in.start()
    cache_in.start()
    runs = group // RUN
    anc_in.wait()
    len_in.wait()
    for run in range(runs):
        far = (anc_ref[dom * group + run * RUN] // group) ^ dom
        far_ref[run] = jnp.full(far_ref.shape[1:], far.astype(jnp.float32)).astype(jnp.bfloat16)
    particle = dom * group + lax.axis_index("ctx")
    limit_ref[...] = jnp.full(limit_ref.shape, len_ref[anc_ref[particle]] * PAGE)
    prompt_in.wait()
    half_ref[...] = prompt_ref[...].reshape(rows, width)
    cache_in.wait()
    for k, out_ref in enumerate(out_refs):
        for run in range(runs):
            first = (dom ^ k) * group + run * RUN

            @pl.when(anc_ref[first] // group == dom)
            def _(first=first, out_ref=out_ref):
                for slot in range(RUN):
                    local = anc_ref[first + slot] % group
                    out_ref[slot] = cache_ref[local].reshape(cache_ref.shape[1], width)


def route_kernel(dom_count, far_ref, *refs):
    in_refs, (out_hbm, out_ref, sem) = refs[:dom_count], refs[-3:]
    width = out_ref.shape[2]
    for run in range(far_ref.shape[0]):
        far = far_ref[run]
        for slot in range(RUN):
            picked = in_refs[0][slot]
            for k in range(1, len(in_refs)):
                here = jnp.concatenate([far == k] * (width // far.shape[1]), axis=1)
                picked = jnp.where(here, in_refs[k][slot], picked)
            out_ref[run * RUN + slot] = picked
    out = pltpu.make_async_copy(out_ref, out_hbm, sem)
    out.start()
    out.wait()


def stack_kernel(*refs):
    pieces, rows_ref = refs[:Z], refs[-1]
    for number, piece in enumerate(pieces):
        rows_ref[number * piece.shape[0] : (number + 1) * piece.shape[0], :] = piece[...]


def head_rows(q_ref, g, gq):
    return jnp.concatenate(
        [q_ref[:, (g * gq + j) * HD : (g * gq + j + 1) * HD] for j in range(gq)], axis=0
    )


def dot_nt(a, b):
    return lax.dot_general(a, b, (((1,), (1,)), ((), ())), preferred_element_type=jnp.float32)


def dot_nn(a, b):
    return lax.dot_general(a, b, (((1,), (0,)), ((), ())), preferred_element_type=jnp.float32)


def gather_kernel(q_hbm, new_ref, *refs):
    pieces, (kv_ref, q_ref, sems) = refs[:-3], refs[-3:]
    q_rows = q_ref.shape[0] // Q_COPIES
    copies = []
    for number in range(Q_COPIES):
        rows_at = pl.ds(number * q_rows, q_rows)
        copies.append(pltpu.make_async_copy(q_hbm.at[rows_at], q_ref.at[rows_at], sems.at[number]))
        copies[number].start()
    kv_ref[:SPAN, :] = new_ref[...].reshape(SPAN, kv_ref.shape[1])
    at = SPAN
    for piece in pieces:
        kv_ref[at : at + piece.shape[0], :] = piece[...]
        at += piece.shape[0]
    for copy in copies:
        copy.wait()


def attend_kernel(limit_ref, q_ref, kv_ref, *refs):
    late, (cache_ref, out_ref, stage, sems) = refs[:-4], refs[-4:]
    width = kv_ref.shape[1] // 2
    gen = cache_ref.shape[0]
    kvh = width // HD
    gq = q_ref.shape[1] // width
    old = kv_ref.shape[0] - SPAN + sum(piece.shape[0] for piece in late)
    token = lax.broadcasted_iota(jnp.int32, (SPAN, SPAN), 0)
    causal = lax.broadcasted_iota(jnp.int32, (SPAN, SPAN), 1) <= token
    visible = lax.broadcasted_iota(jnp.int32, (SPAN, gen), 1) < jnp.broadcast_to(limit_ref[:1], (SPAN, gen))
    ones = jnp.ones((SPAN + old + gen, HD), jnp.bfloat16)
    keys, values = [], []
    for g in range(kvh):
        k_at = slice(g * HD, (g + 1) * HD)
        v_at = slice(width + g * HD, width + (g + 1) * HD)
        keys.append(jnp.concatenate([ref[:, k_at] for ref in (kv_ref, *late, cache_ref)], axis=0))
        value = jnp.concatenate([ref[:, v_at] for ref in (kv_ref, *late, cache_ref)], axis=0)
        values.append(jnp.concatenate([value, ones], axis=1))
    chunk = CHUNK * HD
    per_group = gq // CHUNK
    count = q_ref.shape[1] // chunk

    def scores_of(c):
        return dot_nt(head_rows(q_ref, c, CHUNK), keys[c // per_group])

    copies = []
    ahead = scores_of(0)
    for c in range(count):
        scores = ahead
        if c + 1 < count:
            ahead = scores_of(c + 1)
        weights = []
        for j in range(CHUNK):
            s = scores[j * SPAN : (j + 1) * SPAN]
            s_new = jnp.where(causal, s[:, :SPAN], NEGATIVE)
            s_cache = jnp.where(visible, s[:, SPAN + old :], NEGATIVE)
            s = jnp.concatenate([s_new, s[:, SPAN : SPAN + old], s_cache], axis=1)
            top = jnp.max(s, axis=1, keepdims=True)
            weights.append(jnp.exp2((s - top) * SCALE2).astype(jnp.bfloat16))
        out = dot_nn(jnp.concatenate(weights, axis=0), values[c // per_group])
        out = (out[:, :HD] / out[:, HD:]).astype(jnp.bfloat16)
        for j in range(CHUNK):
            stage[:, (c * CHUNK + j) * HD : (c * CHUNK + j + 1) * HD] = out[j * SPAN : (j + 1) * SPAN]
        columns = pl.ds(c * chunk, chunk)
        copy = pltpu.make_async_copy(stage.at[:, columns], out_ref.at[:, columns], sems.at[c])
        copy.start()
        copies.append(copy)
    for copy in copies:
        copy.wait()


def swap(x, axis, distance):
    return lax.ppermute(x, axis, [(i, i ^ distance) for i in range(lax.axis_size(axis))])


def on_device(q_new, kv_new, prompt_kv, cache_kv, ancestors, lengths):
    dom_count = lax.axis_size("dom")
    ctx_count = lax.axis_size("ctx")
    y_count = ctx_count // Z
    group, page_rows, _, width = cache_kv.shape
    tokens, q_width = q_new.shape
    half_rows = prompt_kv.shape[0] // 2
    shape = jax.ShapeDtypeStruct
    half, *rest = pl.pallas_call(
        functools.partial(pack_kernel, dom_count),
        out_shape=(
            shape((half_rows, 2 * width), jnp.bfloat16),
            *[shape((RUN, page_rows, 2 * width), jnp.bfloat16)] * dom_count,
            shape((group // RUN, page_rows, HD), jnp.bfloat16),
            shape((8, ctx_count * page_rows), jnp.int32),
        ),
        in_specs=[HBM] * 4,
        out_specs=(VMEM,) * (3 + dom_count),
        scratch_shapes=[
            pltpu.SMEM(ancestors.shape, jnp.int32),
            pltpu.SMEM(lengths.shape, jnp.int32),
            pltpu.VMEM((half_rows, 2, width), jnp.bfloat16),
            pltpu.VMEM(cache_kv.shape, jnp.bfloat16),
            pltpu.SemaphoreType.DMA((4,)),
        ],
        compiler_params=params(12),
        name="pack",
    )(*(pltpu.with_memory_space_constraint(x, pltpu.HBM) for x in (ancestors, lengths, prompt_kv, cache_kv)))
    outgoing, (far, limit) = rest[:dom_count], rest[dom_count:]

    pieces = [half] + [swap(half, "ctx", k * y_count) for k in range(1, Z)]

    incoming = outgoing[:1] + [swap(outgoing[k], "dom", k) for k in range(1, dom_count)]
    routed = pl.pallas_call(
        functools.partial(route_kernel, dom_count),
        out_shape=pltpu.HBM((group, page_rows, 2 * width), jnp.bfloat16),
        in_specs=[VMEM] * (1 + dom_count),
        out_specs=HBM,
        scratch_shapes=[pltpu.VMEM((group, page_rows, 2 * width), jnp.bfloat16), pltpu.SemaphoreType.DMA],
        compiler_params=params(12),
        name="route",
    )(far, *incoming)
    rows = pl.pallas_call(
        stack_kernel,
        out_shape=shape((Z * half_rows, 2 * width), jnp.bfloat16),
        in_specs=[VMEM] * Z + [HBM],
        out_specs=VMEM,
        compiler_params=params(12),
        name="stack",
    )(*pieces, pltpu.with_memory_space_constraint(routed, pltpu.HBM))
    over_y = [swap(rows, "ctx", k) for k in range(1, y_count)]
    pieces = [rows, swap(rows, "dom", 1), *over_y]
    late = [swap(piece, "dom", 1) for piece in over_y]
    pages = lax.all_to_all(routed, "ctx", split_axis=0, concat_axis=0, tiled=True)
    pages = pages.reshape(ctx_count * page_rows, 2 * width)

    key_count = SPAN + sum(piece.shape[0] for piece in pieces)
    kv, queries = pl.pallas_call(
        gather_kernel,
        out_shape=(shape((key_count, 2 * width), jnp.bfloat16), shape(q_new.shape, q_new.dtype)),
        in_specs=[HBM] + [VMEM] * (1 + len(pieces)),
        out_specs=(VMEM, VMEM),
        scratch_shapes=[pltpu.SemaphoreType.DMA((Q_COPIES,))],
        compiler_params=params(16),
        cost_estimate=pl.CostEstimate(flops=10**10, bytes_accessed=2**22, transcendentals=0),
        name="gather",
    )(pltpu.with_memory_space_constraint(q_new, pltpu.HBM), kv_new, *pieces)
    return pl.pallas_call(
        attend_kernel,
        out_shape=shape((tokens, q_width), jnp.bfloat16),
        in_specs=[VMEM] * (4 + len(late)),
        out_specs=HBM,
        scratch_shapes=[pltpu.VMEM((tokens, q_width), jnp.bfloat16), pltpu.SemaphoreType.DMA((q_width // (CHUNK * HD),))],
        compiler_params=params(40 if prompt_kv.shape[0] * ctx_count > 1024 else 24),
        name="attend",
    )(limit, queries, kv, *late, pages)


def solution(mesh):
    placed = (
        P(("dom", "ctx"), None),
        P(("dom", "ctx"), None, None),
        P("ctx", None, None),
        P("dom", "ctx", None, None),
        P(),
        P(),
    )
    return jax.shard_map(
        on_device, mesh=mesh, in_specs=placed, out_specs=P(("dom", "ctx"), None), check_vma=False
    )
```
